32 devices in a mesh: clip: 8 (over y, x, core), wt: 4 (over z).
Axes of the slice: x: 2, y: 2, z: 4, core: 2. Of those that a mesh axis runs over, the one named last changes fastest.
Arguments:
- encoded: bfloat16 [10048, 768], P(('clip', 'wt')), may hold values from -6 to 6
- visible_at: int32 [64, 157], P(('clip', 'wt')), may hold values from 0 to 1567, as said below
- project_weight: bfloat16 [768, 384], P('wt'), may hold values from -0.21875 to 0.21875
- mask_token: bfloat16 [384], P('wt'), may hold values from -6 to 6
- first_gain: bfloat16 [384], P('wt'), may hold values from 0.5 to 1.5
- first_shift: bfloat16 [384], P('wt'), may hold values from -1.75 to 1.75
- inputs_weight: bfloat16 [384, 1152], P('wt'), may hold values from -0.3125 to 0.3125
- query_bias: bfloat16 [384], P('wt'), may hold values from -1.75 to 1.75
- value_bias: bfloat16 [384], P('wt'), may hold values from -1.75 to 1.75
- merge_weight: bfloat16 [384, 384], P('wt'), may hold values from -1.25 to 1.25
- merge_bias: bfloat16 [384], P('wt'), may hold values from -1.75 to 1.75
- second_gain: bfloat16 [384], P('wt'), may hold values from 0.5 to 1.5
- second_shift: bfloat16 [384], P('wt'), may hold values from -1.75 to 1.75
- expand_weight: bfloat16 [384, 1536], P('wt'), may hold values from -0.3125 to 0.3125
- expand_bias: bfloat16 [1536], P('wt'), may hold values from -1.75 to 1.75
- reduce_weight: bfloat16 [1536, 384], P('wt'), may hold values from -0.15625 to 0.15625
- reduce_bias: bfloat16 [384], P('wt'), may hold values from -1.75 to 1.75
- upstream: bfloat16 [100352, 384], P(('clip', 'wt')), may hold values from -6 to 6
Outputs:
- decoded: bfloat16 [100352, 384], P(('clip', 'wt'))
- encoded_grad: bfloat16 [10048, 768], P(('clip', 'wt'))
- grad_project_weight: float32 [768, 384], P('wt')
- grad_mask_token: float32 [384], P('wt')
- grad_first_gain: float32 [384], P('wt')
- grad_first_shift: float32 [384], P('wt')
- grad_inputs_weight: float32 [384, 1152], P('wt')
- grad_query_bias: float32 [384], P('wt')
- grad_value_bias: float32 [384], P('wt')
- grad_merge_weight: float32 [384, 384], P('wt')
- grad_merge_bias: float32 [384], P('wt')
- grad_second_gain: float32 [384], P('wt')
- grad_second_shift: float32 [384], P('wt')
- grad_expand_weight: float32 [384, 1536], P('wt')
- grad_expand_bias: float32 [1536], P('wt')
- grad_reduce_weight: float32 [1536, 384], P('wt')
- grad_reduce_bias: float32 [384], P('wt')
The draws below stay inside these ranges and needn't reach their ends.
Inputs may be any that keep to these rules, and one draw needn't show every extreme that they name: `visible_at`: each row names 157 distinct token places of one copy, in no particular order.
All inputs are finite; a program needn't handle non-finite values.
Results may differ from the reference program's by a relative error of at most 0.018.
Values may be sent and summed in bfloat16 or wider, within the bound.
A program may use at most 384 MiB of HBM per device.

```python
import math
import jax
import jax.numpy as jnp
from jax import lax

D = 384
E = 768
H = 6
HEAD = 64
FF = 1536
L = 1568
VIS = 157
COPY_DEV = 2
COPIES = 64
N_CLIP = 8
N_WT = 4


def draw_visible_at(key, part):
    key = jax.random.fold_in(key, 7)
    copy_keys = jax.random.split(key, COPIES)

    def one_copy(subkey):
        return jax.random.permutation(subkey, L)[:VIS].astype(jnp.int32)
    return jax.vmap(one_copy)(copy_keys)


def steps_of(rng, dims, shards, smallest, largest):
    def one(position, shards_of):
        draws = jax.random.uniform(jax.random.fold_in(jax.random.fold_in(rng, 6), position), (shards_of,), jnp.float32, smallest / len(shards), largest / len(shards))
        return jnp.repeat(jnp.exp(draws), dims[position] // shards_of).reshape((-1,) + (1,) * (len(dims) - position - 1))

    level = one(*shards[0])
    for cut in shards[1:]:
        level = level * one(*cut)
    return level


def gaussian(stream_key, dims, spread, reach, cuts=(), kind=jnp.bfloat16):
    values = jax.random.normal(stream_key, dims, jnp.float32) * spread
    if len(cuts) > 0:
        values = steps_of(stream_key, dims, cuts, -0.22, 0.18) * values
    return jnp.clip(values, min=-reach, max=reach).astype(kind)


def setup_inputs(seed: int = 0) -> dict:
    arg_keys = jax.random.split(jax.random.key(seed), 19)
    return {
        "encoded": gaussian(arg_keys[0], (COPIES * VIS, E), 1.0, 6.0, ((0, 32),)),
        "visible_at": draw_visible_at(jax.random.fold_in(arg_keys[18], 71), 0),
        "project_weight": gaussian(arg_keys[2], (E, D), E ** -0.5, 0.21875, ((0, 4),)),
        "mask_token": gaussian(arg_keys[3], (D,), 1.0, 6.0, ((0, 4),)),
        "first_gain": jnp.clip(1.0 + 0.1 * jax.random.normal(arg_keys[4], (D,), jnp.float32), 0.5, 1.5).astype(jnp.bfloat16),
        "first_shift": gaussian(arg_keys[5], (D,), 0.3, 1.75, ((0, 4),)),
        "inputs_weight": gaussian(arg_keys[6], (D, 3 * D), D ** -0.5, 0.3125, ((0, 4),)),
        "query_bias": gaussian(arg_keys[7], (D,), 0.3, 1.75, ((0, 4),)),
        "value_bias": gaussian(arg_keys[8], (D,), 0.3, 1.75, ((0, 4),)),
        "merge_weight": gaussian(arg_keys[9], (D, D), (D // 16) ** -0.5, 1.25, ((0, 4),)),
        "merge_bias": gaussian(arg_keys[10], (D,), 0.3, 1.75, ((0, 4),)),
        "second_gain": jnp.clip(1.0 + 0.1 * jax.random.normal(arg_keys[11], (D,), jnp.float32), 0.5, 1.5).astype(jnp.bfloat16),
        "second_shift": gaussian(arg_keys[12], (D,), 0.3, 1.75, ((0, 4),)),
        "expand_weight": gaussian(arg_keys[13], (D, FF), D ** -0.5, 0.3125, ((0, 4),)),
        "expand_bias": gaussian(arg_keys[14], (FF,), 0.3, 1.75, ((0, 4),)),
        "reduce_weight": gaussian(arg_keys[15], (FF, D), FF ** -0.5, 0.15625, ((0, 4),)),
        "reduce_bias": gaussian(arg_keys[16], (D,), 0.3, 1.75, ((0, 4),)),
        "upstream": gaussian(arg_keys[17], (COPIES * L, D), 1.0, 6.0, ((0, 32),)),
    }


EPSILON = 1e-06

@jax.custom_vjp
def low(v):
    return lax.optimization_barrier(v.astype(jnp.bfloat16)).astype(jnp.float32)

@jax.custom_vjp
def low_back(v):
    return v

def low_keep(v):
    return (low(v), None)

def low_pass(kept, grad):
    return (grad,)

def back_keep(v):
    return (v, None)

def back_low(kept, grad):
    return (low(grad),)
low.defvjp(low_keep, low_pass)
low_back.defvjp(back_keep, back_low)

def product(left, right):
    return jnp.dot(left, right, precision=lax.Precision.HIGHEST)

def sinusoid_table(length, model_width):
    places = jnp.arange(length, dtype=jnp.int32).astype(jnp.float32)[:, None]
    columns = jnp.arange(model_width, dtype=jnp.int32)
    exponent = (2 * (columns // 2)).astype(jnp.float32) / model_width
    angles = places / jnp.power(10000.0, exponent)[None, :]
    return jnp.where(columns[None, :] % 2 == 0, jnp.sin(angles), jnp.cos(angles))

def layer_norm(inputs, gain_vector, shift_vector):
    center = inputs - lax.optimization_barrier(jnp.mean(inputs, -1, keepdims=True))
    variance = lax.optimization_barrier(jnp.mean(center * center, -1, keepdims=True))
    return center * lax.rsqrt(variance + EPSILON) * gain_vector + shift_vector

def decoder_layer(weight_all, seen_rows, places, positions):
    project_weight, mask_token, first_gain, first_shift, inputs_weight, query_bias, value_bias, merge_weight, merge_bias, second_gain, second_shift, expand_weight, expand_bias, reduce_weight, reduce_bias = weight_all
    projected = low(low_back(product(seen_rows, project_weight)))
    stream = jnp.broadcast_to(mask_token, (L, D)).at[places].set(projected) + positions
    normed_first = low(layer_norm(stream, first_gain, first_shift))
    zero_bias = jnp.zeros_like(query_bias)
    mixed = low(low_back(product(normed_first, inputs_weight) + jnp.concatenate([query_bias, zero_bias, value_bias])))
    heads_view = mixed.reshape(L, 3, H, HEAD)
    query_rows = heads_view[:, 0]
    key_rows = heads_view[:, 1]
    value_rows = heads_view[:, 2]
    scores = low_back(jnp.einsum('qhd,khd->hqk', query_rows, key_rows, precision=lax.Precision.HIGHEST) * (1.0 / math.sqrt(HEAD)))
    weights = low(jax.nn.softmax(scores, axis=-1))
    context = jnp.einsum('hqk,khd->qhd', weights, value_rows, precision=lax.Precision.HIGHEST).reshape(L, D)
    context = low(low_back(context))
    after_attn = stream + low_back(product(context, merge_weight) + merge_bias)
    normed_second = low(layer_norm(after_attn, second_gain, second_shift))
    lifted = low_back(product(normed_second, expand_weight) + expand_bias)
    activated = low(jax.nn.gelu(lifted, approximate=False))
    return after_attn + low_back(product(activated, reduce_weight) + reduce_bias)

def reference(encoded, visible_at, project_weight, mask_token, first_gain, first_shift, inputs_weight, query_bias, value_bias, merge_weight, merge_bias, second_gain, second_shift, expand_weight, expand_bias, reduce_weight, reduce_bias, upstream):
    weight_all = tuple((item.astype(jnp.float32) for item in (project_weight, mask_token, first_gain, first_shift, inputs_weight, query_bias, value_bias, merge_weight, merge_bias, second_gain, second_shift, expand_weight, expand_bias, reduce_weight, reduce_bias)))
    positions = sinusoid_table(L, D)
    copy_total = COPY_DEV * N_CLIP * N_WT
    copy_ids = jnp.arange(copy_total, dtype=jnp.int32)
    owner_block = copy_ids // COPY_DEV
    copy_slot = copy_ids % COPY_DEV
    clip_index = owner_block // N_WT
    weight_index = owner_block % N_WT
    group_copy = clip_index * COPY_DEV + copy_slot
    group_row = group_copy[:, None] * VIS + jnp.arange(VIS, dtype=jnp.int32)[None, :]
    source_clip = group_row % N_CLIP
    source_slot = group_row // N_CLIP
    arrival = ((source_clip * N_WT + weight_index[:, None]) * (COPY_DEV * VIS) + source_slot).astype(jnp.int32)
    seen_all = encoded.astype(jnp.float32)[arrival.reshape(-1)].reshape(copy_total, VIS, E)
    cotangent = upstream.astype(jnp.float32).reshape(copy_total, L, D) * 0.5
    zero_grads = tuple((jnp.zeros_like(item) for item in weight_all))

    def one_copy(totals, pieces):
        seen_rows, places, copy_cotangent = pieces

        def forward_copy(weights_now, rows_now):
            return decoder_layer(weights_now, rows_now, places, positions)
        output, pullback = jax.vjp(forward_copy, weight_all, seen_rows)
        grads_now, grad_rows = pullback(copy_cotangent)
        totals = tuple((left + right for left, right in zip(totals, grads_now)))
        return (totals, (output.astype(jnp.bfloat16), grad_rows))
    grads, (decoded_all, grad_seen) = lax.scan(one_copy, zero_grads, (seen_all, visible_at, cotangent))
    encoded_grad = jnp.zeros((copy_total * VIS, E), jnp.float32).at[arrival.reshape(-1)].set(grad_seen.reshape(copy_total * VIS, E)).astype(jnp.bfloat16)
    return (decoded_all.reshape(copy_total * L, D), encoded_grad, grads[0], grads[1], grads[2], grads[3], grads[4], grads[5], grads[6], grads[7], grads[8], grads[9], grads[10], grads[11], grads[12], grads[13], grads[14])
```

```python
import math

import jax
import jax.numpy as jnp
import numpy as np
from jax import lax
from jax.experimental import pallas as pl
from jax.experimental.pallas import tpu as pltpu
from jax.sharding import PartitionSpec as P

H = 6
HEAD = 64
L = 1568
LANES = 128
LP = -(-L // LANES) * LANES
EPSILON = 1e-06
LOG2E = math.log2(math.e)
Q_SCALE = LOG2E / math.sqrt(HEAD)
ROOT_HALF = math.sqrt(0.5)
INV_ROOT_TWO_PI = 1.0 / math.sqrt(2.0 * math.pi)
SAFE_EXPONENT = 100.0
VMEM_LIMIT = 60 * 2**20
FFC = 256
Q_BLOCKS = ((0, 896), (896, LP - 896))
F32 = jnp.float32
BF16 = jnp.bfloat16


def params(**kw):
    return pltpu.CompilerParams(vmem_limit_bytes=VMEM_LIMIT, **kw)


def dg(a, b, ca, cb):
    return lax.dot_general(a, b, (((ca,), (cb,)), ((), ())), preferred_element_type=F32)


def position_table(width):
    places = np.arange(L, dtype=np.float64)[None, :]
    columns = np.arange(width)
    exponent = (2 * (columns // 2)).astype(np.float64) / width
    angles = places / np.power(10000.0, exponent)[:, None]
    return np.where(columns[:, None] % 2 == 0, np.sin(angles), np.cos(angles)).astype(np.float32)


def norm_stats(x):
    center = x - jnp.mean(x, 0, keepdims=True)
    recip = lax.rsqrt(jnp.mean(center * center, 0, keepdims=True) + EPSILON)
    return center * recip, recip


def norm_back(e, scaled, recip, gain):
    lifted = e * gain
    return recip * (
        lifted
        - jnp.mean(lifted, 0, keepdims=True)
        - scaled * jnp.mean(lifted * scaled, 0, keepdims=True)
    )


def split3(x):
    hi = x.astype(BF16)
    rest = x - hi.astype(F32)
    mid = rest.astype(BF16)
    low = (rest - mid.astype(F32)).astype(BF16)
    return hi, mid, low


def aug_rows(x):
    hi, mid, low = split3(x)
    row = lax.broadcasted_iota(jnp.int32, (16, x.shape[1]), 0)
    zero = jnp.zeros((16, x.shape[1]), F32)
    out = jnp.where(row == 0, hi.astype(F32), zero)
    out = jnp.where(row == 1, mid.astype(F32), out)
    out = jnp.where(row == 2, low.astype(F32), out)
    return out.astype(BF16)


def one_hot(target_ref, copy):
    place = lax.broadcasted_iota(jnp.int32, (target_ref.shape[0], L), 1)
    return (target_ref[...] - copy * L == place).astype(F32)


def pre_kernel(arrived, target, wp, cols, pos, win, bin_col, stream_out, q_out, kv_out, k_rows, v_rows):
    copy = pl.program_id(0)
    width = wp.shape[1]
    proj = dg(arrived[...], wp[...], 1, 0).astype(BF16)
    hot = one_hot(target, copy)
    covered = jnp.sum(hot, 0, keepdims=True)
    stream = dg(proj, hot.astype(BF16), 0, 0) + (1.0 - covered) * cols[:, 0:1] + pos[...]
    stream_out[0] = stream
    scaled, _ = norm_stats(stream)
    normed = (scaled * cols[:, 1:2] + cols[:, 2:3]).astype(BF16)
    lane = lax.broadcasted_iota(jnp.int32, (L, LANES), 1)
    ones = (lane < HEAD + 3).astype(BF16)
    for part in range(3):
        sl = slice(part * width, (part + 1) * width)
        mixed = dg(win[:, sl], normed, 0, 0) + bin_col[sl, :]
        if part == 0:
            q_out[0, :, :L] = (mixed * Q_SCALE).astype(BF16)
            q_out[0, :, L:] = jnp.zeros((width, LP - L), BF16)
        else:
            mixed = mixed.astype(BF16)
            kv_out[0, (part - 1) * width : part * width, :] = mixed
            dst = k_rows if part == 1 else v_rows
            for h in range(H):
                dst[0, h] = ones
                dst[0, h, :, :HEAD] = mixed[h * HEAD : (h + 1) * HEAD].T


def pre(arrived, target, wp, cols, pos, win, bin_col):
    a, e = arrived.shape
    d = wp.shape[1]
    const = lambda *s: pl.BlockSpec(s, lambda c: (0,) * len(s))
    lead = lambda *s: pl.BlockSpec((1,) + s, lambda c: (c,) + (0,) * len(s))
    return pl.pallas_call(
        pre_kernel,
        grid=(2,),
        in_specs=[const(a, e), const(a, 1), const(e, d), const(d, 8), const(d, L), const(d, 3 * d), const(3 * d, 1)],
        out_specs=[lead(d, L), lead(d, LP), lead(2 * d, L), lead(H, L, LANES), lead(H, L, LANES)],
        out_shape=[
            jax.ShapeDtypeStruct((2, d, L), F32),
            jax.ShapeDtypeStruct((2, d, LP), BF16),
            jax.ShapeDtypeStruct((2, 2 * d, L), BF16),
            jax.ShapeDtypeStruct((2, H, L, LANES), BF16),
            jax.ShapeDtypeStruct((2, H, L, LANES), BF16),
        ],
        compiler_params=params(),
    )(arrived, target, wp, cols, pos, win, bin_col)


def attend_kernel(k_rows, q, kt, vt, o_out, lse_out, v_aug):
    row = lax.broadcasted_iota(jnp.int32, (16, L), 0)
    v_aug[:HEAD] = vt[0]
    v_aug[HEAD:] = (row == 0).astype(F32).astype(BF16)
    qf = q[0].astype(F32)
    kf = kt[0].astype(F32)
    bound = jnp.max(jnp.sum(qf * qf, 0, keepdims=True)) * jnp.max(jnp.sum(kf * kf, 0, keepdims=True))
    safe = bound <= SAFE_EXPONENT * SAFE_EXPONENT

    def run(shift):
        for start, size in Q_BLOCKS:
            sl = slice(start, start + size)
            s = dg(k_rows[0, 0, :, :HEAD], q[0, :, sl], 1, 0)
            top = 0.0
            if shift:
                top = jnp.max(s, 0, keepdims=True)
                s = s - top
            e = jnp.exp2(s).astype(BF16)
            o = dg(v_aug[...], e, 1, 0)
            total = o[HEAD : HEAD + 1]
            o_out[0, :, sl] = o[:HEAD] * (1.0 / total)
            lse_out[0, 0, :, sl] = aug_rows(-(top + jnp.log2(total)))

    pl.when(safe)(lambda: run(False))
    pl.when(jnp.logical_not(safe))(lambda: run(True))


def attend(k_rows, q, kv):
    d = q.shape[1]
    head = lambda off: (lambda i: (i // H, i % H + off, 0))
    return pl.pallas_call(
        attend_kernel,
        grid=(2 * H,),
        in_specs=[
            pl.BlockSpec((1, 1, L, LANES), lambda i: (i // H, i % H, 0, 0)),
            pl.BlockSpec((1, HEAD, LP), head(0)),
            pl.BlockSpec((1, HEAD, L), head(0)),
            pl.BlockSpec((1, HEAD, L), head(H)),
        ],
        out_specs=[
            pl.BlockSpec((1, HEAD, LP), head(0)),
            pl.BlockSpec((1, 1, 16, LP), lambda i: (i // H, i % H, 0, 0)),
        ],
        out_shape=[
            jax.ShapeDtypeStruct((2, d, LP), F32),
            jax.ShapeDtypeStruct((2, H, 16, LP), BF16),
        ],
        scratch_shapes=[pltpu.VMEM((HEAD + 16, L), BF16)],
        compiler_params=params(),
    )(k_rows, q, kv, kv)


def attend_back_kernel(k_rows, v_rows, q, lse, do, dsum, kt, dq, dk, dv, q_aug, do_aug):
    q_aug[:HEAD] = q[0]
    q_aug[HEAD : HEAD + 16] = lse[0, 0]
    q_aug[HEAD + 16 :] = jnp.zeros((LANES - HEAD - 16, LP), BF16)
    do_aug[:HEAD] = do[0]
    do_aug[HEAD : HEAD + 16] = dsum[0, 0]
    do_aug[HEAD + 16 :] = jnp.zeros((LANES - HEAD - 16, LP), BF16)
    k_sum = None
    v_sum = None
    for start, size in Q_BLOCKS:
        sl = slice(start, start + size)
        p = jnp.exp2(dg(k_rows[0, 0], q_aug[:, sl], 1, 0))
        dp = dg(v_rows[0, 0], do_aug[:, sl], 1, 0)
        ds = (p * dp).astype(BF16)
        v_part = dg(do_aug[:HEAD, sl], p.astype(BF16), 1, 1)
        k_part = dg(q_aug[:HEAD, sl], ds, 1, 1)
        v_sum = v_part if v_sum is None else v_sum + v_part
        k_sum = k_part if k_sum is None else k_sum + k_part
        if start + size == LP:
            dq[0, :, start:] = (dg(kt[0], ds, 1, 0)[:, : L - start] * (1.0 / math.sqrt(HEAD))).astype(BF16)
        else:
            dq[0, :, sl] = (dg(kt[0], ds, 1, 0) * (1.0 / math.sqrt(HEAD))).astype(BF16)
    dk[0] = (k_sum * (1.0 / LOG2E)).astype(BF16)
    dv[0] = v_sum.astype(BF16)


def attend_back(k_rows, v_rows, q, lse, do, dsum, kv):
    d = q.shape[1]
    head = lambda i: (i // H, i % H, 0)
    wide = lambda i: (i // H, i % H, 0, 0)
    return pl.pallas_call(
        attend_back_kernel,
        grid=(2 * H,),
        in_specs=[
            pl.BlockSpec((1, 1, L, LANES), wide),
            pl.BlockSpec((1, 1, L, LANES), wide),
            pl.BlockSpec((1, HEAD, LP), head),
            pl.BlockSpec((1, 1, 16, LP), wide),
            pl.BlockSpec((1, HEAD, LP), head),
            pl.BlockSpec((1, 1, 16, LP), wide),
            pl.BlockSpec((1, HEAD, L), head),
        ],
        out_specs=[pl.BlockSpec((1, HEAD, L), head)] * 3,
        out_shape=[jax.ShapeDtypeStruct((2, d, L), BF16)] * 3,
        scratch_shapes=[pltpu.VMEM((LANES, LP), BF16)] * 2,
        compiler_params=params(),
    )(k_rows, v_rows, q, lse, do, dsum, kv)


def mid_kernel(o, stream, up, wm, we, wr, be, cols,
               dec, ga_out, do_out, dsum_out, dwm, dwe, dwr, dvec, dbe, drb,
               after, stats, n2, act_s, gl_s, g_s):
    copy = pl.program_id(0)
    ff = pl.program_id(1)
    last = pl.num_programs(1) - 1
    d = wm.shape[0]

    @pl.when((copy == 0) & (ff == 0))
    def _():
        dwm[...] = jnp.zeros_like(dwm)
        dwe[...] = jnp.zeros_like(dwe)
        dwr[...] = jnp.zeros_like(dwr)
        dvec[...] = jnp.zeros_like(dvec)
        dbe[...] = jnp.zeros_like(dbe)
        drb[...] = jnp.zeros_like(drb)

    @pl.when(ff == 0)
    def _():
        ctx = o[0, :, :L].astype(BF16)
        x = stream[0] + dg(wm[...], ctx, 0, 0) + cols[:, 3:4]
        after[...] = x
        mean = jnp.mean(x, 0, keepdims=True)
        center = x - mean
        recip = lax.rsqrt(jnp.mean(center * center, 0, keepdims=True) + EPSILON)
        stats[0:1] = mean
        stats[1:2] = recip
        n2[:d] = (center * recip * cols[:, 4:5] + cols[:, 5:6]).astype(BF16)
        row = lax.broadcasted_iota(jnp.int32, (16, L), 0)
        n2[d:] = (row == 0).astype(F32).astype(BF16)
        g = (up[0].astype(F32) * 0.5).astype(BF16)
        g_s[...] = g
        drb[...] += dg(jnp.ones((8, L), BF16), g, 1, 0)

    rows = pl.ds(pl.multiple_of(ff * FFC, FFC), FFC)
    g = g_s[...]
    lifted = dg(we[:, rows], n2[:d], 0, 0) + be[rows, :]
    bell = jnp.exp(-0.5 * lifted * lifted)
    cdf = 0.5 * (1.0 + lax.erf(lifted * ROOT_HALF))
    act = (lifted * cdf).astype(BF16)
    slope = cdf + lifted * bell * INV_ROOT_TWO_PI
    gl = (dg(wr[rows, :], g, 1, 1) * slope).astype(BF16)
    act_s[rows, :] = act
    gl_s[rows, :] = gl
    dwr[rows, :] += dg(act, g, 1, 0)
    grad = dg(n2[...], gl, 1, 1)
    dwe[:, rows] += grad[:d]
    dbe[:, rows] += grad[d : d + 8]

    @pl.when(ff == last)
    def _():
        x = after[...]
        out = x + dg(wr[...], act_s[...], 0, 0) + cols[:, 6:7]
        dec[0] = out.astype(BF16).T
        scaled = (x - stats[0:1]) * stats[1:2]
        e = dg(we[...], gl_s[...], 1, 0)
        dvec[:, 0:1] += jnp.sum(e * scaled, 1, keepdims=True)
        dvec[:, 1:2] += jnp.sum(e, 1, keepdims=True)
        back = norm_back(e, scaled, stats[1:2], cols[:, 4:5])
        ga = g_s[...].T.astype(F32) + back
        ga_out[0] = ga
        gm = ga.astype(BF16)
        dvec[:, 2:3] += jnp.sum(gm.astype(F32), 1, keepdims=True)
        ctx = o[0, :, :L]
        dwm[...] += dg(ctx.astype(BF16), gm, 1, 1)
        do = dg(wm[...], gm, 1, 0).astype(BF16)
        do_out[0, :, :L] = do
        do_out[0, :, L:] = jnp.zeros((d, LP - L), BF16)
        prod = do.astype(F32) * ctx
        for h in range(H):
            dsum_out[0, h, :, :L] = aug_rows(
                -jnp.sum(prod[h * HEAD : (h + 1) * HEAD], 0, keepdims=True)
            )
            dsum_out[0, h, :, L:] = jnp.zeros((16, LP - L), BF16)


def mid(o, stream, up, wm, we, wr, be, cols):
    d = wm.shape[0]
    f = we.shape[1]
    once = pl.Buffered(1)
    const = lambda *s: pl.BlockSpec(s, lambda c, k: (0,) * len(s), pipeline_mode=once)
    acc = lambda *s: pl.BlockSpec(s, lambda c, k: (0,) * len(s), pipeline_mode=once)
    lead = lambda *s: pl.BlockSpec((1,) + s, lambda c, k: (c,) + (0,) * len(s))
    shape = jax.ShapeDtypeStruct
    return pl.pallas_call(
        mid_kernel,
        grid=(2, f // FFC),
        in_specs=[lead(d, LP), lead(d, L), lead(L, d), const(d, d), const(d, f), const(f, d), const(f, 1), const(d, 8)],
        out_specs=[
            lead(L, d), lead(d, L), lead(d, LP), lead(H, 16, LP),
            acc(d, d), acc(d, f), acc(f, d), acc(d, LANES), acc(8, f), acc(8, d),
        ],
        out_shape=[
            shape((2, L, d), BF16), shape((2, d, L), F32), shape((2, d, LP), BF16), shape((2, H, 16, LP), BF16),
            shape((d, d), F32), shape((d, f), F32), shape((f, d), F32), shape((d, LANES), F32),
            shape((8, f), F32), shape((8, d), F32),
        ],
        scratch_shapes=[
            pltpu.VMEM((d, L), F32), pltpu.VMEM((8, L), F32), pltpu.VMEM((d + 16, L), BF16),
            pltpu.VMEM((f, L), BF16), pltpu.VMEM((f, L), BF16), pltpu.VMEM((L, d), BF16),
        ],
        compiler_params=params(),
    )(o, stream, up, wm, we, wr, be, cols)


def post_kernel(dq, dk, dv, stream, ga, target, arrived, win, cols, dwin, dbin, dvec, gp_out, dwp, n1, gp_s):
    copy = pl.program_id(0)
    d = win.shape[0]

    @pl.when(copy == 0)
    def _():
        dwin[...] = jnp.zeros_like(dwin)
        dbin[...] = jnp.zeros_like(dbin)
        dvec[...] = jnp.zeros_like(dvec)
        gp_s[...] = jnp.zeros_like(gp_s)

    x = stream[0]
    scaled, recip = norm_stats(x)
    n1[:d] = (scaled * cols[:, 1:2] + cols[:, 2:3]).astype(BF16)
    row = lax.broadcasted_iota(jnp.int32, (16, L), 0)
    n1[d:] = (row == 0).astype(F32).astype(BF16)
    e = None
    for part, ref in enumerate((dq, dk, dv)):
        sl = slice(part * d, (part + 1) * d)
        grad = dg(n1[...], ref[0], 1, 1)
        dwin[:, sl] += grad[:d]
        dbin[:, sl] += grad[d : d + 8]
        term = dg(win[:, sl], ref[0], 1, 0)
        e = term if e is None else e + term
    dvec[:, 0:1] += jnp.sum(e * scaled, 1, keepdims=True)
    dvec[:, 1:2] += jnp.sum(e, 1, keepdims=True)
    gs = ga[0] + norm_back(e, scaled, recip, cols[:, 1:2])
    hot = one_hot(target, copy)
    covered = jnp.sum(hot, 0, keepdims=True)
    dvec[:, 2:3] += jnp.sum(gs * (1.0 - covered), 1, keepdims=True)
    gp_s[...] += dg(hot.astype(BF16), gs.astype(BF16), 1, 1)

    @pl.when(copy == 1)
    def _():
        gp = gp_s[...].astype(BF16)
        gp_out[...] = gp
        dwp[...] = dg(arrived[...], gp, 0, 0)


def post(dq, dk, dv, stream, ga, target, arrived, win, cols):
    a, e = arrived.shape
    d = win.shape[0]
    once = pl.Buffered(1)
    const = lambda *s: pl.BlockSpec(s, lambda c: (0,) * len(s), pipeline_mode=once)
    lead = lambda *s: pl.BlockSpec((1,) + s, lambda c: (c,) + (0,) * len(s))
    shape = jax.ShapeDtypeStruct
    return pl.pallas_call(
        post_kernel,
        grid=(2,),
        in_specs=[lead(d, L), lead(d, L), lead(d, L), lead(d, L), lead(d, L), const(a, 1), const(a, e), const(d, 3 * d), const(d, 8)],
        out_specs=[const(d, 3 * d), const(8, 3 * d), const(d, LANES), const(a, d), const(e, d)],
        out_shape=[shape((d, 3 * d), F32), shape((8, 3 * d), F32), shape((d, LANES), F32), shape((a, d), BF16), shape((e, d), F32)],
        scratch_shapes=[pltpu.VMEM((d + 16, L), BF16), pltpu.VMEM((a, d), F32)],
        compiler_params=params(),
    )(dq, dk, dv, stream, ga, target, arrived, win, cols)


def layer(arrived, target, up, w):
    (wp, token, gain1, shift1, win, bq, bv, wm, bm, gain2, shift2, we, be, wr, br) = w
    d = wp.shape[1]
    f = lambda v: v.astype(F32)
    cols = jnp.stack([f(token), f(gain1), f(shift1), f(bm), f(gain2), f(shift2), f(br), jnp.zeros((d,), F32)], 1)
    bin_col = jnp.concatenate([f(bq), jnp.zeros((d,), F32), f(bv)])[:, None]
    pos = jnp.asarray(position_table(d))
    tcol = target[:, None]
    stream, q, kv, k_rows, v_rows = pre(arrived, tcol, wp, cols, pos, win, bin_col)
    o, lse = attend(k_rows, q, kv)
    dec, ga, do, dsum, dwm, dwe, dwr, vec2, dbe, drb = mid(
        o, stream, up.reshape(2, L, d), wm, we, wr, f(be)[:, None], cols
    )
    dq, dk, dv = attend_back(k_rows, v_rows, q, lse, do, dsum, kv)
    dwin, dbin, vec1, gp, dwp = post(dq, dk, dv, stream, ga, tcol, arrived, win, cols)
    grads = (
        dwp, vec1[:, 2], vec1[:, 0], vec1[:, 1], dwin, dbin[0, :d], dbin[0, 2 * d :], dwm, vec2[:, 2],
        vec2[:, 0], vec2[:, 1], dwe, dbe[0], dwr, drb[0],
    )
    return dec.reshape(2 * L, d), gp, grads


def per_device(encoded, visible_at, *rest):
    weights, upstream = rest[:-1], rest[-1]
    clip_count = lax.axis_size("clip")
    my_clip = lax.axis_index("clip")
    held, width_in = encoded.shape
    seen = visible_at.shape[1]
    d = weights[0].shape[1]
    cap = -(-held // clip_count)
    cap = -(-cap // 16) * 16
    peer = jnp.arange(clip_count, dtype=jnp.int32)[:, None]
    slot = jnp.arange(cap, dtype=jnp.int32)[None, :]
    first_out = (peer * held - my_clip + clip_count - 1) // clip_count
    picked = jnp.take(encoded, jnp.clip(first_out + slot, 0, held - 1).reshape(-1), axis=0)
    arrived = lax.all_to_all(
        picked.reshape(clip_count, cap, width_in), "clip", split_axis=0, concat_axis=0, tiled=True
    ).reshape(clip_count * cap, width_in)
    first_in = (my_clip * held - peer + clip_count - 1) // clip_count
    local = peer + clip_count * (first_in + slot) - my_clip * held
    valid = (local < held).reshape(-1)
    local = jnp.clip(local, 0, held - 1).reshape(-1)
    target = jnp.take(visible_at.reshape(-1), local) + local // seen * L
    target = jnp.where(valid, target, -1)
    big = [i for i, v in enumerate(weights) if v.ndim == 2]
    small = [i for i, v in enumerate(weights) if v.ndim == 1]
    full = {i: lax.all_gather(weights[i], "wt", axis=0, tiled=True) for i in big}
    packed = lax.all_gather(jnp.concatenate([weights[i] for i in small]), "wt", axis=0)
    at = 0
    for i in small:
        n = weights[i].shape[0]
        full[i] = packed[:, at : at + n].reshape(-1)
        at += n
    w = tuple(full[i] for i in range(len(weights)))
    decoded, gp, grads = layer(arrived, target, upstream, w)
    returned = lax.all_to_all(
        gp.reshape(clip_count, cap, d), "clip", split_axis=0, concat_axis=0, tiled=True
    ).reshape(clip_count * cap, d)
    own = jnp.arange(held, dtype=jnp.int32)
    dest = (my_clip + clip_count * own) // held
    place = dest * cap + own - jnp.take(first_out[:, 0], dest)
    hot = (place[:, None] == jnp.arange(clip_count * cap, dtype=jnp.int32)[None, :]).astype(BF16)
    own_grad = jnp.dot(hot, returned, preferred_element_type=F32).astype(BF16)
    encoded_grad = lax.dot_general(
        own_grad, w[0], (((1,), (1,)), ((), ())), preferred_element_type=F32
    ).astype(BF16)
    out = {}
    scatter = lambda v: lax.psum_scatter(v.astype(BF16), "wt", scatter_dimension=0, tiled=True)
    for i in big:
        out[i] = scatter(grads[i])
    wt = lax.axis_size("wt")
    pack = jnp.concatenate([grads[i].reshape(wt, -1) for i in small], 1)
    pack = scatter(pack)[0]
    total = lax.psum(tuple(out[i] for i in big) + (pack,), "clip")
    for k, i in enumerate(big):
        out[i] = total[k].astype(F32)
    at = 0
    for i in small:
        n = weights[i].shape[0]
        out[i] = total[-1][at : at + n].astype(F32)
        at += n
    return (decoded, encoded_grad) + tuple(out[i] for i in range(len(weights)))


def solution(mesh):
    both, wt = P(("clip", "wt"), None), P("wt")
    mat = P("wt", None)
    params_in = (mat, wt, wt, wt, mat, wt, wt, mat, wt, wt, wt, mat, wt, mat, wt)
    return jax.shard_map(
        per_device,
        mesh=mesh,
        in_specs=(both, both) + params_in + (both,),
        out_specs=(both, both) + params_in,
        check_vma=False,
    )
```

```python
import functools
import math

import jax
import jax.numpy as jnp
import numpy as np
from jax import lax
from jax.experimental import pallas as pl
from jax.experimental.pallas import tpu as pltpu
from jax.sharding import PartitionSpec as P

H = 6
HEAD = 64
L = 1568
LANES = 128
LP = -(-L // LANES) * LANES
EPSILON = 1e-06
LOG2E = math.log2(math.e)
Q_SCALE = LOG2E / math.sqrt(HEAD)
ROOT_HALF = math.sqrt(0.5)
INV_ROOT_TWO_PI = 1.0 / math.sqrt(2.0 * math.pi)
SAFE_EXPONENT = 100.0
VMEM_LIMIT = 60 * 2**20
FFC = 256
Q_BLOCKS = ((0, 896), (896, LP - 896))
F32 = jnp.float32
BF16 = jnp.bfloat16


SEG = 16
ROWS = 384
MESH = pl.DeviceIdType.MESH
TOKEN, GAIN1, SHIFT1, BIAS_Q, BIAS_V, BIAS_M, GAIN2, SHIFT2, BIAS_R, BIAS_E = range(10)


def params(**kw):
    return pltpu.CompilerParams(vmem_limit_bytes=VMEM_LIMIT, **kw)


def cost(flops, moved=0):
    return pl.CostEstimate(flops=int(flops), bytes_accessed=int(moved), transcendentals=0)


def up16(x):
    return -(-x // SEG) * SEG


def segments(parts, share):
    out = []
    at = 0
    for name, rows in parts:
        for r in range(0, rows, SEG):
            out.append((name, r, at // share, at % share))
            at += SEG
    return out


def dg(a, b, ca, cb):
    return lax.dot_general(a, b, (((ca,), (cb,)), ((), ())), preferred_element_type=F32)


def position_table(width):
    places = np.arange(L, dtype=np.float64)[None, :]
    columns = np.arange(width)
    exponent = (2 * (columns // 2)).astype(np.float64) / width
    angles = places / np.power(10000.0, exponent)[:, None]
    return np.where(columns[:, None] % 2 == 0, np.sin(angles), np.cos(angles)).astype(np.float32)


def norm_stats(x):
    center = x - jnp.mean(x, 0, keepdims=True)
    recip = lax.rsqrt(jnp.mean(center * center, 0, keepdims=True) + EPSILON)
    return center * recip, recip


def norm_back(e, scaled, recip, gain):
    lifted = e * gain
    return recip * (
        lifted
        - jnp.mean(lifted, 0, keepdims=True)
        - scaled * jnp.mean(lifted * scaled, 0, keepdims=True)
    )


def split3(x):
    hi = x.astype(BF16)
    rest = x - hi.astype(F32)
    mid = rest.astype(BF16)
    low = (rest - mid.astype(F32)).astype(BF16)
    return hi, mid, low


def aug_rows(x):
    hi, mid, low = split3(x)
    row = lax.broadcasted_iota(jnp.int32, (16, x.shape[1]), 0)
    zero = jnp.zeros((16, x.shape[1]), F32)
    out = jnp.where(row == 0, hi.astype(F32), zero)
    out = jnp.where(row == 1, mid.astype(F32), out)
    out = jnp.where(row == 2, low.astype(F32), out)
    return out.astype(BF16)


def one_hot(vis, width):
    place = lax.broadcasted_iota(jnp.int32, (vis.shape[0], width), 1).astype(F32)
    return (vis == place).astype(F32)


def first_slot(dest, held, clip, n):
    return (dest * held - clip + n - 1) // n


def interleave(rows, cols, clip, source, held, seen, seen_pad, n, by_row):
    first = (clip * held - source + n - 1) // n
    base = source + n * first - clip * held
    place = lax.broadcasted_iota(jnp.int32, (rows, cols), 0 if by_row else 1)
    slot = lax.broadcasted_iota(jnp.int32, (rows, cols), 1 if by_row else 0)
    second = place >= seen_pad
    local = jnp.where(second, place - (seen_pad - seen), place)
    good = (place < seen) | (second & (place < seen_pad + seen))
    return (good & (local == base + n * slot)).astype(F32).astype(BF16)


def greet(n, m, clip, wt):
    barrier = pltpu.get_barrier_semaphore()
    for k in range(1, n):
        pl.semaphore_signal(barrier, inc=1, device_id=(lax.rem(clip + k, n), wt), device_id_type=MESH)
    for k in range(1, m):
        pl.semaphore_signal(barrier, inc=1, device_id=(clip, lax.rem(wt + k, m)), device_id_type=MESH)
    pl.semaphore_wait(barrier, n + m - 2)


def remote(src, dst, send, recv, clip, wt):
    return pltpu.make_async_remote_copy(
        src_ref=src, dst_ref=dst, send_sem=send, recv_sem=recv, device_id=(clip, wt), device_id_type=MESH
    )


def enter_kernel(n, m, share, cap, seen_pad, *refs):
    (enc, vis_in, wp_in, win_in, *vecs) = refs[:14]
    (seen_out, vis_out, wp, win, cols, be) = refs[14:20]
    (pack, gath, out_rows, in_rows, vec_s, vis_s, zs, zr, bs, br, fs, fr, rs, rr) = refs[20:]
    clip = lax.axis_index("clip")
    wt = lax.axis_index("wt")
    held = enc.shape[0]
    seen = vis_in.shape[1]
    wp_rows = wp_in.shape[0]
    win_rows = win_in.shape[0]
    half = n // 2
    plan = segments(
        [("wp", wp_rows)] + [(j, win_rows) for j in range(3)] + [("vec", SEG)], share
    )
    vec_s[...] = jnp.zeros_like(vec_s)
    for i, ref in enumerate(vecs):
        vec_s[i : i + 1, : ref.shape[1]] = ref[...].astype(F32)
    for name, r, slot, at in plan:
        if name == "wp":
            piece = wp_in[r : r + SEG]
        elif name == "vec":
            piece = vec_s[...].astype(BF16)
        else:
            piece = win_in[r : r + SEG, name * ROWS : (name + 1) * ROWS]
        pack[slot, at : at + SEG] = piece
    for at in range(len(plan) * SEG, n * share, SEG):
        pack[at // share, at % share : at % share + SEG] = jnp.zeros((SEG, ROWS), BF16)
    greet(n, m, clip, wt)

    sends = []
    for k in range(1, m):
        copy = remote(pack.at[clip], gath.at[clip, wt], zs.at[k], zr.at[k], clip, lax.rem(wt + k, m))
        copy.start()
        sends.append(copy)
    gath[clip, wt] = pack[clip]

    rows_at = lax.broadcasted_iota(jnp.int32, (cap, held), 0)
    cols_at = lax.broadcasted_iota(jnp.int32, (cap, held), 1)
    row_sends = []
    for k in [*range(2, n, 2), *range(3, n, 2), 1, 0] if n > 2 else range(n - 1, -1, -1):
        dest = lax.rem(clip + k, n)
        hot = (rows_at + first_slot(dest, held, clip, n) == cols_at).astype(F32).astype(BF16)
        rows = dg(hot, enc[...], 1, 0).astype(BF16)
        if k == 0:
            in_rows[clip] = rows
        else:
            out_rows[k] = rows
            copy = remote(out_rows.at[k], in_rows.at[clip], rs.at[k], rr.at[k], dest, wt)
            copy.start()
            row_sends.append(copy)

    for k in range(1, m):
        source = lax.rem(wt - k + m, m)
        remote(pack.at[clip], gath.at[clip, source], zs.at[k], zr.at[k], clip, source).wait_recv()
    for j in range(1, half):
        copy = remote(gath.at[clip], gath.at[clip], bs.at[j], br.at[j], lax.rem(clip + 2 * j, n), wt)
        copy.start()
        sends.append(copy)
    partner = clip + 1 - 2 * lax.rem(clip, 2)
    copy = remote(gath.at[clip], gath.at[clip], fs.at[0], fr.at[0], partner, wt)
    copy.start()
    sends.append(copy)

    vis_s[...] = jnp.full(vis_s.shape, -1.0, F32)
    vis_s[0:2, :seen] = vis_in[...].astype(F32)
    turned = vis_s[...].T
    for copy_at in range(2):
        vis_out[copy_at] = turned[:seen_pad, copy_at : copy_at + 1]

    for j in range(1, half):
        source = lax.rem(clip - 2 * j + n, n)
        remote(gath.at[source], gath.at[source], bs.at[j], br.at[j], source, wt).wait_recv()
        copy = remote(gath.at[source], gath.at[source], fs.at[j], fr.at[j], partner, wt)
        copy.start()
        sends.append(copy)

    for k in range(1, n):
        source = lax.rem(clip - k + n, n)
        remote(out_rows.at[k], in_rows.at[source], rs.at[k], rr.at[k], source, wt).wait_recv()
    total = None
    for source in range(n):
        hot = interleave(2 * seen_pad, cap, clip, source, held, seen, seen_pad, n, True)
        part = dg(hot, in_rows[source], 1, 0)
        total = part if total is None else total + part
    total = total.astype(BF16)
    seen_out[0] = total[:seen_pad]
    seen_out[1] = total[seen_pad:]

    for j in range(half):
        source = lax.rem(partner - 2 * j + n, n)
        remote(gath.at[source], gath.at[source], fs.at[j], fr.at[j], partner, wt).wait_recv()
    for z in range(m):
        for name, r, slot, at in plan:
            piece = gath[slot, z, at : at + SEG]
            if name == "wp":
                wp[z * wp_rows + r : z * wp_rows + r + SEG] = piece
            elif name == "vec":
                turned = piece.astype(F32).T
                small = vecs[0].shape[1]
                cols[z * small : (z + 1) * small] = turned[:small]
                large = vecs[BIAS_E].shape[1]
                be[z * large : (z + 1) * large] = turned[:large, BIAS_E : BIAS_E + 1]
            else:
                win[z * win_rows + r : z * win_rows + r + SEG, name * ROWS : (name + 1) * ROWS] = piece
    for copy in sends + row_sends:
        copy.wait_send()


def enter(n, m, enc, vis, wp, win, vecs):
    held, e = enc.shape
    seen = vis.shape[1]
    seen_pad = up16(seen)
    d = wp.shape[1]
    cap = up16(-(-held // n))
    share = up16(-(-(wp.shape[0] + 3 * win.shape[0] + SEG) // n))
    whole = pl.BlockSpec(memory_space=pltpu.VMEM)
    shape = jax.ShapeDtypeStruct
    dma = pltpu.SemaphoreType.DMA
    ins = (enc, vis, wp, win, *[v[None, :] for v in vecs])
    return pl.pallas_call(
        functools.partial(enter_kernel, n, m, share, cap, seen_pad),
        in_specs=[whole] * len(ins),
        out_specs=[whole] * 6,
        out_shape=[
            shape((2, seen_pad, e), BF16), shape((2, seen_pad, 1), F32), shape((e, d), BF16),
            shape((d, 3 * d), BF16), shape((d, 16), F32), shape((vecs[BIAS_E].shape[0] * m, 1), F32),
        ],
        scratch_shapes=[
            pltpu.VMEM((n, share, ROWS), BF16), pltpu.VMEM((n, m, share, ROWS), BF16),
            pltpu.VMEM((n, cap, e), BF16), pltpu.VMEM((n, cap, e), BF16),
            pltpu.VMEM((SEG, ROWS), F32), pltpu.VMEM((8, 2 * LANES), F32),
            dma((m,)), dma((m,)), dma((n // 2,)), dma((n // 2,)), dma((n // 2,)), dma((n // 2,)), dma((n,)), dma((n,)),
        ],
        compiler_params=params(collective_id=0, has_side_effects=True),
        cost_estimate=cost(6e9, 4e6),
    )(*ins)


def pre_kernel(seen, vis, wp, cols, pos, win, stream_out, q_out, kv_out, k_rows, v_rows):
    width = wp.shape[1]
    proj = dg(seen[0], wp[...], 1, 0).astype(BF16)
    hot = one_hot(vis[0], L)
    covered = jnp.sum(hot, 0, keepdims=True)
    stream = dg(proj, hot.astype(BF16), 0, 0) + (1.0 - covered) * cols[:, TOKEN : TOKEN + 1] + pos[...]
    stream_out[0] = stream
    scaled, _ = norm_stats(stream)
    normed = (scaled * cols[:, GAIN1 : GAIN1 + 1] + cols[:, SHIFT1 : SHIFT1 + 1]).astype(BF16)
    lane = lax.broadcasted_iota(jnp.int32, (L, LANES), 1)
    ones = (lane < HEAD + 3).astype(F32).astype(BF16)
    for part in range(3):
        sl = slice(part * width, (part + 1) * width)
        mixed = dg(win[:, sl], normed, 0, 0)
        if part == 0:
            q_out[0, :, :L] = ((mixed + cols[:, BIAS_Q : BIAS_Q + 1]) * Q_SCALE).astype(BF16)
            q_out[0, :, L:] = jnp.zeros((width, LP - L), BF16)
        else:
            if part == 2:
                mixed = mixed + cols[:, BIAS_V : BIAS_V + 1]
            mixed = mixed.astype(BF16)
            kv_out[0, (part - 1) * width : part * width, :] = mixed
            dst = k_rows if part == 1 else v_rows
            for h in range(H):
                dst[0, h] = ones
                dst[0, h, :, :HEAD] = mixed[h * HEAD : (h + 1) * HEAD].T


def pre(seen, vis, wp, cols, pos, win):
    _, a, e = seen.shape
    d = wp.shape[1]
    const = lambda *s: pl.BlockSpec(s, lambda c: (0,) * len(s))
    lead = lambda *s: pl.BlockSpec((1,) + s, lambda c: (c,) + (0,) * len(s))
    return pl.pallas_call(
        pre_kernel,
        grid=(2,),
        in_specs=[lead(a, e), lead(a, 1), const(e, d), const(d, 16), const(d, L), const(d, 3 * d)],
        out_specs=[lead(d, L), lead(d, LP), lead(2 * d, L), lead(H, L, LANES), lead(H, L, LANES)],
        out_shape=[
            jax.ShapeDtypeStruct((2, d, L), F32),
            jax.ShapeDtypeStruct((2, d, LP), BF16),
            jax.ShapeDtypeStruct((2, 2 * d, L), BF16),
            jax.ShapeDtypeStruct((2, H, L, LANES), BF16),
            jax.ShapeDtypeStruct((2, H, L, LANES), BF16),
        ],
        compiler_params=params(),
        cost_estimate=cost(12e9, 2e7),
    )(seen, vis, wp, cols, pos, win)


def attend_kernel(k_rows, q, kt, vt, o_out, lse_out, v_aug):
    row = lax.broadcasted_iota(jnp.int32, (16, L), 0)
    v_aug[:HEAD] = vt[0]
    v_aug[HEAD:] = (row == 0).astype(F32).astype(BF16)
    qf = q[0].astype(F32)
    kf = kt[0].astype(F32)
    bound = jnp.max(jnp.sum(qf * qf, 0, keepdims=True)) * jnp.max(jnp.sum(kf * kf, 0, keepdims=True))
    safe = bound <= SAFE_EXPONENT * SAFE_EXPONENT

    def run(shift):
        for start, size in Q_BLOCKS:
            sl = slice(start, start + size)
            s = dg(k_rows[0, 0, :, :HEAD], q[0, :, sl], 1, 0)
            top = 0.0
            if shift:
                top = jnp.max(s, 0, keepdims=True)
                s = s - top
            e = jnp.exp2(s).astype(BF16)
            o = dg(v_aug[...], e, 1, 0)
            total = o[HEAD : HEAD + 1]
            o_out[0, :, sl] = o[:HEAD] * (1.0 / total)
            lse_out[0, 0, :, sl] = aug_rows(-(top + jnp.log2(total)))

    pl.when(safe)(lambda: run(False))
    pl.when(jnp.logical_not(safe))(lambda: run(True))


def attend(k_rows, q, kv):
    d = q.shape[1]
    head = lambda off: (lambda i: (i // H, i % H + off, 0))
    return pl.pallas_call(
        attend_kernel,
        grid=(2 * H,),
        in_specs=[
            pl.BlockSpec((1, 1, L, LANES), lambda i: (i // H, i % H, 0, 0)),
            pl.BlockSpec((1, HEAD, LP), head(0)),
            pl.BlockSpec((1, HEAD, L), head(0)),
            pl.BlockSpec((1, HEAD, L), head(H)),
        ],
        out_specs=[
            pl.BlockSpec((1, HEAD, LP), head(0)),
            pl.BlockSpec((1, 1, 16, LP), lambda i: (i // H, i % H, 0, 0)),
        ],
        out_shape=[
            jax.ShapeDtypeStruct((2, d, LP), F32),
            jax.ShapeDtypeStruct((2, H, 16, LP), BF16),
        ],
        scratch_shapes=[pltpu.VMEM((HEAD + 16, L), BF16)],
        compiler_params=params(),
        cost_estimate=cost(3e10, 2e7),
    )(k_rows, q, kv, kv)


def attend_back_kernel(k_rows, v_rows, q, lse, do, dsum, kt, dq, dk, dv, q_aug, do_aug):
    q_aug[:HEAD] = q[0]
    q_aug[HEAD : HEAD + 16] = lse[0, 0]
    q_aug[HEAD + 16 :] = jnp.zeros((LANES - HEAD - 16, LP), BF16)
    do_aug[:HEAD] = do[0]
    do_aug[HEAD : HEAD + 16] = dsum[0, 0]
    do_aug[HEAD + 16 :] = jnp.zeros((LANES - HEAD - 16, LP), BF16)
    k_sum = None
    v_sum = None
    for start, size in Q_BLOCKS:
        sl = slice(start, start + size)
        p = jnp.exp2(dg(k_rows[0, 0], q_aug[:, sl], 1, 0))
        dp = dg(v_rows[0, 0], do_aug[:, sl], 1, 0)
        ds = (p * dp).astype(BF16)
        v_part = dg(do_aug[:HEAD, sl], p.astype(BF16), 1, 1)
        k_part = dg(q_aug[:HEAD, sl], ds, 1, 1)
        v_sum = v_part if v_sum is None else v_sum + v_part
        k_sum = k_part if k_sum is None else k_sum + k_part
        if start + size == LP:
            dq[0, :, start:] = (dg(kt[0], ds, 1, 0)[:, : L - start] * (1.0 / math.sqrt(HEAD))).astype(BF16)
        else:
            dq[0, :, sl] = (dg(kt[0], ds, 1, 0) * (1.0 / math.sqrt(HEAD))).astype(BF16)
    dk[0] = (k_sum * (1.0 / LOG2E)).astype(BF16)
    dv[0] = v_sum.astype(BF16)


def attend_back(k_rows, v_rows, q, lse, do, dsum, kv):
    d = q.shape[1]
    head = lambda i: (i // H, i % H, 0)
    wide = lambda i: (i // H, i % H, 0, 0)
    return pl.pallas_call(
        attend_back_kernel,
        grid=(2 * H,),
        in_specs=[
            pl.BlockSpec((1, 1, L, LANES), wide),
            pl.BlockSpec((1, 1, L, LANES), wide),
            pl.BlockSpec((1, HEAD, LP), head),
            pl.BlockSpec((1, 1, 16, LP), wide),
            pl.BlockSpec((1, HEAD, LP), head),
            pl.BlockSpec((1, 1, 16, LP), wide),
            pl.BlockSpec((1, HEAD, L), head),
        ],
        out_specs=[pl.BlockSpec((1, HEAD, L), head)] * 3,
        out_shape=[jax.ShapeDtypeStruct((2, d, L), BF16)] * 3,
        scratch_shapes=[pltpu.VMEM((LANES, LP), BF16)] * 2,
        compiler_params=params(),
        cost_estimate=cost(8e10, 4e7),
    )(k_rows, v_rows, q, lse, do, dsum, kv)


def mlp_parts(d, f, m):
    return [("wm", d // m)] + [(j, d // m) for j in range(f // ROWS)] + [("wr", f // m)]


def mid_kernel(n, m, share, o, stream, up, wpack, be, cols,
               dec, ga_out, do_out, dsum_out, gpack, vec_out,
               wm, we, wr, dwm, dwe, dwr, dvec, dbe, drb, stats, n2, act_s, gl_s, g_s):
    copy = pl.program_id(0)
    ff = pl.program_id(1)
    last = pl.num_programs(1) - 1
    d = wm.shape[0]
    f = wr.shape[0]
    parts = mlp_parts(d, f, m)

    @pl.when((copy == 0) & (ff == 0))
    def _():
        for z in range(m):
            at = 0
            for name, rows in parts:
                piece = wpack[z, at : at + rows]
                dst = slice(z * rows, (z + 1) * rows)
                if name == "wm":
                    wm[dst] = piece
                elif name == "wr":
                    wr[dst] = piece
                else:
                    we[dst, name * ROWS : (name + 1) * ROWS] = piece
                at += rows
        dwm[...] = jnp.zeros_like(dwm)
        dwe[...] = jnp.zeros_like(dwe)
        dwr[...] = jnp.zeros_like(dwr)
        dvec[...] = jnp.zeros_like(dvec)
        dbe[...] = jnp.zeros_like(dbe)
        drb[...] = jnp.zeros_like(drb)

    @pl.when(ff == 0)
    def _():
        ctx = o[0, :, :L].astype(BF16)
        x = stream[0] + dg(wm[...], ctx, 0, 0) + cols[:, BIAS_M : BIAS_M + 1]
        ga_out[0] = x
        mean = jnp.mean(x, 0, keepdims=True)
        center = x - mean
        recip = lax.rsqrt(jnp.mean(center * center, 0, keepdims=True) + EPSILON)
        stats[0:1] = mean
        stats[1:2] = recip
        n2[:d] = (center * recip * cols[:, GAIN2 : GAIN2 + 1] + cols[:, SHIFT2 : SHIFT2 + 1]).astype(BF16)
        row = lax.broadcasted_iota(jnp.int32, (16, L), 0)
        n2[d:] = (row == 0).astype(F32).astype(BF16)
        g = (up[0].astype(F32) * 0.5).astype(BF16)
        g_s[...] = g
        drb[...] += dg(jnp.ones((8, L), BF16), g, 1, 0)

    rows = pl.ds(pl.multiple_of(ff * FFC, FFC), FFC)
    g = g_s[...]
    lifted = dg(we[:, rows], n2[:d], 0, 0) + be[rows, :]
    bell = jnp.exp(-0.5 * lifted * lifted)
    cdf = 0.5 * (1.0 + lax.erf(lifted * ROOT_HALF))
    act = (lifted * cdf).astype(BF16)
    slope = cdf + lifted * bell * INV_ROOT_TWO_PI
    gl = (dg(wr[rows, :], g, 1, 1) * slope).astype(BF16)
    act_s[rows, :] = act
    gl_s[rows, :] = gl
    dwr[rows, :] += dg(act, g, 1, 0)
    grad = dg(n2[...], gl, 1, 1)
    dwe[:, rows] += grad[:d]
    dbe[:, rows] += grad[d : d + 8]

    @pl.when(ff == last)
    def _():
        x = ga_out[0]
        out = x + dg(wr[...], act_s[...], 0, 0) + cols[:, BIAS_R : BIAS_R + 1]
        dec[0] = out.astype(BF16).T
        scaled = (x - stats[0:1]) * stats[1:2]
        e = dg(we[...], gl_s[...], 1, 0)
        dvec[:, 0:1] += jnp.sum(e * scaled, 1, keepdims=True)
        dvec[:, 1:2] += jnp.sum(e, 1, keepdims=True)
        back = norm_back(e, scaled, stats[1:2], cols[:, GAIN2 : GAIN2 + 1])
        ga = g_s[...].T.astype(F32) + back
        ga_out[0] = ga
        gm = ga.astype(BF16)
        dvec[:, 2:3] += jnp.sum(gm.astype(F32), 1, keepdims=True)
        ctx = o[0, :, :L]
        dwm[...] += dg(ctx.astype(BF16), gm, 1, 1)
        do = dg(wm[...], gm, 1, 0).astype(BF16)
        do_out[0, :, :L] = do
        do_out[0, :, L:] = jnp.zeros((d, LP - L), BF16)
        prod = do.astype(F32) * ctx
        for h in range(H):
            dsum_out[0, h, :, :L] = aug_rows(
                -jnp.sum(prod[h * HEAD : (h + 1) * HEAD], 0, keepdims=True)
            )
            dsum_out[0, h, :, L:] = jnp.zeros((16, LP - L), BF16)

    @pl.when((ff == last) & (copy == 1))
    def _():
        plan = segments(parts, share)
        for z in range(m):
            for name, r, slot, at in plan:
                if name == "wm":
                    piece = dwm[z * (d // m) + r : z * (d // m) + r + SEG]
                elif name == "wr":
                    piece = dwr[z * (f // m) + r : z * (f // m) + r + SEG]
                else:
                    piece = dwe[z * (d // m) + r : z * (d // m) + r + SEG, name * ROWS : (name + 1) * ROWS]
                gpack[slot, z, at : at + SEG] = piece.astype(BF16)
            for at in range(len(plan) * SEG, n * share, SEG):
                gpack[at // share, z, at % share : at % share + SEG] = jnp.zeros((SEG, ROWS), BF16)
        turned = dvec[...].T
        vec_out[...] = jnp.zeros_like(vec_out)
        vec_out[BIAS_M : BIAS_M + 1] = turned[2:3]
        vec_out[GAIN2 : GAIN2 + 1] = turned[0:1]
        vec_out[SHIFT2 : SHIFT2 + 1] = turned[1:2]
        vec_out[BIAS_R : BIAS_R + 1] = drb[0:1]
        for j in range(f // ROWS):
            vec_out[BIAS_E + j : BIAS_E + j + 1] = dbe[0:1, j * ROWS : (j + 1) * ROWS]


def mid(n, m, share, o, stream, up, wpack, be, cols):
    d = cols.shape[0]
    f = be.shape[0]
    once = pl.Buffered(1)
    const = lambda *s: pl.BlockSpec(s, lambda c, k: (0,) * len(s), pipeline_mode=once)
    lead = lambda *s: pl.BlockSpec((1,) + s, lambda c, k: (c,) + (0,) * len(s))
    shape = jax.ShapeDtypeStruct
    vm = pltpu.VMEM
    return pl.pallas_call(
        functools.partial(mid_kernel, n, m, share),
        grid=(2, f // FFC),
        in_specs=[lead(d, LP), lead(d, L), lead(L, d), const(*wpack.shape), const(f, 1), const(d, 16)],
        out_specs=[
            lead(L, d), lead(d, L), lead(d, LP), lead(H, 16, LP), const(n, m, share, ROWS), const(16, d),
        ],
        out_shape=[
            shape((2, L, d), BF16), shape((2, d, L), F32), shape((2, d, LP), BF16), shape((2, H, 16, LP), BF16),
            shape((n, m, share, ROWS), BF16), shape((16, d), F32),
        ],
        scratch_shapes=[
            vm((d, d), BF16), vm((d, f), BF16), vm((f, d), BF16),
            vm((d, d), F32), vm((d, f), F32), vm((f, d), F32), vm((d, LANES), F32), vm((8, f), F32), vm((8, d), F32),
            vm((8, L), F32), vm((d + 16, L), BF16),
            vm((f, L), BF16), vm((f, L), BF16), vm((L, d), BF16),
        ],
        compiler_params=params(),
        cost_estimate=cost(5e10, 4e7),
    )(o, stream, up, wpack, be, cols)


def post_kernel(n, m, share, held, seen_len, dq, dk, dv, stream, ga, seen, vis, win, cols, vec_in,
                gpack, gp_out, dwin, dbin, dvec, dwp, n1, gp_s):
    copy = pl.program_id(0)
    clip = lax.axis_index("clip")
    d = win.shape[0]
    e_width = dwp.shape[0]
    seen_pad = seen.shape[1]
    cap = gp_out.shape[1]

    @pl.when(copy == 0)
    def _():
        dwin[...] = jnp.zeros_like(dwin)
        dbin[...] = jnp.zeros_like(dbin)
        dvec[...] = jnp.zeros_like(dvec)
        dwp[...] = jnp.zeros_like(dwp)

    x = stream[0]
    scaled, recip = norm_stats(x)
    n1[:d] = (scaled * cols[:, GAIN1 : GAIN1 + 1] + cols[:, SHIFT1 : SHIFT1 + 1]).astype(BF16)
    row = lax.broadcasted_iota(jnp.int32, (16, L), 0)
    n1[d:] = (row == 0).astype(F32).astype(BF16)
    e = None
    for part, ref in enumerate((dq, dk, dv)):
        sl = slice(part * d, (part + 1) * d)
        grad = dg(n1[...], ref[0], 1, 1)
        dwin[:, sl] += grad[:d]
        dbin[:, sl] += grad[d : d + 8]
        term = dg(win[:, sl], ref[0], 1, 0)
        e = term if e is None else e + term
    dvec[:, 0:1] += jnp.sum(e * scaled, 1, keepdims=True)
    dvec[:, 1:2] += jnp.sum(e, 1, keepdims=True)
    gs = ga[0] + norm_back(e, scaled, recip, cols[:, GAIN1 : GAIN1 + 1])
    hot = one_hot(vis[0], L)
    covered = jnp.sum(hot, 0, keepdims=True)
    dvec[:, 2:3] += jnp.sum(gs * (1.0 - covered), 1, keepdims=True)
    gp = dg(hot.astype(BF16), gs.astype(BF16), 1, 1).astype(BF16)
    gp_s[pl.ds(pl.multiple_of(copy * seen_pad, SEG), seen_pad), :] = gp
    dwp[...] += dg(seen[0], gp, 0, 0)

    @pl.when(copy == 1)
    def _():
        for source in range(n):
            pick = interleave(cap, 2 * seen_pad, clip, source, held, seen_len, seen_pad, n, False)
            gp_out[source] = dg(pick, gp_s[...], 1, 0).astype(BF16)
        turned = dvec[...].T
        row = lax.broadcasted_iota(jnp.int32, (16, d), 0)
        vec = vec_in[...]
        vec = jnp.where(row == TOKEN, turned[2:3], vec)
        vec = jnp.where(row == GAIN1, turned[0:1], vec)
        vec = jnp.where(row == SHIFT1, turned[1:2], vec)
        vec = jnp.where(row == BIAS_Q, dbin[0:1, :d], vec)
        vec = jnp.where(row == BIAS_V, dbin[0:1, 2 * d :], vec).astype(BF16)
        wp_rows = e_width // m
        win_rows = d // m
        plan = segments([("wp", wp_rows)] + [(j, win_rows) for j in range(3)] + [("vec", SEG)], share)
        for z in range(m):
            for name, r, slot, at in plan:
                if name == "wp":
                    piece = dwp[z * wp_rows + r : z * wp_rows + r + SEG].astype(BF16)
                elif name == "vec":
                    piece = vec
                else:
                    piece = dwin[
                        z * win_rows + r : z * win_rows + r + SEG, name * ROWS : (name + 1) * ROWS
                    ].astype(BF16)
                gpack[slot, z, at : at + SEG] = piece
            for at in range(len(plan) * SEG, n * share, SEG):
                gpack[at // share, z, at % share : at % share + SEG] = jnp.zeros((SEG, ROWS), BF16)


def post(n, m, share, held, seen_len, dq, dk, dv, stream, ga, seen, vis, win, cols, vec_in):
    _, a, e = seen.shape
    d = win.shape[0]
    cap = up16(-(-held // n))
    once = pl.Buffered(1)
    const = lambda *s: pl.BlockSpec(s, lambda c: (0,) * len(s), pipeline_mode=once)
    lead = lambda *s: pl.BlockSpec((1,) + s, lambda c: (c,) + (0,) * len(s))
    shape = jax.ShapeDtypeStruct
    vm = pltpu.VMEM
    return pl.pallas_call(
        functools.partial(post_kernel, n, m, share, held, seen_len),
        grid=(2,),
        in_specs=[
            lead(d, L), lead(d, L), lead(d, L), lead(d, L), lead(d, L), lead(a, e), lead(a, 1),
            const(d, 3 * d), const(d, 16), const(16, d),
        ],
        out_specs=[const(n, m, share, ROWS), const(n, cap, d)],
        out_shape=[shape((n, m, share, ROWS), BF16), shape((n, cap, d), BF16)],
        scratch_shapes=[
            vm((d, 3 * d), F32), vm((8, 3 * d), F32), vm((d, LANES), F32), vm((e, d), F32),
            vm((d + 16, L), BF16), vm((2 * a, d), BF16),
        ],
        compiler_params=params(),
        cost_estimate=cost(2e10, 2e7),
    )(dq, dk, dv, stream, ga, seen, vis, win, cols, vec_in)


def leave_kernel(n, m, gpack, gp, mlp, fin, ret, mlp_out, a1, a2s, a2r, tot, tot_b, brecv, fin_s, ret_s, mlp_s,
                 gs, gr, s1, r1, s2, r2, sb, rb, sc, rc, sm, rm, sf, rf):
    clip = lax.axis_index("clip")
    wt = lax.axis_index("wt")
    half = n // 2
    core = lax.rem(clip, 2)
    chip = clip // 2
    partner = clip + 1 - 2 * core
    mlp_s[clip] = mlp[...]
    greet(n, m, clip, wt)
    sends = []
    order = [*range(1, half), 0]
    for j in order:
        spot = lax.rem(chip + j, half)
        copy = remote(gpack.at[2 * spot + 1 - core], a1.at[j], s1.at[j], r1.at[j], partner, wt)
        copy.start()
        sends.append(copy)
    for k in [*range(2, n, 2), *range(1, n, 2)]:
        dest = lax.rem(clip + k, n)
        copy = remote(gp.at[dest], ret_s.at[clip], gs.at[k], gr.at[k], dest, wt)
        copy.start()
        sends.append(copy)
    ret_s[clip] = gp[clip]
    for j in range(1, half):
        copy = remote(mlp_s.at[clip], mlp_s.at[clip], sm.at[j], rm.at[j], lax.rem(clip + 2 * j, n), wt)
        copy.start()
        sends.append(copy)
    copy = remote(mlp_s.at[clip], mlp_s.at[clip], sf.at[0], rf.at[0], partner, wt)
    copy.start()
    sends.append(copy)
    for j in order:
        spot = lax.rem(chip + j, half)
        mine = 2 * spot + core
        remote(gpack.at[mine], a1.at[j], s1.at[j], r1.at[j], partner, wt).wait_recv()
        both = gpack[mine].astype(F32) + a1[j].astype(F32)
        if j == 0:
            tot[...] = both
        else:
            a2s[j] = both.astype(BF16)
            copy = remote(a2s.at[j], a2r.at[j], s2.at[j], r2.at[j], mine, wt)
            copy.start()
            sends.append(copy)
    for j in range(1, half):
        source = lax.rem(clip - 2 * j + n, n)
        remote(a2s.at[j], a2r.at[j], s2.at[j], r2.at[j], source, wt).wait_recv()
        tot[...] += a2r[j].astype(F32)
    tot_b[...] = tot[...].astype(BF16)
    for k in range(1, m):
        zz = lax.rem(wt + k, m)
        copy = remote(tot_b.at[zz], brecv.at[k], sb.at[k], rb.at[k], clip, zz)
        copy.start()
        sends.append(copy)
    for j in range(1, half):
        source = lax.rem(clip - 2 * j + n, n)
        remote(mlp_s.at[source], mlp_s.at[source], sm.at[j], rm.at[j], source, wt).wait_recv()
        copy = remote(mlp_s.at[source], mlp_s.at[source], sf.at[j], rf.at[j], partner, wt)
        copy.start()
        sends.append(copy)
    total = tot[wt]
    for k in range(1, m):
        source = lax.rem(wt - k + m, m)
        remote(tot_b.at[source], brecv.at[k], sb.at[k], rb.at[k], clip, source).wait_recv()
        total = total + brecv[k].astype(F32)
    fin_s[clip] = total.astype(BF16)
    for k in [*range(2, n, 2), *range(1, n, 2)]:
        dest = lax.rem(clip + k, n)
        copy = remote(fin_s.at[clip], fin_s.at[clip], sc.at[k], rc.at[k], dest, wt)
        copy.start()
        sends.append(copy)
    for k in range(1, n):
        source = lax.rem(clip - k + n, n)
        remote(gp.at[source], ret_s.at[source], gs.at[k], gr.at[k], source, wt).wait_recv()
    ret[...] = ret_s[...]
    for j in range(half):
        source = lax.rem(partner - 2 * j + n, n)
        remote(mlp_s.at[source], mlp_s.at[source], sf.at[j], rf.at[j], partner, wt).wait_recv()
    mlp_out[...] = mlp_s[...]
    for k in range(1, n):
        source = lax.rem(clip - k + n, n)
        remote(fin_s.at[source], fin_s.at[source], sc.at[k], rc.at[k], source, wt).wait_recv()
    fin[...] = fin_s[...]
    for copy in sends:
        copy.wait_send()


def leave(n, m, gpack, gp, mlp):
    _, _, share, _ = gpack.shape
    _, cap, d = gp.shape
    whole = pl.BlockSpec(memory_space=pltpu.VMEM)
    shape = jax.ShapeDtypeStruct
    vm = pltpu.VMEM
    dma = pltpu.SemaphoreType.DMA
    half = n // 2
    return pl.pallas_call(
        functools.partial(leave_kernel, n, m),
        in_specs=[whole] * 3,
        out_specs=[whole] * 3,
        out_shape=[shape((n, share, ROWS), BF16), shape((n, cap, d), BF16), shape((n,) + mlp.shape, BF16)],
        scratch_shapes=[
            vm((half, m, share, ROWS), BF16), vm((half, m, share, ROWS), BF16), vm((half, m, share, ROWS), BF16),
            vm((m, share, ROWS), F32), vm((m, share, ROWS), BF16), vm((m, share, ROWS), BF16),
            vm((n, share, ROWS), BF16), vm((n, cap, d), BF16), vm((n,) + mlp.shape, BF16),
            dma((n,)), dma((n,)), dma((half,)), dma((half,)), dma((half,)), dma((half,)),
            dma((m,)), dma((m,)), dma((n,)), dma((n,)),
            dma((half,)), dma((half,)), dma((half,)), dma((half,)),
        ],
        compiler_params=params(collective_id=1, has_side_effects=True),
        cost_estimate=cost(4e9, 4e6),
    )(gpack, gp, mlp)


def finish_kernel(n, m, plan, mlp_plan, fin, ret, mlp, wp, egrad, dwp, dwin, dwm, dwe, dwr, *vecs):
    clip = lax.axis_index("clip")
    wt = lax.axis_index("wt")
    held = egrad.shape[0]
    cap = ret.shape[1]
    row = lax.broadcasted_iota(jnp.int32, (held, cap), 0)
    col = lax.broadcasted_iota(jnp.int32, (held, cap), 1)
    own = None
    for dest in range(n):
        start = first_slot(dest, held, clip, n)
        stop = first_slot(dest + 1, held, clip, n)
        hot = ((row - start == col) & (row < stop)).astype(F32).astype(BF16)
        part = dg(hot, ret[dest], 1, 0)
        own = part if own is None else own + part
    egrad[...] = dg(own.astype(BF16), wp[...], 1, 1).astype(BF16)
    for name, r, slot, at in plan:
        piece = fin[slot, at : at + SEG].astype(F32)
        if name == "wp":
            dwp[r : r + SEG] = piece
        elif name != "vec":
            dwin[r : r + SEG, name * ROWS : (name + 1) * ROWS] = piece
        else:
            for z in range(m):
                @pl.when(wt == z)
                def _():
                    for i, ref in enumerate(vecs[:BIAS_E]):
                        w = ref.shape[1]
                        ref[...] = piece[i : i + 1, z * w : (z + 1) * w]
                    w = vecs[BIAS_E].shape[1]
                    line = BIAS_E + z * w // ROWS
                    vecs[BIAS_E][...] = piece[line : line + 1, z * w % ROWS : z * w % ROWS + w]
    for name, r, slot, at in mlp_plan:
        piece = mlp[slot, at : at + SEG].astype(F32)
        if name == "wm":
            dwm[r : r + SEG] = piece
        elif name == "wr":
            dwr[r : r + SEG] = piece
        else:
            dwe[r : r + SEG, name * ROWS : (name + 1) * ROWS] = piece


def finish(n, m, held, fin, ret, mlp, wp, f):
    e, d = wp.shape
    whole = pl.BlockSpec(memory_space=pltpu.VMEM)
    shape = jax.ShapeDtypeStruct
    plan = segments([("wp", e // m)] + [(j, d // m) for j in range(3)] + [("vec", SEG)], fin.shape[1])
    mlp_plan = segments(mlp_parts(d, f, m), mlp.shape[1])
    outs = [shape((held, e), BF16)] + [
        shape((r // m, c), F32) for r, c in ((e, d), (d, 3 * d), (d, d), (d, f), (f, d))
    ] + [shape((1, d // m), F32)] * BIAS_E + [shape((1, f // m), F32)]
    return pl.pallas_call(
        functools.partial(finish_kernel, n, m, plan, mlp_plan),
        in_specs=[whole] * 4,
        out_specs=[whole] * len(outs),
        out_shape=outs,
        compiler_params=params(),
        cost_estimate=cost(1e9, 4e6),
    )(fin, ret, mlp, wp)


def per_device(encoded, visible_at, wp, token, gain1, shift1, win, bq, bv, wm, bm, gain2, shift2, we, be, wr, br, upstream):
    n = lax.axis_size("clip")
    m = lax.axis_size("wt")
    held = encoded.shape[0]
    seen_len = visible_at.shape[1]
    d = wp.shape[1]
    f = be.shape[0] * m
    pieces = [wm] + [we[:, j * ROWS : (j + 1) * ROWS] for j in range(f // ROWS)] + [wr]
    local = jnp.concatenate(pieces, 0)
    wpack = lax.all_gather(local, "wt", axis=0, tiled=True).reshape(m, local.shape[0], ROWS)
    vecs = (token, gain1, shift1, bq, bv, bm, gain2, shift2, br, be)
    seen, vis, wp_full, win_full, cols, be_col = enter(n, m, encoded, visible_at, wp, win, vecs)
    pos = jnp.asarray(position_table(d))
    stream, q, kv, k_rows, v_rows = pre(seen, vis, wp_full, cols, pos, win_full)
    o, lse = attend(k_rows, q, kv)
    share = up16(-(-local.shape[0] // n))
    dec, ga, do, dsum, mlp, vec2 = mid(n, m, share, o, stream, upstream.reshape(2, L, d), wpack, be_col, cols)
    mlp = mlp.reshape(n * m * share, ROWS)
    mlp = lax.psum_scatter(mlp, "clip", scatter_dimension=0, tiled=True)
    mlp = lax.psum_scatter(mlp, "wt", scatter_dimension=0, tiled=True)
    dq, dk, dv = attend_back(k_rows, v_rows, q, lse, do, dsum, kv)
    share = up16(-(-(wp.shape[0] + 3 * win.shape[0] + SEG) // n))
    gpack, gp = post(n, m, share, held, seen_len, dq, dk, dv, stream, ga, seen, vis, win_full, cols, vec2)
    fin, ret, mlp = leave(n, m, gpack, gp, mlp)
    egrad, dwp, dwin, dwm, dwe, dwr, *small = finish(n, m, held, fin, ret, mlp, wp_full, f)
    t, g1, s1, vq, vv, vm, g2, s2, vr, ve = [v.reshape(-1) for v in small]
    return (
        dec.reshape(2 * L, d), egrad, dwp, t, g1, s1, dwin, vq, vv, dwm, vm, g2, s2, dwe, ve, dwr, vr,
    )


def solution(mesh):
    both, wt = P(("clip", "wt"), None), P("wt")
    mat = P("wt", None)
    params_in = (mat, wt, wt, wt, mat, wt, wt, mat, wt, wt, wt, mat, wt, mat, wt)
    return jax.shard_map(
        per_device,
        mesh=mesh,
        in_specs=(both, both) + params_in + (both,),
        out_specs=(both, both) + params_in,
        check_vma=False,
    )
```

```python
import functools
import math

import jax
import jax.numpy as jnp
import numpy as np
from jax import lax
from jax.experimental import pallas as pl
from jax.experimental.pallas import tpu as pltpu
from jax.sharding import PartitionSpec as P

H = 6
HEAD = 64
L = 1568
LANES = 128
LP = -(-L // LANES) * LANES
KP = L
EPSILON = 1e-06
LOG2E = math.log2(math.e)
Q_SCALE = LOG2E / math.sqrt(HEAD)
ROOT_HALF = math.sqrt(0.5)
INV_ROOT_TWO_PI = 1.0 / math.sqrt(2.0 * math.pi)
SAFE_EXPONENT = 60.0
VMEM_LIMIT = 60 * 2**20
FFC = 512
Q_BLOCKS = ((0, 896), (896, LP - 896))
F32 = jnp.float32
BF16 = jnp.bfloat16


SEG = 16
ROWS = 384
MESH = pl.DeviceIdType.MESH
TOKEN, GAIN1, SHIFT1, BIAS_Q, BIAS_V, BIAS_M, GAIN2, SHIFT2, BIAS_R, BIAS_E = range(10)


def params(**kw):
    return pltpu.CompilerParams(vmem_limit_bytes=VMEM_LIMIT, **kw)


def cost(flops, moved=0):
    return pl.CostEstimate(flops=int(flops), bytes_accessed=int(moved), transcendentals=0)


def up16(x):
    return -(-x // SEG) * SEG


def segments(parts, share):
    out = []
    at = 0
    for name, rows in parts:
        for r in range(0, rows, SEG):
            out.append((name, r, at // share, at % share))
            at += SEG
    return out


def dg(a, b, ca, cb):
    return lax.dot_general(a, b, (((ca,), (cb,)), ((), ())), preferred_element_type=F32)


def position_table(width):
    places = np.arange(LP, dtype=np.float64)[None, :]
    columns = np.arange(width)
    exponent = (2 * (columns // 2)).astype(np.float64) / width
    angles = places / np.power(10000.0, exponent)[:, None]
    return np.where(columns[:, None] % 2 == 0, np.sin(angles), np.cos(angles)).astype(np.float32)


def norm_stats(x):
    center = x - jnp.mean(x, 0, keepdims=True)
    recip = lax.rsqrt(jnp.mean(center * center, 0, keepdims=True) + EPSILON)
    return center * recip, recip


def norm_back(e, scaled, recip, gain):
    lifted = e * gain
    return recip * (
        lifted
        - jnp.mean(lifted, 0, keepdims=True)
        - scaled * jnp.mean(lifted * scaled, 0, keepdims=True)
    )


def split3(x):
    hi = x.astype(BF16)
    rest = x - hi.astype(F32)
    mid = rest.astype(BF16)
    low = (rest - mid.astype(F32)).astype(BF16)
    return hi, mid, low


def aug_rows(x):
    hi, mid, low = split3(x)
    row = lax.broadcasted_iota(jnp.int32, (16, x.shape[1]), 0)
    zero = jnp.zeros((16, x.shape[1]), F32)
    out = jnp.where(row == 0, hi.astype(F32), zero)
    out = jnp.where(row == 1, mid.astype(F32), out)
    out = jnp.where(row == 2, low.astype(F32), out)
    return out.astype(BF16)


def one_hot(vis, width):
    place = lax.broadcasted_iota(jnp.int32, (vis.shape[0], width), 1).astype(F32)
    return (vis == place).astype(F32)


def first_slot(dest, held, clip, n):
    return (dest * held - clip + n - 1) // n


def interleave(rows, cols, clip, source, held, seen, seen_pad, n, by_row):
    first = (clip * held - source + n - 1) // n
    base = source + n * first - clip * held
    place = lax.broadcasted_iota(jnp.int32, (rows, cols), 0 if by_row else 1)
    slot = lax.broadcasted_iota(jnp.int32, (rows, cols), 1 if by_row else 0)
    second = place >= seen_pad
    local = jnp.where(second, place - (seen_pad - seen), place)
    good = (place < seen) | (second & (place < seen_pad + seen))
    return (good & (local == base + n * slot)).astype(F32).astype(BF16)


def greet(n, m, clip, wt):
    barrier = pltpu.get_barrier_semaphore()
    for k in range(1, n):
        pl.semaphore_signal(barrier, inc=1, device_id=(lax.rem(clip + k, n), wt), device_id_type=MESH)
    for k in range(1, m):
        pl.semaphore_signal(barrier, inc=1, device_id=(clip, lax.rem(wt + k, m)), device_id_type=MESH)
    pl.semaphore_wait(barrier, n + m - 2)


def remote(src, dst, send, recv, clip, wt):
    return pltpu.make_async_remote_copy(
        src_ref=src, dst_ref=dst, send_sem=send, recv_sem=recv, device_id=(clip, wt), device_id_type=MESH
    )


def enter_kernel(n, m, share, cap, seen_pad, *refs):
    (enc, vis_in, wp_in, win_in, *vecs) = refs[:14]
    (seen_out, vis_out, wp, win, cols, be) = refs[14:20]
    (pack, gath, out_rows, in_rows, vec_s, vis_s, zs, zr, bs, br, fs, fr, rs, rr) = refs[20:]
    clip = lax.axis_index("clip")
    wt = lax.axis_index("wt")
    held = enc.shape[0]
    seen = vis_in.shape[1]
    wp_rows = wp_in.shape[0]
    win_rows = win_in.shape[0]
    half = n // 2
    plan = segments(
        [("wp", wp_rows)] + [(j, win_rows) for j in range(3)] + [("vec", SEG)], share
    )
    vec_s[...] = jnp.zeros_like(vec_s)
    for i, ref in enumerate(vecs):
        vec_s[i, : ref.shape[0]] = ref[...].astype(F32)
    for name, r, slot, at in plan:
        if name == "wp":
            piece = wp_in[r : r + SEG]
        elif name == "vec":
            piece = vec_s[...].astype(BF16)
        else:
            piece = win_in[r : r + SEG, name * ROWS : (name + 1) * ROWS]
        pack[slot, at : at + SEG] = piece
    for at in range(len(plan) * SEG, n * share, SEG):
        pack[at // share, at % share : at % share + SEG] = jnp.zeros((SEG, ROWS), BF16)
    greet(n, m, clip, wt)

    sends = []
    partner = clip + 1 - 2 * lax.rem(clip, 2)
    for k in range(1, m):
        copy = remote(pack.at[clip], gath.at[clip, wt], zs.at[k], zr.at[k], clip, lax.rem(wt + k, m))
        copy.start()
        sends.append(copy)
    gath[clip, wt] = pack[clip]

    def spread(k):
        z = lax.rem(wt - k + m, m)
        for j in [*range(1, half), 0]:
            piece = gath.at[clip, z]
            dest = lax.rem(clip + 2 * j, n) if j else partner
            copy = remote(piece, piece, bs.at[j, k], br.at[j, k], dest, wt)
            copy.start()
            sends.append(copy)

    spread(0)

    rows_at = lax.broadcasted_iota(jnp.int32, (cap, held), 0)
    cols_at = lax.broadcasted_iota(jnp.int32, (cap, held), 1)
    row_sends = []
    for k in [*range(2, n, 2), *range(3, n, 2), 1, 0] if n > 2 else range(n - 1, -1, -1):
        dest = lax.rem(clip + k, n)
        hot = (rows_at + first_slot(dest, held, clip, n) == cols_at).astype(F32).astype(BF16)
        rows = dg(hot, enc[...], 1, 0).astype(BF16)
        if k == 0:
            in_rows[clip] = rows
        else:
            out_rows[k] = rows
            copy = remote(out_rows.at[k], in_rows.at[clip], rs.at[k], rr.at[k], dest, wt)
            copy.start()
            row_sends.append(copy)

    for k in range(1, m):
        source = lax.rem(wt - k + m, m)
        remote(pack.at[clip], gath.at[clip, source], zs.at[k], zr.at[k], clip, source).wait_recv()
        spread(k)

    vis_s[...] = jnp.full(vis_s.shape, -1.0, F32)
    vis_s[0:2, :seen] = vis_in[...].astype(F32)
    turned = vis_s[...].T
    for copy_at in range(2):
        vis_out[copy_at] = turned[:seen_pad, copy_at : copy_at + 1]

    for k in range(m):
        z = lax.rem(wt - k + m, m)
        for j in range(1, half):
            source = lax.rem(clip - 2 * j + n, n)
            piece = gath.at[source, z]
            remote(piece, piece, bs.at[j, k], br.at[j, k], source, wt).wait_recv()
            copy = remote(piece, piece, fs.at[j, k], fr.at[j, k], partner, wt)
            copy.start()
            sends.append(copy)

    for k in range(1, n):
        source = lax.rem(clip - k + n, n)
        remote(out_rows.at[k], in_rows.at[source], rs.at[k], rr.at[k], source, wt).wait_recv()
    total = None
    for source in range(n):
        hot = interleave(2 * seen_pad, cap, clip, source, held, seen, seen_pad, n, True)
        part = dg(hot, in_rows[source], 1, 0)
        total = part if total is None else total + part
    total = total.astype(BF16)
    seen_out[0] = total[:seen_pad]
    seen_out[1] = total[seen_pad:]

    for k in range(m):
        z = lax.rem(wt - k + m, m)
        for j in range(half):
            source = lax.rem(partner - 2 * j + n, n)
            piece = gath.at[source, z]
            sems = (fs.at[j, k], fr.at[j, k]) if j else (bs.at[0, k], br.at[0, k])
            remote(piece, piece, *sems, partner, wt).wait_recv()
    for z in range(m):
        for name, r, slot, at in plan:
            piece = gath[slot, z, at : at + SEG]
            if name == "wp":
                wp[z * wp_rows + r : z * wp_rows + r + SEG] = piece
            elif name == "vec":
                turned = piece.astype(F32).T
                small = vecs[0].shape[0]
                cols[z * small : (z + 1) * small] = turned[:small]
                large = vecs[BIAS_E].shape[0]
                be[z * large : (z + 1) * large] = turned[:large, BIAS_E : BIAS_E + 1]
            else:
                win[z * win_rows + r : z * win_rows + r + SEG, name * ROWS : (name + 1) * ROWS] = piece
    for copy in sends + row_sends:
        copy.wait_send()


def pack_kernel(wm, we, wr, out, sems):
    rows = wm.shape[0]
    moves = [(wm, 0, rows)]
    moves += [(we.at[:, j * ROWS : (j + 1) * ROWS], rows * (j + 1), rows) for j in range(we.shape[1] // ROWS)]
    moves += [(wr, rows * len(moves), wr.shape[0])]
    copies = []
    for i, (src, at, size) in enumerate(moves):
        copy = pltpu.make_async_copy(src, out.at[at : at + size], sems.at[i])
        copy.start()
        copies.append(copy)
    for copy in copies:
        copy.wait()


def pack_mlp(wm, we, wr):
    rows = wm.shape[0] + wm.shape[0] * (we.shape[1] // ROWS) + wr.shape[0]
    return pl.pallas_call(
        pack_kernel,
        in_specs=[pl.BlockSpec(memory_space=pl.ANY)] * 3,
        out_specs=pl.BlockSpec(memory_space=pl.ANY),
        out_shape=jax.ShapeDtypeStruct((rows, ROWS), BF16),
        scratch_shapes=[pltpu.SemaphoreType.DMA((2 + we.shape[1] // ROWS,))],
        cost_estimate=cost(0, 1.3e6),
    )(wm, we, wr)


def enter(n, m, enc, vis, wp, win, vecs):
    held, e = enc.shape
    seen = vis.shape[1]
    seen_pad = up16(seen)
    d = wp.shape[1]
    cap = up16(-(-held // n))
    share = up16(-(-(wp.shape[0] + 3 * win.shape[0] + SEG) // n))
    whole = pl.BlockSpec(memory_space=pltpu.VMEM)
    shape = jax.ShapeDtypeStruct
    dma = pltpu.SemaphoreType.DMA
    ins = (enc, vis, wp, win, *vecs)
    return pl.pallas_call(
        functools.partial(enter_kernel, n, m, share, cap, seen_pad),
        in_specs=[whole] * len(ins),
        out_specs=[whole] * 6,
        out_shape=[
            shape((2, seen_pad, e), BF16), shape((2, seen_pad, 1), F32), shape((e, d), BF16),
            shape((d, 3 * d), BF16), shape((d, 16), F32), shape((vecs[BIAS_E].shape[0] * m, 1), F32),
        ],
        scratch_shapes=[
            pltpu.VMEM((n, share, ROWS), BF16), pltpu.VMEM((n, m, share, ROWS), BF16),
            pltpu.VMEM((n, cap, e), BF16), pltpu.VMEM((n, cap, e), BF16),
            pltpu.VMEM((SEG, ROWS), F32), pltpu.VMEM((8, 2 * LANES), F32),
            dma((m,)), dma((m,)), dma((n // 2, m)), dma((n // 2, m)), dma((n // 2, m)), dma((n // 2, m)),
            dma((n,)), dma((n,)),
        ],
        compiler_params=params(collective_id=0, has_side_effects=True),
        cost_estimate=cost(6e9, 4e6),
    )(*ins)


def pre_kernel(seen, vis, wp, cols, pos, win, stream_out, q_out, kv_out, k_rows, v_rows):
    width = wp.shape[1]
    proj = dg(seen[0], wp[...], 1, 0).astype(BF16)
    hot = one_hot(vis[0], LP)
    covered = jnp.sum(hot, 0, keepdims=True)
    stream = dg(proj, hot.astype(BF16), 0, 0) + (1.0 - covered) * cols[:, TOKEN : TOKEN + 1] + pos[...]
    stream_out[0] = stream
    scaled, _ = norm_stats(stream)
    normed = (scaled * cols[:, GAIN1 : GAIN1 + 1] + cols[:, SHIFT1 : SHIFT1 + 1]).astype(BF16)
    lane = lax.broadcasted_iota(jnp.int32, (KP, LANES), 1)
    token = lax.broadcasted_iota(jnp.int32, (KP, LANES), 0)
    ones = ((lane < HEAD + 3) & (token < L)).astype(F32).astype(BF16)
    for part in range(3):
        sl = slice(part * width, (part + 1) * width)
        mixed = dg(win[:, sl], normed, 0, 0)
        if part == 0:
            q_out[0] = ((mixed + cols[:, BIAS_Q : BIAS_Q + 1]) * Q_SCALE).astype(BF16)
        else:
            if part == 2:
                mixed = mixed + cols[:, BIAS_V : BIAS_V + 1]
            mixed = mixed.astype(BF16)
            kv_out[0, (part - 1) * width : part * width, :L] = mixed[:, :L]
            kv_out[0, (part - 1) * width : part * width, L:] = jnp.zeros((width, LP - L), BF16)
            dst = k_rows if part == 1 else v_rows
            for h in range(H):
                dst[0, h] = ones
                dst[0, h, :L, :HEAD] = mixed[h * HEAD : (h + 1) * HEAD].T[:L]


def pre(seen, vis, wp, cols, pos, win):
    _, a, e = seen.shape
    d = wp.shape[1]
    const = lambda *s: pl.BlockSpec(s, lambda c: (0,) * len(s))
    lead = lambda *s: pl.BlockSpec((1,) + s, lambda c: (c,) + (0,) * len(s))
    return pl.pallas_call(
        pre_kernel,
        grid=(2,),
        in_specs=[lead(a, e), lead(a, 1), const(e, d), const(d, 16), const(d, LP), const(d, 3 * d)],
        out_specs=[lead(d, LP), lead(d, LP), lead(2 * d, LP), lead(H, KP, LANES), lead(H, KP, LANES)],
        out_shape=[
            jax.ShapeDtypeStruct((2, d, LP), F32),
            jax.ShapeDtypeStruct((2, d, LP), BF16),
            jax.ShapeDtypeStruct((2, 2 * d, LP), BF16),
            jax.ShapeDtypeStruct((2, H, KP, LANES), BF16),
            jax.ShapeDtypeStruct((2, H, KP, LANES), BF16),
        ],
        compiler_params=params(),
        cost_estimate=cost(12e9, 2e7),
    )(seen, vis, wp, cols, pos, win)


def attend_kernel(k_rows, q, kt, vt, o_out, inv_out, e_out, v_aug):
    row = lax.broadcasted_iota(jnp.int32, (16, KP), 0)
    token = lax.broadcasted_iota(jnp.int32, (16, KP), 1)
    v_aug[:HEAD] = vt[0, :, :KP]
    v_aug[HEAD:] = ((row == 0) & (token < L)).astype(F32).astype(BF16)
    qf = q[0].astype(F32)
    kf = kt[0].astype(F32)
    bound = jnp.max(jnp.sum(qf * qf, 0, keepdims=True)) * jnp.max(jnp.sum(kf * kf, 0, keepdims=True))
    safe = bound <= SAFE_EXPONENT * SAFE_EXPONENT

    def run(shift):
        for start, size in Q_BLOCKS:
            sl = slice(start, start + size)
            s = dg(k_rows[0, 0, :, :HEAD], q[0, :, sl], 1, 0)
            if shift:
                key = lax.broadcasted_iota(jnp.int32, (KP, size), 0)
                s = jnp.where(key < L, s, -jnp.inf)
                s = s - jnp.max(s, 0, keepdims=True)
            e = jnp.exp2(s).astype(BF16)
            e_out[0, 0, :, sl] = e
            o = dg(v_aug[...], e, 1, 0)
            inv = 1.0 / o[HEAD : HEAD + 1]
            o_out[0, :, sl] = o[:HEAD] * inv
            inv_out[0, 0, :, sl] = inv

    pl.when(safe)(lambda: run(False))
    pl.when(jnp.logical_not(safe))(lambda: run(True))


def attend(k_rows, q, kv):
    d = q.shape[1]
    head = lambda off: (lambda i: (i // H, i % H + off, 0))
    wide = lambda i: (i // H, i % H, 0, 0)
    return pl.pallas_call(
        attend_kernel,
        grid=(2 * H,),
        in_specs=[
            pl.BlockSpec((1, 1, KP, LANES), wide),
            pl.BlockSpec((1, HEAD, LP), head(0)),
            pl.BlockSpec((1, HEAD, LP), head(0)),
            pl.BlockSpec((1, HEAD, LP), head(H)),
        ],
        out_specs=[
            pl.BlockSpec((1, HEAD, LP), head(0)),
            pl.BlockSpec((1, 1, 1, LP), wide),
            pl.BlockSpec((1, 1, KP, LP), wide),
        ],
        out_shape=[
            jax.ShapeDtypeStruct((2, d, LP), F32),
            jax.ShapeDtypeStruct((2, H, 1, LP), F32),
            jax.ShapeDtypeStruct((2, H, KP, LP), BF16),
        ],
        scratch_shapes=[pltpu.VMEM((HEAD + 16, KP), BF16)],
        compiler_params=params(),
        cost_estimate=cost(3e10, 2e7),
    )(k_rows, q, kv, kv)


def attend_back_kernel(e, v_rows, q, do, dsum, kt, dq, dk, dv, do_aug):
    do_aug[:HEAD] = do[0]
    do_aug[HEAD : HEAD + 16] = dsum[0, 0]
    do_aug[HEAD + 16 :] = jnp.zeros((LANES - HEAD - 16, LP), BF16)
    k_sum = None
    v_sum = None
    for start, size in Q_BLOCKS:
        sl = slice(start, start + size)
        p = e[0, 0, :, sl]
        dp = dg(v_rows[0, 0], do_aug[:, sl], 1, 0)
        ds = (p.astype(F32) * dp).astype(BF16)
        v_part = dg(do_aug[:HEAD, sl], p, 1, 1)
        k_part = dg(q[0, :, sl], ds, 1, 1)
        v_sum = v_part if v_sum is None else v_sum + v_part
        k_sum = k_part if k_sum is None else k_sum + k_part
        dq[0, :, sl] = (dg(kt[0, :, :KP], ds, 1, 0) * (1.0 / math.sqrt(HEAD))).astype(BF16)
    for dst, total in ((dk, k_sum * (1.0 / LOG2E)), (dv, v_sum)):
        dst[0, :, :L] = total[:, :L].astype(BF16)
        dst[0, :, L:] = jnp.zeros((HEAD, LP - L), BF16)


def attend_back(e, v_rows, q, do, dsum, kv):
    d = q.shape[1]
    head = lambda i: (i // H, i % H, 0)
    wide = lambda i: (i // H, i % H, 0, 0)
    return pl.pallas_call(
        attend_back_kernel,
        grid=(2 * H,),
        in_specs=[
            pl.BlockSpec((1, 1, KP, LP), wide),
            pl.BlockSpec((1, 1, KP, LANES), wide),
            pl.BlockSpec((1, HEAD, LP), head),
            pl.BlockSpec((1, HEAD, LP), head),
            pl.BlockSpec((1, 1, 16, LP), wide),
            pl.BlockSpec((1, HEAD, LP), head),
        ],
        out_specs=[pl.BlockSpec((1, HEAD, LP), head)] * 3,
        out_shape=[jax.ShapeDtypeStruct((2, d, LP), BF16)] * 3,
        scratch_shapes=[pltpu.VMEM((LANES, LP), BF16)],
        compiler_params=params(),
        cost_estimate=cost(8e10, 4e7),
    )(e, v_rows, q, do, dsum, kv)


def mlp_parts(d, f, m):
    return [("wm", d // m)] + [(j, d // m) for j in range(f // ROWS)] + [("wr", f // m)]


def mid_kernel(n, m, share, o, inv, stream, up, wpack, be, cols,
               dec, ga_out, do_out, dsum_out, gpack, vec_out,
               wm, we, wr, dwm, dwe, dwr, dvec, dbe, drb, stats, n2, act_s, gl_s, g_s):
    copy = pl.program_id(0)
    ff = pl.program_id(1)
    last = pl.num_programs(1) - 1
    d = wm.shape[0]
    f = wr.shape[0]
    parts = mlp_parts(d, f, m)

    @pl.when((copy == 0) & (ff == 0))
    def _():
        for z in range(m):
            at = 0
            for name, rows in parts:
                piece = wpack[z, at : at + rows]
                dst = slice(z * rows, (z + 1) * rows)
                if name == "wm":
                    wm[dst] = piece
                elif name == "wr":
                    wr[dst] = piece
                else:
                    we[dst, name * ROWS : (name + 1) * ROWS] = piece
                at += rows
        dwm[...] = jnp.zeros_like(dwm)
        dwe[...] = jnp.zeros_like(dwe)
        dwr[...] = jnp.zeros_like(dwr)
        dvec[...] = jnp.zeros_like(dvec)
        dbe[...] = jnp.zeros_like(dbe)
        drb[...] = jnp.zeros_like(drb)

    @pl.when(ff == 0)
    def _():
        ctx = o[0].astype(BF16)
        x = stream[0] + dg(wm[...], ctx, 0, 0) + cols[:, BIAS_M : BIAS_M + 1]
        ga_out[0] = x
        mean = jnp.mean(x, 0, keepdims=True)
        center = x - mean
        recip = lax.rsqrt(jnp.mean(center * center, 0, keepdims=True) + EPSILON)
        stats[0:1] = mean
        stats[1:2] = recip
        n2[:d] = (center * recip * cols[:, GAIN2 : GAIN2 + 1] + cols[:, SHIFT2 : SHIFT2 + 1]).astype(BF16)
        row = lax.broadcasted_iota(jnp.int32, (16, LP), 0)
        n2[d:] = (row == 0).astype(F32).astype(BF16)
        g = (up[0].astype(F32) * 0.5).astype(BF16)
        g_s[:L] = g
        g_s[L:] = jnp.zeros((LP - L, d), BF16)
        drb[...] += dg(jnp.ones((8, L), BF16), g, 1, 0)

    rows = pl.ds(pl.multiple_of(ff * FFC, FFC), FFC)
    g = g_s[...]
    lifted = dg(we[:, rows], n2[:d], 0, 0) + be[rows, :]
    bell = jnp.exp(-0.5 * lifted * lifted)
    cdf = 0.5 * (1.0 + lax.erf(lifted * ROOT_HALF))
    act = (lifted * cdf).astype(BF16)
    slope = cdf + lifted * bell * INV_ROOT_TWO_PI
    gl = (dg(wr[rows, :], g, 1, 1) * slope).astype(BF16)
    act_s[rows, :] = act
    gl_s[rows, :] = gl

    @pl.when(ff == last)
    def _():
        x = ga_out[0]
        dwr[...] += dg(act_s[...], g_s[...], 1, 0)
        grad = dg(n2[...], gl_s[...], 1, 1)
        dwe[...] += grad[:d]
        dbe[...] += grad[d : d + 8]
        out = x + dg(wr[...], act_s[...], 0, 0) + cols[:, BIAS_R : BIAS_R + 1]
        dec[0] = out.astype(BF16).T[:L]
        scaled = (x - stats[0:1]) * stats[1:2]
        e = dg(we[...], gl_s[...], 1, 0)
        dvec[:, 0:1] += jnp.sum(e * scaled, 1, keepdims=True)
        dvec[:, 1:2] += jnp.sum(e, 1, keepdims=True)
        back = norm_back(e, scaled, stats[1:2], cols[:, GAIN2 : GAIN2 + 1])
        ga = g_s[...].T.astype(F32) + back
        ga_out[0] = ga
        gm = ga.astype(BF16)
        dvec[:, 2:3] += jnp.sum(gm.astype(F32), 1, keepdims=True)
        ctx = o[0]
        dwm[...] += dg(ctx.astype(BF16), gm, 1, 1)
        do = dg(wm[...], gm, 1, 0)
        for h in range(H):
            hs = slice(h * HEAD, (h + 1) * HEAD)
            part = (do[hs] * inv[0, h]).astype(BF16)
            do_out[0, hs] = part
            dsum_out[0, h] = aug_rows(-jnp.sum(part.astype(F32) * ctx[hs], 0, keepdims=True))

    @pl.when((ff == last) & (copy == 1))
    def _():
        plan = segments(parts, share)
        for z in range(m):
            for name, r, slot, at in plan:
                if name == "wm":
                    piece = dwm[z * (d // m) + r : z * (d // m) + r + SEG]
                elif name == "wr":
                    piece = dwr[z * (f // m) + r : z * (f // m) + r + SEG]
                else:
                    piece = dwe[z * (d // m) + r : z * (d // m) + r + SEG, name * ROWS : (name + 1) * ROWS]
                gpack[slot, z, at : at + SEG] = piece.astype(BF16)
            for at in range(len(plan) * SEG, n * share, SEG):
                gpack[at // share, z, at % share : at % share + SEG] = jnp.zeros((SEG, ROWS), BF16)
        turned = dvec[...].T
        vec_out[...] = jnp.zeros_like(vec_out)
        vec_out[BIAS_M : BIAS_M + 1] = turned[2:3]
        vec_out[GAIN2 : GAIN2 + 1] = turned[0:1]
        vec_out[SHIFT2 : SHIFT2 + 1] = turned[1:2]
        vec_out[BIAS_R : BIAS_R + 1] = drb[0:1]
        for j in range(f // ROWS):
            vec_out[BIAS_E + j : BIAS_E + j + 1] = dbe[0:1, j * ROWS : (j + 1) * ROWS]


def mid(n, m, share, o, inv, stream, up, wpack, be, cols):
    d = cols.shape[0]
    f = be.shape[0]
    once = pl.Buffered(1)
    const = lambda *s: pl.BlockSpec(s, lambda c, k: (0,) * len(s), pipeline_mode=once)
    lead = lambda *s: pl.BlockSpec((1,) + s, lambda c, k: (c,) + (0,) * len(s))
    shape = jax.ShapeDtypeStruct
    vm = pltpu.VMEM
    return pl.pallas_call(
        functools.partial(mid_kernel, n, m, share),
        grid=(2, f // FFC),
        in_specs=[lead(d, LP), lead(H, 1, LP), lead(d, LP), lead(L, d), const(*wpack.shape), const(f, 1), const(d, 16)],
        out_specs=[
            lead(L, d), lead(d, LP), lead(d, LP), lead(H, 16, LP), const(n, m, share, ROWS), const(16, d),
        ],
        out_shape=[
            shape((2, L, d), BF16), shape((2, d, LP), F32), shape((2, d, LP), BF16), shape((2, H, 16, LP), BF16),
            shape((n, m, share, ROWS), BF16), shape((16, d), F32),
        ],
        scratch_shapes=[
            vm((d, d), BF16), vm((d, f), BF16), vm((f, d), BF16),
            vm((d, d), F32), vm((d, f), F32), vm((f, d), F32), vm((d, LANES), F32), vm((8, f), F32), vm((8, d), F32),
            vm((8, LP), F32), vm((d + 16, LP), BF16),
            vm((f, LP), BF16), vm((f, LP), BF16), vm((LP, d), BF16),
        ],
        compiler_params=params(),
        cost_estimate=cost(5e10, 4e7),
    )(o, inv, stream, up, wpack, be, cols)


def post_kernel(n, m, share, held, seen_len, dq, dk, dv, stream, ga, seen, vis, win, cols, vec_in,
                gpack, gp_out, dwin, dbin, dvec, dwp, n1, gp_s):
    copy = pl.program_id(0)
    clip = lax.axis_index("clip")
    d = win.shape[0]
    e_width = dwp.shape[0]
    seen_pad = seen.shape[1]
    cap = gp_out.shape[1]

    @pl.when(copy == 0)
    def _():
        dwin[...] = jnp.zeros_like(dwin)
        dbin[...] = jnp.zeros_like(dbin)
        dvec[...] = jnp.zeros_like(dvec)
        dwp[...] = jnp.zeros_like(dwp)

    x = stream[0]
    scaled, recip = norm_stats(x)
    n1[:d] = (scaled * cols[:, GAIN1 : GAIN1 + 1] + cols[:, SHIFT1 : SHIFT1 + 1]).astype(BF16)
    row = lax.broadcasted_iota(jnp.int32, (16, LP), 0)
    n1[d:] = (row == 0).astype(F32).astype(BF16)
    e = None
    for part, ref in enumerate((dq, dk, dv)):
        sl = slice(part * d, (part + 1) * d)
        grad = dg(n1[...], ref[0], 1, 1)
        dwin[:, sl] += grad[:d]
        dbin[:, sl] += grad[d : d + 8]
        term = dg(win[:, sl], ref[0], 1, 0)
        e = term if e is None else e + term
    dvec[:, 0:1] += jnp.sum(e * scaled, 1, keepdims=True)
    dvec[:, 1:2] += jnp.sum(e, 1, keepdims=True)
    gs = ga[0] + norm_back(e, scaled, recip, cols[:, GAIN1 : GAIN1 + 1])
    hot = one_hot(vis[0], LP)
    token = lax.broadcasted_iota(jnp.int32, (1, LP), 1)
    masked = jnp.where(token < L, 1.0 - jnp.sum(hot, 0, keepdims=True), 0.0)
    dvec[:, 2:3] += jnp.sum(gs * masked, 1, keepdims=True)
    gp = dg(hot.astype(BF16), gs.astype(BF16), 1, 1).astype(BF16)
    gp_s[pl.ds(pl.multiple_of(copy * seen_pad, SEG), seen_pad), :] = gp
    dwp[...] += dg(seen[0], gp, 0, 0)

    @pl.when(copy == 1)
    def _():
        for source in range(n):
            pick = interleave(cap, 2 * seen_pad, clip, source, held, seen_len, seen_pad, n, False)
            gp_out[source] = dg(pick, gp_s[...], 1, 0).astype(BF16)
        turned = dvec[...].T
        row = lax.broadcasted_iota(jnp.int32, (16, d), 0)
        vec = vec_in[...]
        vec = jnp.where(row == TOKEN, turned[2:3], vec)
        vec = jnp.where(row == GAIN1, turned[0:1], vec)
        vec = jnp.where(row == SHIFT1, turned[1:2], vec)
        vec = jnp.where(row == BIAS_Q, dbin[0:1, :d], vec)
        vec = jnp.where(row == BIAS_V, dbin[0:1, 2 * d :], vec).astype(BF16)
        wp_rows = e_width // m
        win_rows = d // m
        plan = segments([("wp", wp_rows)] + [(j, win_rows) for j in range(3)] + [("vec", SEG)], share)
        for z in range(m):
            for name, r, slot, at in plan:
                if name == "wp":
                    piece = dwp[z * wp_rows + r : z * wp_rows + r + SEG].astype(BF16)
                elif name == "vec":
                    piece = vec
                else:
                    piece = dwin[
                        z * win_rows + r : z * win_rows + r + SEG, name * ROWS : (name + 1) * ROWS
                    ].astype(BF16)
                gpack[slot, z, at : at + SEG] = piece
            for at in range(len(plan) * SEG, n * share, SEG):
                gpack[at // share, z, at % share : at % share + SEG] = jnp.zeros((SEG, ROWS), BF16)


def post(n, m, share, held, seen_len, dq, dk, dv, stream, ga, seen, vis, win, cols, vec_in):
    _, a, e = seen.shape
    d = win.shape[0]
    cap = up16(-(-held // n))
    once = pl.Buffered(1)
    const = lambda *s: pl.BlockSpec(s, lambda c: (0,) * len(s), pipeline_mode=once)
    lead = lambda *s: pl.BlockSpec((1,) + s, lambda c: (c,) + (0,) * len(s))
    shape = jax.ShapeDtypeStruct
    vm = pltpu.VMEM
    return pl.pallas_call(
        functools.partial(post_kernel, n, m, share, held, seen_len),
        grid=(2,),
        in_specs=[
            lead(d, LP), lead(d, LP), lead(d, LP), lead(d, LP), lead(d, LP), lead(a, e), lead(a, 1),
            const(d, 3 * d), const(d, 16), const(16, d),
        ],
        out_specs=[const(n, m, share, ROWS), const(n, cap, d)],
        out_shape=[shape((n, m, share, ROWS), BF16), shape((n, cap, d), BF16)],
        scratch_shapes=[
            vm((d, 3 * d), F32), vm((8, 3 * d), F32), vm((d, LANES), F32), vm((e, d), F32),
            vm((d + 16, LP), BF16), vm((2 * a, d), BF16),
        ],
        compiler_params=params(),
        cost_estimate=cost(2e10, 2e7),
    )(dq, dk, dv, stream, ga, seen, vis, win, cols, vec_in)


def leave_kernel(n, m, gpack, gp, mlp, fin, ret, mlp_out, a1, a2s, a2r, tot, tot_b, brecv, fin_s, ret_s, mlp_s,
                 gs, gr, s1, r1, s2, r2, sb, rb, sc, rc, sm, rm, sf, rf):
    clip = lax.axis_index("clip")
    wt = lax.axis_index("wt")
    half = n // 2
    core = lax.rem(clip, 2)
    chip = clip // 2
    partner = clip + 1 - 2 * core
    mlp_s[clip] = mlp[...]
    greet(n, m, clip, wt)
    sends = []

    def send(*args):
        copy = remote(*args)
        copy.start()
        sends.append(copy)

    order = [*range(1, half), 0]
    turns = [*range(1, m), 0]
    for k in turns:
        zz = lax.rem(wt + k, m)
        for j in order:
            spot = lax.rem(chip + j, half)
            send(gpack.at[2 * spot + 1 - core, zz], a1.at[j, k], s1.at[j, k], r1.at[j, k], partner, wt)
    for k in turns:
        zz = lax.rem(wt + k, m)
        for j in order:
            mine = 2 * lax.rem(chip + j, half) + core
            remote(gpack.at[mine, zz], a1.at[j, k], s1.at[j, k], r1.at[j, k], partner, wt).wait_recv()
            both = gpack[mine, zz].astype(F32) + a1[j, k].astype(F32)
            if j == 0:
                tot[k] = both
            else:
                a2s[j, k] = both.astype(BF16)
                send(a2s.at[j, k], a2r.at[j, k], s2.at[j, k], r2.at[j, k], mine, wt)
    for k in [*range(2, n, 2), *range(1, n, 2)]:
        dest = lax.rem(clip + k, n)
        send(gp.at[dest], ret_s.at[clip], gs.at[k], gr.at[k], dest, wt)
    ret_s[clip] = gp[clip]
    for j in order:
        dest = lax.rem(clip + 2 * j, n) if j else partner
        send(mlp_s.at[clip], mlp_s.at[clip], sm.at[j], rm.at[j], dest, wt)
    for k in turns:
        zz = lax.rem(wt + k, m)
        total = tot[k]
        for j in range(1, half):
            source = lax.rem(clip - 2 * j + n, n)
            remote(a2s.at[j, k], a2r.at[j, k], s2.at[j, k], r2.at[j, k], source, wt).wait_recv()
            total = total + a2r[j, k].astype(F32)
        if k:
            tot_b[k] = total.astype(BF16)
            send(tot_b.at[k], brecv.at[k], sb.at[k], rb.at[k], clip, zz)
    for k in range(1, m):
        source = lax.rem(wt - k + m, m)
        remote(tot_b.at[k], brecv.at[k], sb.at[k], rb.at[k], clip, source).wait_recv()
        total = total + brecv[k].astype(F32)
    fin_s[clip] = total.astype(BF16)
    for k in [*range(2, n, 2), *range(1, n, 2)]:
        send(fin_s.at[clip], fin_s.at[clip], sc.at[k], rc.at[k], lax.rem(clip + k, n), wt)
    for j in range(1, half):
        source = lax.rem(clip - 2 * j + n, n)
        remote(mlp_s.at[source], mlp_s.at[source], sm.at[j], rm.at[j], source, wt).wait_recv()
        send(mlp_s.at[source], mlp_s.at[source], sf.at[j], rf.at[j], partner, wt)
    for k in range(1, n):
        source = lax.rem(clip - k + n, n)
        remote(gp.at[source], ret_s.at[source], gs.at[k], gr.at[k], source, wt).wait_recv()
    ret[...] = ret_s[...]
    for j in range(half):
        source = lax.rem(partner - 2 * j + n, n)
        sems = (sf.at[j], rf.at[j]) if j else (sm.at[0], rm.at[0])
        remote(mlp_s.at[source], mlp_s.at[source], *sems, partner, wt).wait_recv()
    mlp_out[...] = mlp_s[...]
    for k in range(1, n):
        source = lax.rem(clip - k + n, n)
        remote(fin_s.at[source], fin_s.at[source], sc.at[k], rc.at[k], source, wt).wait_recv()
    fin[...] = fin_s[...]
    for copy in sends:
        copy.wait_send()


def leave(n, m, gpack, gp, mlp):
    _, _, share, _ = gpack.shape
    _, cap, d = gp.shape
    whole = pl.BlockSpec(memory_space=pltpu.VMEM)
    shape = jax.ShapeDtypeStruct
    vm = pltpu.VMEM
    dma = pltpu.SemaphoreType.DMA
    half = n // 2
    return pl.pallas_call(
        functools.partial(leave_kernel, n, m),
        in_specs=[whole] * 3,
        out_specs=[whole] * 3,
        out_shape=[shape((n, share, ROWS), BF16), shape((n, cap, d), BF16), shape((n,) + mlp.shape, BF16)],
        scratch_shapes=[
            vm((half, m, share, ROWS), BF16), vm((half, m, share, ROWS), BF16), vm((half, m, share, ROWS), BF16),
            vm((m, share, ROWS), F32), vm((m, share, ROWS), BF16), vm((m, share, ROWS), BF16),
            vm((n, share, ROWS), BF16), vm((n, cap, d), BF16), vm((n,) + mlp.shape, BF16),
            dma((n,)), dma((n,)), dma((half, m)), dma((half, m)), dma((half, m)), dma((half, m)),
            dma((m,)), dma((m,)), dma((n,)), dma((n,)),
            dma((half,)), dma((half,)), dma((half,)), dma((half,)),
        ],
        compiler_params=params(collective_id=1, has_side_effects=True),
        cost_estimate=cost(4e9, 4e6),
    )(gpack, gp, mlp)


def finish_kernel(n, m, plan, mlp_plan, fin, ret, mlp, wp, egrad, dwp, dwin, dwm, dwe, dwr, *vecs):
    clip = lax.axis_index("clip")
    wt = lax.axis_index("wt")
    held = egrad.shape[0]
    cap = ret.shape[1]
    row = lax.broadcasted_iota(jnp.int32, (held, cap), 0)
    col = lax.broadcasted_iota(jnp.int32, (held, cap), 1)
    own = None
    for dest in range(n):
        start = first_slot(dest, held, clip, n)
        stop = first_slot(dest + 1, held, clip, n)
        hot = ((row - start == col) & (row < stop)).astype(F32).astype(BF16)
        part = dg(hot, ret[dest], 1, 0)
        own = part if own is None else own + part
    egrad[...] = dg(own.astype(BF16), wp[...], 1, 1).astype(BF16)
    for name, r, slot, at in plan:
        piece = fin[slot, at : at + SEG].astype(F32)
        if name == "wp":
            dwp[r : r + SEG] = piece
        elif name != "vec":
            dwin[r : r + SEG, name * ROWS : (name + 1) * ROWS] = piece
        else:
            for z in range(m):
                @pl.when(wt == z)
                def _():
                    for i, ref in enumerate(vecs[:BIAS_E]):
                        w = ref.shape[0]
                        ref[...] = piece[i, z * w : (z + 1) * w]
                    w = vecs[BIAS_E].shape[0]
                    line = BIAS_E + z * w // ROWS
                    vecs[BIAS_E][...] = piece[line, z * w % ROWS : z * w % ROWS + w]
    for name, r, slot, at in mlp_plan:
        piece = mlp[slot, at : at + SEG].astype(F32)
        if name == "wm":
            dwm[r : r + SEG] = piece
        elif name == "wr":
            dwr[r : r + SEG] = piece
        else:
            dwe[r : r + SEG, name * ROWS : (name + 1) * ROWS] = piece


def finish(n, m, held, fin, ret, mlp, wp, f):
    e, d = wp.shape
    whole = pl.BlockSpec(memory_space=pltpu.VMEM)
    shape = jax.ShapeDtypeStruct
    plan = segments([("wp", e // m)] + [(j, d // m) for j in range(3)] + [("vec", SEG)], fin.shape[1])
    mlp_plan = segments(mlp_parts(d, f, m), mlp.shape[1])
    outs = [shape((held, e), BF16)] + [
        shape((r // m, c), F32) for r, c in ((e, d), (d, 3 * d), (d, d), (d, f), (f, d))
    ] + [shape((d // m,), F32)] * BIAS_E + [shape((f // m,), F32)]
    return pl.pallas_call(
        functools.partial(finish_kernel, n, m, plan, mlp_plan),
        in_specs=[whole] * 4,
        out_specs=[whole] * len(outs),
        out_shape=outs,
        compiler_params=params(),
        cost_estimate=cost(1e9, 4e6),
    )(fin, ret, mlp, wp)


def core(n, m, held, seen_len, seen, vis, wp, win, cols, be, wpack, upstream, reduce_mlp=None):
    d = cols.shape[0]
    pos = jnp.asarray(position_table(d))
    stream, q, kv, k_rows, v_rows = pre(seen, vis, wp, cols, pos, win)
    o, inv, e = attend(k_rows, q, kv)
    share = up16(-(-wpack.shape[1] // n))
    dec, ga, do, dsum, mlp, vec = mid(n, m, share, o, inv, stream, upstream.reshape(2, L, d), wpack, be, cols)
    if reduce_mlp is not None:
        mlp = reduce_mlp(mlp)
    dq, dk, dv = attend_back(e, v_rows, q, do, dsum, kv)
    share = up16(-(-(wp.shape[0] // m + 3 * (d // m) + SEG) // n))
    gpack, gp = post(n, m, share, held, seen_len, dq, dk, dv, stream, ga, seen, vis, win, cols, vec)
    return dec, mlp, gpack, gp


def per_device(encoded, visible_at, wp, token, gain1, shift1, win, bq, bv, wm, bm, gain2, shift2, we, be, wr, br, upstream):
    n = lax.axis_size("clip")
    m = lax.axis_size("wt")
    held = encoded.shape[0]
    seen_len = visible_at.shape[1]
    d = wp.shape[1]
    f = be.shape[0] * m
    local = pack_mlp(wm, we, wr)
    wpack = lax.all_gather(local, "wt", axis=0, tiled=True).reshape(m, local.shape[0], ROWS)
    vecs = (token, gain1, shift1, bq, bv, bm, gain2, shift2, br, be)
    seen, vis, wp_full, win_full, cols, be_col = enter(n, m, encoded, visible_at, wp, win, vecs)

    def reduce_mlp(mlp):
        mlp = lax.psum_scatter(mlp.reshape(-1, ROWS), "clip", scatter_dimension=0, tiled=True)
        return lax.psum_scatter(mlp, "wt", scatter_dimension=0, tiled=True)

    dec, mlp, gpack, gp = core(
        n, m, held, seen_len, seen, vis, wp_full, win_full, cols, be_col, wpack, upstream, reduce_mlp
    )
    fin, ret, mlp = leave(n, m, gpack, gp, mlp)
    egrad, dwp, dwin, dwm, dwe, dwr, *small = finish(n, m, held, fin, ret, mlp, wp_full, f)
    t, g1, s1, vq, vv, vm, g2, s2, vr, ve = small
    return (
        dec.reshape(2 * L, d), egrad, dwp, t, g1, s1, dwin, vq, vv, dwm, vm, g2, s2, dwe, ve, dwr, vr,
    )


def solution(mesh):
    both, wt = P(("clip", "wt"), None), P("wt")
    mat = P("wt", None)
    params_in = (mat, wt, wt, wt, mat, wt, wt, mat, wt, wt, wt, mat, wt, mat, wt)
    return jax.shard_map(
        per_device,
        mesh=mesh,
        in_specs=(both, both) + params_in + (both,),
        out_specs=(both, both) + params_in,
        check_vma=False,
    )
```

```python
import functools
import math

import jax
import jax.numpy as jnp
import numpy as np
from jax import lax
from jax.experimental import pallas as pl
from jax.experimental.pallas import tpu as pltpu
from jax.sharding import PartitionSpec as P

H = 6
HEAD = 64
L = 1568
LANES = 128
LP = -(-L // LANES) * LANES
KP = L
EPSILON = 1e-06
LOG2E = math.log2(math.e)
Q_SCALE = LOG2E / math.sqrt(HEAD)
ROOT_HALF = math.sqrt(0.5)
INV_ROOT_TWO_PI = 1.0 / math.sqrt(2.0 * math.pi)
SAFE_EXPONENT = 60.0
VMEM_LIMIT = 60 * 2**20
FFC = 512
Q_BLOCKS = ((0, 896), (896, LP - 896))
F32 = jnp.float32
BF16 = jnp.bfloat16


SEG = 16
ROWS = 384
MESH = pl.DeviceIdType.MESH
TOKEN, GAIN1, SHIFT1, BIAS_Q, BIAS_V, BIAS_M, GAIN2, SHIFT2, BIAS_R, BIAS_E = range(10)


def params(**kw):
    return pltpu.CompilerParams(vmem_limit_bytes=VMEM_LIMIT, **kw)


def cost(flops, moved=0):
    return pl.CostEstimate(flops=int(flops), bytes_accessed=int(moved), transcendentals=0)


def up16(x):
    return -(-x // SEG) * SEG


def segments(parts, share):
    out = []
    at = 0
    for name, rows in parts:
        for r in range(0, rows, SEG):
            out.append((name, r, at // share, at % share))
            at += SEG
    return out


def dg(a, b, ca, cb):
    return lax.dot_general(a, b, (((ca,), (cb,)), ((), ())), preferred_element_type=F32)


def position_table(width):
    places = np.arange(LP, dtype=np.float64)[None, :]
    columns = np.arange(width)
    exponent = (2 * (columns // 2)).astype(np.float64) / width
    angles = places / np.power(10000.0, exponent)[:, None]
    return np.where(columns[:, None] % 2 == 0, np.sin(angles), np.cos(angles)).astype(np.float32)


def norm_stats(x):
    center = x - jnp.mean(x, 0, keepdims=True)
    recip = lax.rsqrt(jnp.mean(center * center, 0, keepdims=True) + EPSILON)
    return center * recip, recip


def norm_back(e, scaled, recip, gain):
    lifted = e * gain
    return recip * (
        lifted
        - jnp.mean(lifted, 0, keepdims=True)
        - scaled * jnp.mean(lifted * scaled, 0, keepdims=True)
    )


def split3(x):
    hi = x.astype(BF16)
    rest = x - hi.astype(F32)
    mid = rest.astype(BF16)
    low = (rest - mid.astype(F32)).astype(BF16)
    return hi, mid, low


def aug_rows(x):
    hi, mid, low = split3(x)
    row = lax.broadcasted_iota(jnp.int32, (16, x.shape[1]), 0)
    zero = jnp.zeros((16, x.shape[1]), F32)
    out = jnp.where(row == 0, hi.astype(F32), zero)
    out = jnp.where(row == 1, mid.astype(F32), out)
    out = jnp.where(row == 2, low.astype(F32), out)
    return out.astype(BF16)


def one_hot(vis, width):
    place = lax.broadcasted_iota(jnp.int32, (vis.shape[0], width), 1).astype(F32)
    return (vis == place).astype(F32)


def first_slot(dest, held, clip, n):
    return (dest * held - clip + n - 1) // n


def interleave(rows, cols, clip, source, held, seen, seen_pad, n, by_row):
    first = (clip * held - source + n - 1) // n
    base = source + n * first - clip * held
    place = lax.broadcasted_iota(jnp.int32, (rows, cols), 0 if by_row else 1)
    slot = lax.broadcasted_iota(jnp.int32, (rows, cols), 1 if by_row else 0)
    second = place >= seen_pad
    local = jnp.where(second, place - (seen_pad - seen), place)
    good = (place < seen) | (second & (place < seen_pad + seen))
    return (good & (local == base + n * slot)).astype(F32).astype(BF16)


def greet(n, m, clip, wt):
    barrier = pltpu.get_barrier_semaphore()
    for k in range(1, n):
        pl.semaphore_signal(barrier, inc=1, device_id=(lax.rem(clip + k, n), wt), device_id_type=MESH)
    for k in range(1, m):
        pl.semaphore_signal(barrier, inc=1, device_id=(clip, lax.rem(wt + k, m)), device_id_type=MESH)
    pl.semaphore_wait(barrier, n + m - 2)


def remote(src, dst, send, recv, clip, wt):
    return pltpu.make_async_remote_copy(
        src_ref=src, dst_ref=dst, send_sem=send, recv_sem=recv, device_id=(clip, wt), device_id_type=MESH
    )


def enter_kernel(n, m, share, cap, seen_pad, *refs):
    (enc, vis_in, wp_in, win_in, *vecs) = refs[:14]
    (seen_out, vis_out, wp, win, cols, be) = refs[14:20]
    (pack, gath, out_rows, in_rows, vec_s, vis_s, zs, zr, bs, br, fs, fr, rs, rr) = refs[20:]
    clip = lax.axis_index("clip")
    wt = lax.axis_index("wt")
    held = enc.shape[0]
    seen = vis_in.shape[1]
    wp_rows = wp_in.shape[0]
    win_rows = win_in.shape[0]
    half = n // 2
    plan = segments(
        [("wp", wp_rows)] + [(j, win_rows) for j in range(3)] + [("vec", SEG)], share
    )
    vec_s[...] = jnp.zeros_like(vec_s)
    for i, ref in enumerate(vecs):
        vec_s[i, : ref.shape[0]] = ref[...].astype(F32)
    for name, r, slot, at in plan:
        if name == "wp":
            piece = wp_in[r : r + SEG]
        elif name == "vec":
            piece = vec_s[...].astype(BF16)
        else:
            piece = win_in[r : r + SEG, name * ROWS : (name + 1) * ROWS]
        pack[slot, at : at + SEG] = piece
    for at in range(len(plan) * SEG, n * share, SEG):
        pack[at // share, at % share : at % share + SEG] = jnp.zeros((SEG, ROWS), BF16)
    greet(n, m, clip, wt)

    sends = []
    partner = clip + 1 - 2 * lax.rem(clip, 2)
    for k in range(1, m):
        copy = remote(pack.at[clip], gath.at[clip, wt], zs.at[k], zr.at[k], clip, lax.rem(wt + k, m))
        copy.start()
        sends.append(copy)
    gath[clip, wt] = pack[clip]

    def spread(k):
        z = lax.rem(wt - k + m, m)
        for j in [*range(1, half), 0]:
            piece = gath.at[clip, z]
            dest = lax.rem(clip + 2 * j, n) if j else partner
            copy = remote(piece, piece, bs.at[j, k], br.at[j, k], dest, wt)
            copy.start()
            sends.append(copy)

    spread(0)

    rows_at = lax.broadcasted_iota(jnp.int32, (cap, held), 0)
    cols_at = lax.broadcasted_iota(jnp.int32, (cap, held), 1)
    row_sends = []
    for k in [*range(2, n, 2), *range(3, n, 2), 1, 0] if n > 2 else range(n - 1, -1, -1):
        dest = lax.rem(clip + k, n)
        hot = (rows_at + first_slot(dest, held, clip, n) == cols_at).astype(F32).astype(BF16)
        rows = dg(hot, enc[...], 1, 0).astype(BF16)
        if k == 0:
            in_rows[clip] = rows
        else:
            out_rows[k] = rows
            copy = remote(out_rows.at[k], in_rows.at[clip], rs.at[k], rr.at[k], dest, wt)
            copy.start()
            row_sends.append(copy)

    for k in range(1, m):
        source = lax.rem(wt - k + m, m)
        remote(pack.at[clip], gath.at[clip, source], zs.at[k], zr.at[k], clip, source).wait_recv()
        spread(k)

    vis_s[...] = jnp.full(vis_s.shape, -1.0, F32)
    vis_s[0:2, :seen] = vis_in[...].astype(F32)
    turned = vis_s[...].T
    for copy_at in range(2):
        vis_out[copy_at] = turned[:seen_pad, copy_at : copy_at + 1]

    for k in range(m):
        z = lax.rem(wt - k + m, m)
        for j in range(1, half):
            source = lax.rem(clip - 2 * j + n, n)
            piece = gath.at[source, z]
            remote(piece, piece, bs.at[j, k], br.at[j, k], source, wt).wait_recv()
            copy = remote(piece, piece, fs.at[j, k], fr.at[j, k], partner, wt)
            copy.start()
            sends.append(copy)

    for k in range(1, n):
        source = lax.rem(clip - k + n, n)
        remote(out_rows.at[k], in_rows.at[source], rs.at[k], rr.at[k], source, wt).wait_recv()
    total = None
    for source in range(n):
        hot = interleave(2 * seen_pad, cap, clip, source, held, seen, seen_pad, n, True)
        part = dg(hot, in_rows[source], 1, 0)
        total = part if total is None else total + part
    total = total.astype(BF16)
    seen_out[0] = total[:seen_pad]
    seen_out[1] = total[seen_pad:]

    for k in range(m):
        z = lax.rem(wt - k + m, m)
        for j in range(half):
            source = lax.rem(partner - 2 * j + n, n)
            piece = gath.at[source, z]
            sems = (fs.at[j, k], fr.at[j, k]) if j else (bs.at[0, k], br.at[0, k])
            remote(piece, piece, *sems, partner, wt).wait_recv()
    for z in range(m):
        for name, r, slot, at in plan:
            piece = gath[slot, z, at : at + SEG]
            if name == "wp":
                wp[z * wp_rows + r : z * wp_rows + r + SEG] = piece
            elif name == "vec":
                turned = piece.astype(F32).T
                small = vecs[0].shape[0]
                cols[z * small : (z + 1) * small] = turned[:small]
                large = vecs[BIAS_E].shape[0]
                be[z * large : (z + 1) * large] = turned[:large, BIAS_E : BIAS_E + 1]
            else:
                win[z * win_rows + r : z * win_rows + r + SEG, name * ROWS : (name + 1) * ROWS] = piece
    for copy in sends + row_sends:
        copy.wait_send()


def pack_kernel(wm, we, wr, out):
    rows = wm.shape[0]
    out[:rows] = wm[...]
    at = rows
    for j in range(we.shape[1] // ROWS):
        out[at : at + rows] = we[:, j * ROWS : (j + 1) * ROWS]
        at += rows
    out[at:] = wr[...]


def pack_mlp(wm, we, wr):
    rows = wm.shape[0] + wm.shape[0] * (we.shape[1] // ROWS) + wr.shape[0]
    whole = pl.BlockSpec(memory_space=pltpu.VMEM)
    return pl.pallas_call(
        pack_kernel,
        in_specs=[whole] * 3,
        out_specs=whole,
        out_shape=jax.ShapeDtypeStruct((rows, ROWS), BF16),
        compiler_params=params(),
        cost_estimate=cost(0, 1.3e6),
    )(wm, we, wr)


def enter(n, m, enc, vis, wp, win, vecs):
    held, e = enc.shape
    seen = vis.shape[1]
    seen_pad = up16(seen)
    d = wp.shape[1]
    cap = up16(-(-held // n))
    share = up16(-(-(wp.shape[0] + 3 * win.shape[0] + SEG) // n))
    whole = pl.BlockSpec(memory_space=pltpu.VMEM)
    shape = jax.ShapeDtypeStruct
    dma = pltpu.SemaphoreType.DMA
    ins = (enc, vis, wp, win, *vecs)
    return pl.pallas_call(
        functools.partial(enter_kernel, n, m, share, cap, seen_pad),
        in_specs=[whole] * len(ins),
        out_specs=[whole] * 6,
        out_shape=[
            shape((2, seen_pad, e), BF16), shape((2, seen_pad, 1), F32), shape((e, d), BF16),
            shape((d, 3 * d), BF16), shape((d, 16), F32), shape((vecs[BIAS_E].shape[0] * m, 1), F32),
        ],
        scratch_shapes=[
            pltpu.VMEM((n, share, ROWS), BF16), pltpu.VMEM((n, m, share, ROWS), BF16),
            pltpu.VMEM((n, cap, e), BF16), pltpu.VMEM((n, cap, e), BF16),
            pltpu.VMEM((SEG, ROWS), F32), pltpu.VMEM((8, 2 * LANES), F32),
            dma((m,)), dma((m,)), dma((n // 2, m)), dma((n // 2, m)), dma((n // 2, m)), dma((n // 2, m)),
            dma((n,)), dma((n,)),
        ],
        compiler_params=params(collective_id=0, has_side_effects=True),
        cost_estimate=cost(6e9, 4e6),
    )(*ins)


def pre_kernel(seen, vis, wp, cols, pos, win, stream_out, q_out, kv_out, k_rows, v_rows):
    width = wp.shape[1]
    proj = dg(seen[0], wp[...], 1, 0).astype(BF16)
    hot = one_hot(vis[0], LP)
    covered = jnp.sum(hot, 0, keepdims=True)
    stream = dg(proj, hot.astype(BF16), 0, 0) + (1.0 - covered) * cols[:, TOKEN : TOKEN + 1] + pos[...]
    stream_out[0] = stream
    scaled, _ = norm_stats(stream)
    normed = (scaled * cols[:, GAIN1 : GAIN1 + 1] + cols[:, SHIFT1 : SHIFT1 + 1]).astype(BF16)
    lane = lax.broadcasted_iota(jnp.int32, (KP, LANES), 1)
    token = lax.broadcasted_iota(jnp.int32, (KP, LANES), 0)
    ones = ((lane < HEAD + 3) & (token < L)).astype(F32).astype(BF16)
    for part in range(3):
        sl = slice(part * width, (part + 1) * width)
        mixed = dg(win[:, sl], normed, 0, 0)
        if part == 0:
            q_out[0] = ((mixed + cols[:, BIAS_Q : BIAS_Q + 1]) * Q_SCALE).astype(BF16)
        else:
            if part == 2:
                mixed = mixed + cols[:, BIAS_V : BIAS_V + 1]
            mixed = mixed.astype(BF16)
            kv_out[0, (part - 1) * width : part * width, :L] = mixed[:, :L]
            kv_out[0, (part - 1) * width : part * width, L:] = jnp.zeros((width, LP - L), BF16)
            dst = k_rows if part == 1 else v_rows
            for h in range(H):
                dst[0, h] = ones
                dst[0, h, :L, :HEAD] = mixed[h * HEAD : (h + 1) * HEAD].T[:L]


def pre(seen, vis, wp, cols, pos, win):
    _, a, e = seen.shape
    d = wp.shape[1]
    const = lambda *s: pl.BlockSpec(s, lambda c: (0,) * len(s))
    lead = lambda *s: pl.BlockSpec((1,) + s, lambda c: (c,) + (0,) * len(s))
    return pl.pallas_call(
        pre_kernel,
        grid=(2,),
        in_specs=[lead(a, e), lead(a, 1), const(e, d), const(d, 16), const(d, LP), const(d, 3 * d)],
        out_specs=[lead(d, LP), lead(d, LP), lead(2 * d, LP), lead(H, KP, LANES), lead(H, KP, LANES)],
        out_shape=[
            jax.ShapeDtypeStruct((2, d, LP), F32),
            jax.ShapeDtypeStruct((2, d, LP), BF16),
            jax.ShapeDtypeStruct((2, 2 * d, LP), BF16),
            jax.ShapeDtypeStruct((2, H, KP, LANES), BF16),
            jax.ShapeDtypeStruct((2, H, KP, LANES), BF16),
        ],
        compiler_params=params(),
        cost_estimate=cost(12e9, 2e7),
    )(seen, vis, wp, cols, pos, win)


def attend_kernel(k_rows, q, kt, vt, o_out, inv_out, e_out, v_aug):
    row = lax.broadcasted_iota(jnp.int32, (16, KP), 0)
    token = lax.broadcasted_iota(jnp.int32, (16, KP), 1)
    v_aug[:HEAD] = vt[0, :, :KP]
    v_aug[HEAD:] = ((row == 0) & (token < L)).astype(F32).astype(BF16)
    qf = q[0].astype(F32)
    kf = kt[0].astype(F32)
    bound = jnp.max(jnp.sum(qf * qf, 0, keepdims=True)) * jnp.max(jnp.sum(kf * kf, 0, keepdims=True))
    safe = bound <= SAFE_EXPONENT * SAFE_EXPONENT

    def run(shift):
        for start, size in Q_BLOCKS:
            sl = slice(start, start + size)
            s = dg(k_rows[0, 0, :, :HEAD], q[0, :, sl], 1, 0)
            if shift:
                key = lax.broadcasted_iota(jnp.int32, (KP, size), 0)
                s = jnp.where(key < L, s, -jnp.inf)
                s = s - jnp.max(s, 0, keepdims=True)
            e = jnp.exp2(s).astype(BF16)
            e_out[0, 0, :, sl] = e
            o = dg(v_aug[...], e, 1, 0)
            inv = 1.0 / o[HEAD : HEAD + 1]
            o_out[0, :, sl] = o[:HEAD] * inv
            inv_out[0, 0, :, sl] = inv

    pl.when(safe)(lambda: run(False))
    pl.when(jnp.logical_not(safe))(lambda: run(True))


def attend(k_rows, q, kv):
    d = q.shape[1]
    head = lambda off: (lambda i: (i // H, i % H + off, 0))
    wide = lambda i: (i // H, i % H, 0, 0)
    return pl.pallas_call(
        attend_kernel,
        grid=(2 * H,),
        in_specs=[
            pl.BlockSpec((1, 1, KP, LANES), wide),
            pl.BlockSpec((1, HEAD, LP), head(0)),
            pl.BlockSpec((1, HEAD, LP), head(0)),
            pl.BlockSpec((1, HEAD, LP), head(H)),
        ],
        out_specs=[
            pl.BlockSpec((1, HEAD, LP), head(0)),
            pl.BlockSpec((1, 1, 1, LP), wide),
            pl.BlockSpec((1, 1, KP, LP), wide),
        ],
        out_shape=[
            jax.ShapeDtypeStruct((2, d, LP), F32),
            jax.ShapeDtypeStruct((2, H, 1, LP), F32),
            jax.ShapeDtypeStruct((2, H, KP, LP), BF16),
        ],
        scratch_shapes=[pltpu.VMEM((HEAD + 16, KP), BF16)],
        compiler_params=params(),
        cost_estimate=cost(3e10, 2e7),
    )(k_rows, q, kv, kv)


def attend_back_kernel(e, v_rows, q, do, dsum, kt, dq, dk, dv, do_aug):
    do_aug[:HEAD] = do[0]
    do_aug[HEAD : HEAD + 16] = dsum[0, 0]
    do_aug[HEAD + 16 :] = jnp.zeros((LANES - HEAD - 16, LP), BF16)
    k_sum = None
    v_sum = None
    for start, size in Q_BLOCKS:
        sl = slice(start, start + size)
        p = e[0, 0, :, sl]
        dp = dg(v_rows[0, 0], do_aug[:, sl], 1, 0)
        ds = (p.astype(F32) * dp).astype(BF16)
        v_part = dg(do_aug[:HEAD, sl], p, 1, 1)
        k_part = dg(q[0, :, sl], ds, 1, 1)
        v_sum = v_part if v_sum is None else v_sum + v_part
        k_sum = k_part if k_sum is None else k_sum + k_part
        dq[0, :, sl] = (dg(kt[0, :, :KP], ds, 1, 0) * (1.0 / math.sqrt(HEAD))).astype(BF16)
    for dst, total in ((dk, k_sum * (1.0 / LOG2E)), (dv, v_sum)):
        dst[0, :, :L] = total[:, :L].astype(BF16)
        dst[0, :, L:] = jnp.zeros((HEAD, LP - L), BF16)


def attend_back(e, v_rows, q, do, dsum, kv):
    d = q.shape[1]
    head = lambda i: (i // H, i % H, 0)
    wide = lambda i: (i // H, i % H, 0, 0)
    return pl.pallas_call(
        attend_back_kernel,
        grid=(2 * H,),
        in_specs=[
            pl.BlockSpec((1, 1, KP, LP), wide),
            pl.BlockSpec((1, 1, KP, LANES), wide),
            pl.BlockSpec((1, HEAD, LP), head),
            pl.BlockSpec((1, HEAD, LP), head),
            pl.BlockSpec((1, 1, 16, LP), wide),
            pl.BlockSpec((1, HEAD, LP), head),
        ],
        out_specs=[pl.BlockSpec((1, HEAD, LP), head)] * 3,
        out_shape=[jax.ShapeDtypeStruct((2, d, LP), BF16)] * 3,
        scratch_shapes=[pltpu.VMEM((LANES, LP), BF16)],
        compiler_params=params(),
        cost_estimate=cost(8e10, 4e7),
    )(e, v_rows, q, do, dsum, kv)


def mlp_parts(d, f, m):
    return [("wm", d // m)] + [(j, d // m) for j in range(f // ROWS)] + [("wr", f // m)]


def mid_kernel(n, m, share, o, inv, stream, up, wpack, be, cols,
               dec, ga_out, do_out, dsum_out, gpack, vec_out,
               wm, we, wr, dwm, dwe, dwr, dvec, dbe, drb, stats, n2, act_s, gl_s, g_s):
    copy = pl.program_id(0)
    ff = pl.program_id(1)
    last = pl.num_programs(1) - 1
    d = wm.shape[0]
    f = wr.shape[0]
    parts = mlp_parts(d, f, m)

    @pl.when((copy == 0) & (ff == 0))
    def _():
        for z in range(m):
            at = 0
            for name, rows in parts:
                piece = wpack[z, at : at + rows]
                dst = slice(z * rows, (z + 1) * rows)
                if name == "wm":
                    wm[dst] = piece
                elif name == "wr":
                    wr[dst] = piece
                else:
                    we[dst, name * ROWS : (name + 1) * ROWS] = piece
                at += rows
        dwm[...] = jnp.zeros_like(dwm)
        dwe[...] = jnp.zeros_like(dwe)
        dwr[...] = jnp.zeros_like(dwr)
        dvec[...] = jnp.zeros_like(dvec)
        dbe[...] = jnp.zeros_like(dbe)
        drb[...] = jnp.zeros_like(drb)

    @pl.when(ff == 0)
    def _():
        ctx = o[0].astype(BF16)
        x = stream[0] + dg(wm[...], ctx, 0, 0) + cols[:, BIAS_M : BIAS_M + 1]
        ga_out[0] = x
        mean = jnp.mean(x, 0, keepdims=True)
        center = x - mean
        recip = lax.rsqrt(jnp.mean(center * center, 0, keepdims=True) + EPSILON)
        stats[0:1] = mean
        stats[1:2] = recip
        n2[:d] = (center * recip * cols[:, GAIN2 : GAIN2 + 1] + cols[:, SHIFT2 : SHIFT2 + 1]).astype(BF16)
        row = lax.broadcasted_iota(jnp.int32, (16, LP), 0)
        n2[d:] = (row == 0).astype(F32).astype(BF16)
        g = (up[0].astype(F32) * 0.5).astype(BF16)
        g_s[:L] = g
        g_s[L:] = jnp.zeros((LP - L, d), BF16)
        drb[...] += dg(jnp.ones((8, L), BF16), g, 1, 0)

    rows = pl.ds(pl.multiple_of(ff * FFC, FFC), FFC)
    g = g_s[...]
    lifted = dg(we[:, rows], n2[:d], 0, 0) + be[rows, :]
    bell = jnp.exp(-0.5 * lifted * lifted)
    cdf = 0.5 * (1.0 + lax.erf(lifted * ROOT_HALF))
    act = (lifted * cdf).astype(BF16)
    slope = cdf + lifted * bell * INV_ROOT_TWO_PI
    gl = (dg(wr[rows, :], g, 1, 1) * slope).astype(BF16)
    act_s[rows, :] = act
    gl_s[rows, :] = gl

    @pl.when(ff == last)
    def _():
        x = ga_out[0]
        dwr[...] += dg(act_s[...], g_s[...], 1, 0)
        grad = dg(n2[...], gl_s[...], 1, 1)
        dwe[...] += grad[:d]
        dbe[...] += grad[d : d + 8]
        out = x + dg(wr[...], act_s[...], 0, 0) + cols[:, BIAS_R : BIAS_R + 1]
        dec[0] = out.astype(BF16).T[:L]
        scaled = (x - stats[0:1]) * stats[1:2]
        e = dg(we[...], gl_s[...], 1, 0)
        dvec[:, 0:1] += jnp.sum(e * scaled, 1, keepdims=True)
        dvec[:, 1:2] += jnp.sum(e, 1, keepdims=True)
        back = norm_back(e, scaled, stats[1:2], cols[:, GAIN2 : GAIN2 + 1])
        ga = g_s[...].T.astype(F32) + back
        ga_out[0] = ga
        gm = ga.astype(BF16)
        dvec[:, 2:3] += jnp.sum(gm.astype(F32), 1, keepdims=True)
        ctx = o[0]
        dwm[...] += dg(ctx.astype(BF16), gm, 1, 1)
        do = dg(wm[...], gm, 1, 0)
        for h in range(H):
            hs = slice(h * HEAD, (h + 1) * HEAD)
            part = (do[hs] * inv[0, h]).astype(BF16)
            do_out[0, hs] = part
            dsum_out[0, h] = aug_rows(-jnp.sum(part.astype(F32) * ctx[hs], 0, keepdims=True))

    @pl.when((ff == last) & (copy == 1))
    def _():
        plan = segments(parts, share)
        for z in range(m):
            for name, r, slot, at in plan:
                if name == "wm":
                    piece = dwm[z * (d // m) + r : z * (d // m) + r + SEG]
                elif name == "wr":
                    piece = dwr[z * (f // m) + r : z * (f // m) + r + SEG]
                else:
                    piece = dwe[z * (d // m) + r : z * (d // m) + r + SEG, name * ROWS : (name + 1) * ROWS]
                gpack[slot, z, at : at + SEG] = piece.astype(BF16)
            for at in range(len(plan) * SEG, n * share, SEG):
                gpack[at // share, z, at % share : at % share + SEG] = jnp.zeros((SEG, ROWS), BF16)
        turned = dvec[...].T
        vec_out[...] = jnp.zeros_like(vec_out)
        vec_out[BIAS_M : BIAS_M + 1] = turned[2:3]
        vec_out[GAIN2 : GAIN2 + 1] = turned[0:1]
        vec_out[SHIFT2 : SHIFT2 + 1] = turned[1:2]
        vec_out[BIAS_R : BIAS_R + 1] = drb[0:1]
        for j in range(f // ROWS):
            vec_out[BIAS_E + j : BIAS_E + j + 1] = dbe[0:1, j * ROWS : (j + 1) * ROWS]


def mid(n, m, share, o, inv, stream, up, wpack, be, cols):
    d = cols.shape[0]
    f = be.shape[0]
    once = pl.Buffered(1)
    const = lambda *s: pl.BlockSpec(s, lambda c, k: (0,) * len(s), pipeline_mode=once)
    lead = lambda *s: pl.BlockSpec((1,) + s, lambda c, k: (c,) + (0,) * len(s))
    shape = jax.ShapeDtypeStruct
    vm = pltpu.VMEM
    return pl.pallas_call(
        functools.partial(mid_kernel, n, m, share),
        grid=(2, f // FFC),
        in_specs=[lead(d, LP), lead(H, 1, LP), lead(d, LP), lead(L, d), const(*wpack.shape), const(f, 1), const(d, 16)],
        out_specs=[
            lead(L, d), lead(d, LP), lead(d, LP), lead(H, 16, LP), const(n, m, share, ROWS), const(16, d),
        ],
        out_shape=[
            shape((2, L, d), BF16), shape((2, d, LP), F32), shape((2, d, LP), BF16), shape((2, H, 16, LP), BF16),
            shape((n, m, share, ROWS), BF16), shape((16, d), F32),
        ],
        scratch_shapes=[
            vm((d, d), BF16), vm((d, f), BF16), vm((f, d), BF16),
            vm((d, d), F32), vm((d, f), F32), vm((f, d), F32), vm((d, LANES), F32), vm((8, f), F32), vm((8, d), F32),
            vm((8, LP), F32), vm((d + 16, LP), BF16),
            vm((f, LP), BF16), vm((f, LP), BF16), vm((LP, d), BF16),
        ],
        compiler_params=params(),
        cost_estimate=cost(5e10, 4e7),
    )(o, inv, stream, up, wpack, be, cols)


def post_kernel(n, m, share, held, seen_len, dq, dk, dv, stream, ga, seen, vis, win, cols, vec_in,
                gpack, gp_out, dwin, dbin, dvec, dwp, n1, gp_s):
    copy = pl.program_id(0)
    clip = lax.axis_index("clip")
    d = win.shape[0]
    e_width = dwp.shape[0]
    seen_pad = seen.shape[1]
    cap = gp_out.shape[1]

    @pl.when(copy == 0)
    def _():
        dwin[...] = jnp.zeros_like(dwin)
        dbin[...] = jnp.zeros_like(dbin)
        dvec[...] = jnp.zeros_like(dvec)
        dwp[...] = jnp.zeros_like(dwp)

    x = stream[0]
    scaled, recip = norm_stats(x)
    n1[:d] = (scaled * cols[:, GAIN1 : GAIN1 + 1] + cols[:, SHIFT1 : SHIFT1 + 1]).astype(BF16)
    row = lax.broadcasted_iota(jnp.int32, (16, LP), 0)
    n1[d:] = (row == 0).astype(F32).astype(BF16)
    e = None
    for part, ref in enumerate((dq, dk, dv)):
        sl = slice(part * d, (part + 1) * d)
        grad = dg(n1[...], ref[0], 1, 1)
        dwin[:, sl] += grad[:d]
        dbin[:, sl] += grad[d : d + 8]
        term = dg(win[:, sl], ref[0], 1, 0)
        e = term if e is None else e + term
    dvec[:, 0:1] += jnp.sum(e * scaled, 1, keepdims=True)
    dvec[:, 1:2] += jnp.sum(e, 1, keepdims=True)
    gs = ga[0] + norm_back(e, scaled, recip, cols[:, GAIN1 : GAIN1 + 1])
    hot = one_hot(vis[0], LP)
    token = lax.broadcasted_iota(jnp.int32, (1, LP), 1)
    masked = jnp.where(token < L, 1.0 - jnp.sum(hot, 0, keepdims=True), 0.0)
    dvec[:, 2:3] += jnp.sum(gs * masked, 1, keepdims=True)
    gp = dg(hot.astype(BF16), gs.astype(BF16), 1, 1).astype(BF16)
    gp_s[pl.ds(pl.multiple_of(copy * seen_pad, SEG), seen_pad), :] = gp
    dwp[...] += dg(seen[0], gp, 0, 0)

    @pl.when(copy == 1)
    def _():
        for source in range(n):
            pick = interleave(cap, 2 * seen_pad, clip, source, held, seen_len, seen_pad, n, False)
            gp_out[source] = dg(pick, gp_s[...], 1, 0).astype(BF16)
        turned = dvec[...].T
        row = lax.broadcasted_iota(jnp.int32, (16, d), 0)
        vec = vec_in[...]
        vec = jnp.where(row == TOKEN, turned[2:3], vec)
        vec = jnp.where(row == GAIN1, turned[0:1], vec)
        vec = jnp.where(row == SHIFT1, turned[1:2], vec)
        vec = jnp.where(row == BIAS_Q, dbin[0:1, :d], vec)
        vec = jnp.where(row == BIAS_V, dbin[0:1, 2 * d :], vec).astype(BF16)
        wp_rows = e_width // m
        win_rows = d // m
        plan = segments([("wp", wp_rows)] + [(j, win_rows) for j in range(3)] + [("vec", SEG)], share)
        for z in range(m):
            for name, r, slot, at in plan:
                if name == "wp":
                    piece = dwp[z * wp_rows + r : z * wp_rows + r + SEG].astype(BF16)
                elif name == "vec":
                    piece = vec
                else:
                    piece = dwin[
                        z * win_rows + r : z * win_rows + r + SEG, name * ROWS : (name + 1) * ROWS
                    ].astype(BF16)
                gpack[slot, z, at : at + SEG] = piece
            for at in range(len(plan) * SEG, n * share, SEG):
                gpack[at // share, z, at % share : at % share + SEG] = jnp.zeros((SEG, ROWS), BF16)


def post(n, m, share, held, seen_len, dq, dk, dv, stream, ga, seen, vis, win, cols, vec_in):
    _, a, e = seen.shape
    d = win.shape[0]
    cap = up16(-(-held // n))
    once = pl.Buffered(1)
    const = lambda *s: pl.BlockSpec(s, lambda c: (0,) * len(s), pipeline_mode=once)
    lead = lambda *s: pl.BlockSpec((1,) + s, lambda c: (c,) + (0,) * len(s))
    shape = jax.ShapeDtypeStruct
    vm = pltpu.VMEM
    return pl.pallas_call(
        functools.partial(post_kernel, n, m, share, held, seen_len),
        grid=(2,),
        in_specs=[
            lead(d, LP), lead(d, LP), lead(d, LP), lead(d, LP), lead(d, LP), lead(a, e), lead(a, 1),
            const(d, 3 * d), const(d, 16), const(16, d),
        ],
        out_specs=[const(n, m, share, ROWS), const(n, cap, d)],
        out_shape=[shape((n, m, share, ROWS), BF16), shape((n, cap, d), BF16)],
        scratch_shapes=[
            vm((d, 3 * d), F32), vm((8, 3 * d), F32), vm((d, LANES), F32), vm((e, d), F32),
            vm((d + 16, LP), BF16), vm((2 * a, d), BF16),
        ],
        compiler_params=params(),
        cost_estimate=cost(2e10, 2e7),
    )(dq, dk, dv, stream, ga, seen, vis, win, cols, vec_in)


def leave_kernel(n, m, gpack, gp, mlp, fin, ret, mlp_out, a1, a2s, a2r, tot, tot_b, brecv, fin_s, ret_s, mlp_s,
                 gs, gr, s1, r1, s2, r2, sb, rb, sc, rc, sm, rm, sf, rf):
    clip = lax.axis_index("clip")
    wt = lax.axis_index("wt")
    half = n // 2
    core = lax.rem(clip, 2)
    chip = clip // 2
    partner = clip + 1 - 2 * core
    mlp_s[clip] = mlp[...]
    greet(n, m, clip, wt)
    sends = []

    def send(*args):
        copy = remote(*args)
        copy.start()
        sends.append(copy)

    order = [*range(1, half), 0]
    turns = [*range(1, m), 0]
    for k in turns:
        zz = lax.rem(wt + k, m)
        for j in order:
            spot = lax.rem(chip + j, half)
            send(gpack.at[2 * spot + 1 - core, zz], a1.at[j, k], s1.at[j, k], r1.at[j, k], partner, wt)
    for k in turns:
        zz = lax.rem(wt + k, m)
        for j in order:
            mine = 2 * lax.rem(chip + j, half) + core
            remote(gpack.at[mine, zz], a1.at[j, k], s1.at[j, k], r1.at[j, k], partner, wt).wait_recv()
            both = gpack[mine, zz].astype(F32) + a1[j, k].astype(F32)
            if j == 0:
                tot[k] = both
            else:
                a2s[j, k] = both.astype(BF16)
                send(a2s.at[j, k], a2r.at[j, k], s2.at[j, k], r2.at[j, k], mine, wt)
    for k in [*range(2, n, 2), *range(1, n, 2)]:
        dest = lax.rem(clip + k, n)
        send(gp.at[dest], ret_s.at[clip], gs.at[k], gr.at[k], dest, wt)
    ret_s[clip] = gp[clip]
    for j in order:
        dest = lax.rem(clip + 2 * j, n) if j else partner
        send(mlp_s.at[clip], mlp_s.at[clip], sm.at[j], rm.at[j], dest, wt)
    for k in turns:
        zz = lax.rem(wt + k, m)
        total = tot[k]
        for j in range(1, half):
            source = lax.rem(clip - 2 * j + n, n)
            remote(a2s.at[j, k], a2r.at[j, k], s2.at[j, k], r2.at[j, k], source, wt).wait_recv()
            total = total + a2r[j, k].astype(F32)
        if k:
            tot_b[k] = total.astype(BF16)
            send(tot_b.at[k], brecv.at[k], sb.at[k], rb.at[k], clip, zz)
    for k in range(1, m):
        source = lax.rem(wt - k + m, m)
        remote(tot_b.at[k], brecv.at[k], sb.at[k], rb.at[k], clip, source).wait_recv()
        total = total + brecv[k].astype(F32)
    fin_s[clip] = total.astype(BF16)
    for k in [*range(2, n, 2), *range(1, n, 2)]:
        send(fin_s.at[clip], fin_s.at[clip], sc.at[k], rc.at[k], lax.rem(clip + k, n), wt)
    for j in range(1, half):
        source = lax.rem(clip - 2 * j + n, n)
        remote(mlp_s.at[source], mlp_s.at[source], sm.at[j], rm.at[j], source, wt).wait_recv()
        send(mlp_s.at[source], mlp_s.at[source], sf.at[j], rf.at[j], partner, wt)
    for k in range(1, n):
        source = lax.rem(clip - k + n, n)
        remote(gp.at[source], ret_s.at[source], gs.at[k], gr.at[k], source, wt).wait_recv()
    ret[...] = ret_s[...]
    for j in range(half):
        source = lax.rem(partner - 2 * j + n, n)
        sems = (sf.at[j], rf.at[j]) if j else (sm.at[0], rm.at[0])
        remote(mlp_s.at[source], mlp_s.at[source], *sems, partner, wt).wait_recv()
    mlp_out[...] = mlp_s[...]
    for k in range(1, n):
        source = lax.rem(clip - k + n, n)
        remote(fin_s.at[source], fin_s.at[source], sc.at[k], rc.at[k], source, wt).wait_recv()
    fin[...] = fin_s[...]
    for copy in sends:
        copy.wait_send()


def leave(n, m, gpack, gp, mlp):
    _, _, share, _ = gpack.shape
    _, cap, d = gp.shape
    whole = pl.BlockSpec(memory_space=pltpu.VMEM)
    shape = jax.ShapeDtypeStruct
    vm = pltpu.VMEM
    dma = pltpu.SemaphoreType.DMA
    half = n // 2
    return pl.pallas_call(
        functools.partial(leave_kernel, n, m),
        in_specs=[whole] * 3,
        out_specs=[whole] * 3,
        out_shape=[shape((n, share, ROWS), BF16), shape((n, cap, d), BF16), shape((n,) + mlp.shape, BF16)],
        scratch_shapes=[
            vm((half, m, share, ROWS), BF16), vm((half, m, share, ROWS), BF16), vm((half, m, share, ROWS), BF16),
            vm((m, share, ROWS), F32), vm((m, share, ROWS), BF16), vm((m, share, ROWS), BF16),
            vm((n, share, ROWS), BF16), vm((n, cap, d), BF16), vm((n,) + mlp.shape, BF16),
            dma((n,)), dma((n,)), dma((half, m)), dma((half, m)), dma((half, m)), dma((half, m)),
            dma((m,)), dma((m,)), dma((n,)), dma((n,)),
            dma((half,)), dma((half,)), dma((half,)), dma((half,)),
        ],
        compiler_params=params(collective_id=1, has_side_effects=True),
        cost_estimate=cost(4e9, 4e6),
    )(gpack, gp, mlp)


def finish_kernel(n, m, plan, mlp_plan, fin, ret, mlp, wp, egrad, dwp, dwin, dwm, dwe, dwr, *vecs):
    clip = lax.axis_index("clip")
    wt = lax.axis_index("wt")
    held = egrad.shape[0]
    cap = ret.shape[1]
    row = lax.broadcasted_iota(jnp.int32, (held, cap), 0)
    col = lax.broadcasted_iota(jnp.int32, (held, cap), 1)
    own = None
    for dest in range(n):
        start = first_slot(dest, held, clip, n)
        stop = first_slot(dest + 1, held, clip, n)
        hot = ((row - start == col) & (row < stop)).astype(F32).astype(BF16)
        part = dg(hot, ret[dest], 1, 0)
        own = part if own is None else own + part
    egrad[...] = dg(own.astype(BF16), wp[...], 1, 1).astype(BF16)
    for name, r, slot, at in plan:
        piece = fin[slot, at : at + SEG].astype(F32)
        if name == "wp":
            dwp[r : r + SEG] = piece
        elif name != "vec":
            dwin[r : r + SEG, name * ROWS : (name + 1) * ROWS] = piece
        else:
            for z in range(m):
                @pl.when(wt == z)
                def _():
                    for i, ref in enumerate(vecs[:BIAS_E]):
                        w = ref.shape[0]
                        ref[...] = piece[i, z * w : (z + 1) * w]
                    w = vecs[BIAS_E].shape[0]
                    line = BIAS_E + z * w // ROWS
                    vecs[BIAS_E][...] = piece[line, z * w % ROWS : z * w % ROWS + w]
    for name, r, slot, at in mlp_plan:
        piece = mlp[slot, at : at + SEG].astype(F32)
        if name == "wm":
            dwm[r : r + SEG] = piece
        elif name == "wr":
            dwr[r : r + SEG] = piece
        else:
            dwe[r : r + SEG, name * ROWS : (name + 1) * ROWS] = piece


def finish(n, m, held, fin, ret, mlp, wp, f):
    e, d = wp.shape
    whole = pl.BlockSpec(memory_space=pltpu.VMEM)
    shape = jax.ShapeDtypeStruct
    plan = segments([("wp", e // m)] + [(j, d // m) for j in range(3)] + [("vec", SEG)], fin.shape[1])
    mlp_plan = segments(mlp_parts(d, f, m), mlp.shape[1])
    outs = [shape((held, e), BF16)] + [
        shape((r // m, c), F32) for r, c in ((e, d), (d, 3 * d), (d, d), (d, f), (f, d))
    ] + [shape((d // m,), F32)] * BIAS_E + [shape((f // m,), F32)]
    return pl.pallas_call(
        functools.partial(finish_kernel, n, m, plan, mlp_plan),
        in_specs=[whole] * 4,
        out_specs=[whole] * len(outs),
        out_shape=outs,
        compiler_params=params(),
        cost_estimate=cost(1e9, 4e6),
    )(fin, ret, mlp, wp)


def core(n, m, held, seen_len, seen, vis, wp, win, cols, be, wpack, upstream, reduce_mlp=None):
    d = cols.shape[0]
    pos = jnp.asarray(position_table(d))
    stream, q, kv, k_rows, v_rows = pre(seen, vis, wp, cols, pos, win)
    o, inv, e = attend(k_rows, q, kv)
    share = up16(-(-wpack.shape[1] // n))
    dec, ga, do, dsum, mlp, vec = mid(n, m, share, o, inv, stream, upstream.reshape(2, L, d), wpack, be, cols)
    if reduce_mlp is not None:
        mlp = reduce_mlp(mlp)
    dq, dk, dv = attend_back(e, v_rows, q, do, dsum, kv)
    share = up16(-(-(wp.shape[0] // m + 3 * (d // m) + SEG) // n))
    gpack, gp = post(n, m, share, held, seen_len, dq, dk, dv, stream, ga, seen, vis, win, cols, vec)
    return dec, mlp, gpack, gp


def per_device(encoded, visible_at, wp, token, gain1, shift1, win, bq, bv, wm, bm, gain2, shift2, we, be, wr, br, upstream):
    n = lax.axis_size("clip")
    m = lax.axis_size("wt")
    held = encoded.shape[0]
    seen_len = visible_at.shape[1]
    d = wp.shape[1]
    f = be.shape[0] * m
    local = pack_mlp(wm, we, wr)
    wpack = lax.all_gather(local, "wt", axis=0, tiled=True).reshape(m, local.shape[0], ROWS)
    vecs = (token, gain1, shift1, bq, bv, bm, gain2, shift2, br, be)
    seen, vis, wp_full, win_full, cols, be_col = enter(n, m, encoded, visible_at, wp, win, vecs)

    def reduce_mlp(mlp):
        mlp = lax.psum_scatter(mlp.reshape(-1, ROWS), "clip", scatter_dimension=0, tiled=True)
        return lax.psum_scatter(mlp, "wt", scatter_dimension=0, tiled=True)

    dec, mlp, gpack, gp = core(
        n, m, held, seen_len, seen, vis, wp_full, win_full, cols, be_col, wpack, upstream, reduce_mlp
    )
    fin, ret, mlp = leave(n, m, gpack, gp, mlp)
    egrad, dwp, dwin, dwm, dwe, dwr, *small = finish(n, m, held, fin, ret, mlp, wp_full, f)
    t, g1, s1, vq, vv, vm, g2, s2, vr, ve = small
    return (
        dec.reshape(2 * L, d), egrad, dwp, t, g1, s1, dwin, vq, vv, dwm, vm, g2, s2, dwe, ve, dwr, vr,
    )


def solution(mesh):
    both, wt = P(("clip", "wt"), None), P("wt")
    mat = P("wt", None)
    params_in = (mat, wt, wt, wt, mat, wt, wt, mat, wt, wt, wt, mat, wt, mat, wt)
    return jax.shard_map(
        per_device,
        mesh=mesh,
        in_specs=(both, both) + params_in + (both,),
        out_specs=(both, both) + params_in,
        check_vma=False,
    )
```

```python
import functools
import math

import jax
import jax.numpy as jnp
import numpy as np
from jax import lax
from jax.experimental import pallas as pl
from jax.experimental.pallas import tpu as pltpu
from jax.sharding import PartitionSpec as P

H = 6
HEAD = 64
L = 1568
LANES = 128
LP = -(-L // LANES) * LANES
KP = L
EPSILON = 1e-06
LOG2E = math.log2(math.e)
Q_SCALE = LOG2E / math.sqrt(HEAD)
ROOT_HALF = math.sqrt(0.5)
INV_ROOT_TWO_PI = 1.0 / math.sqrt(2.0 * math.pi)
SAFE_EXPONENT = 60.0
VMEM_LIMIT = 60 * 2**20
FFC = 512
Q_BLOCKS = ((0, 896), (896, LP - 896))
F32 = jnp.float32
BF16 = jnp.bfloat16


SEG = 16
ROWS = 384
MESH = pl.DeviceIdType.MESH
TOKEN, GAIN1, SHIFT1, BIAS_Q, BIAS_V, BIAS_M, GAIN2, SHIFT2, BIAS_R, BIAS_E = range(10)


def params(**kw):
    return pltpu.CompilerParams(vmem_limit_bytes=VMEM_LIMIT, **kw)


def cost(flops, moved=0):
    return pl.CostEstimate(flops=int(flops), bytes_accessed=int(moved), transcendentals=0)


def up16(x):
    return -(-x // SEG) * SEG


def segments(parts, share):
    out = []
    at = 0
    for name, rows in parts:
        for r in range(0, rows, SEG):
            out.append((name, r, at // share, at % share))
            at += SEG
    return out


def dg(a, b, ca, cb):
    return lax.dot_general(a, b, (((ca,), (cb,)), ((), ())), preferred_element_type=F32)


def position_table(width):
    places = np.arange(LP, dtype=np.float64)[None, :]
    columns = np.arange(width)
    exponent = (2 * (columns // 2)).astype(np.float64) / width
    angles = places / np.power(10000.0, exponent)[:, None]
    return np.where(columns[:, None] % 2 == 0, np.sin(angles), np.cos(angles)).astype(np.float32)


def norm_stats(x):
    center = x - jnp.mean(x, 0, keepdims=True)
    recip = lax.rsqrt(jnp.mean(center * center, 0, keepdims=True) + EPSILON)
    return center * recip, recip


def norm_back(e, scaled, recip, gain):
    lifted = e * gain
    return recip * (
        lifted
        - jnp.mean(lifted, 0, keepdims=True)
        - scaled * jnp.mean(lifted * scaled, 0, keepdims=True)
    )


def split3(x):
    hi = x.astype(BF16)
    rest = x - hi.astype(F32)
    mid = rest.astype(BF16)
    low = (rest - mid.astype(F32)).astype(BF16)
    return hi, mid, low


def aug_rows(x):
    hi, mid, low = split3(x)
    row = lax.broadcasted_iota(jnp.int32, (16, x.shape[1]), 0)
    zero = jnp.zeros((16, x.shape[1]), F32)
    out = jnp.where(row == 0, hi.astype(F32), zero)
    out = jnp.where(row == 1, mid.astype(F32), out)
    out = jnp.where(row == 2, low.astype(F32), out)
    return out.astype(BF16)


def one_hot(vis, width):
    place = lax.broadcasted_iota(jnp.int32, (vis.shape[0], width), 1).astype(F32)
    return (vis == place).astype(F32)


def first_slot(dest, held, clip, n):
    return (dest * held - clip + n - 1) // n


def interleave(rows, cols, clip, source, held, seen, seen_pad, n, by_row):
    first = (clip * held - source + n - 1) // n
    base = source + n * first - clip * held
    place = lax.broadcasted_iota(jnp.int32, (rows, cols), 0 if by_row else 1)
    slot = lax.broadcasted_iota(jnp.int32, (rows, cols), 1 if by_row else 0)
    second = place >= seen_pad
    local = jnp.where(second, place - (seen_pad - seen), place)
    good = (place < seen) | (second & (place < seen_pad + seen))
    return (good & (local == base + n * slot)).astype(F32).astype(BF16)


def greet(n, m, clip, wt):
    barrier = pltpu.get_barrier_semaphore()
    for k in range(1, n):
        pl.semaphore_signal(barrier, inc=1, device_id=(lax.rem(clip + k, n), wt), device_id_type=MESH)
    for k in range(1, m):
        pl.semaphore_signal(barrier, inc=1, device_id=(clip, lax.rem(wt + k, m)), device_id_type=MESH)
    pl.semaphore_wait(barrier, n + m - 2)


def remote(src, dst, send, recv, clip, wt):
    return pltpu.make_async_remote_copy(
        src_ref=src, dst_ref=dst, send_sem=send, recv_sem=recv, device_id=(clip, wt), device_id_type=MESH
    )


def enter_kernel(n, m, share, cap, seen_pad, *refs):
    (enc, vis_in, wp_in, win_in, *vecs) = refs[:14]
    (seen_out, vis_out, wp, win, cols, be) = refs[14:20]
    (pack, gath, out_rows, in_rows, vec_s, vis_s, zs, zr, bs, br, fs, fr, rs, rr) = refs[20:]
    clip = lax.axis_index("clip")
    wt = lax.axis_index("wt")
    held = enc.shape[0]
    seen = vis_in.shape[1]
    wp_rows = wp_in.shape[0]
    win_rows = win_in.shape[0]
    half = n // 2
    plan = segments(
        [("wp", wp_rows)] + [(j, win_rows) for j in range(3)] + [("vec", SEG)], share
    )
    vec_s[...] = jnp.zeros_like(vec_s)
    for i, ref in enumerate(vecs):
        vec_s[i, : ref.shape[0]] = ref[...].astype(F32)
    for name, r, slot, at in plan:
        if name == "wp":
            piece = wp_in[r : r + SEG]
        elif name == "vec":
            piece = vec_s[...].astype(BF16)
        else:
            piece = win_in[r : r + SEG, name * ROWS : (name + 1) * ROWS]
        pack[slot, at : at + SEG] = piece
    for at in range(len(plan) * SEG, n * share, SEG):
        pack[at // share, at % share : at % share + SEG] = jnp.zeros((SEG, ROWS), BF16)
    greet(n, m, clip, wt)

    sends = []
    partner = clip + 1 - 2 * lax.rem(clip, 2)
    for k in range(1, m):
        copy = remote(pack.at[clip], gath.at[clip, wt], zs.at[k], zr.at[k], clip, lax.rem(wt + k, m))
        copy.start()
        sends.append(copy)
    gath[clip, wt] = pack[clip]

    def spread(k):
        z = lax.rem(wt - k + m, m)
        for j in [*range(1, half), 0]:
            piece = gath.at[clip, z]
            dest = lax.rem(clip + 2 * j, n) if j else partner
            copy = remote(piece, piece, bs.at[j, k], br.at[j, k], dest, wt)
            copy.start()
            sends.append(copy)

    spread(0)

    rows_at = lax.broadcasted_iota(jnp.int32, (cap, held), 0)
    cols_at = lax.broadcasted_iota(jnp.int32, (cap, held), 1)
    row_sends = []
    for k in [*range(2, n, 2), *range(3, n, 2), 1, 0] if n > 2 else range(n - 1, -1, -1):
        dest = lax.rem(clip + k, n)
        hot = (rows_at + first_slot(dest, held, clip, n) == cols_at).astype(F32).astype(BF16)
        rows = dg(hot, enc[...], 1, 0).astype(BF16)
        if k == 0:
            in_rows[clip] = rows
        else:
            out_rows[k] = rows
            copy = remote(out_rows.at[k], in_rows.at[clip], rs.at[k], rr.at[k], dest, wt)
            copy.start()
            row_sends.append(copy)

    for k in range(1, m):
        source = lax.rem(wt - k + m, m)
        remote(pack.at[clip], gath.at[clip, source], zs.at[k], zr.at[k], clip, source).wait_recv()
        spread(k)

    vis_s[...] = jnp.full(vis_s.shape, -1.0, F32)
    vis_s[0:2, :seen] = vis_in[...].astype(F32)
    turned = vis_s[...].T
    for copy_at in range(2):
        vis_out[copy_at] = turned[:seen_pad, copy_at : copy_at + 1]

    for k in range(m):
        z = lax.rem(wt - k + m, m)
        for j in range(1, half):
            source = lax.rem(clip - 2 * j + n, n)
            piece = gath.at[source, z]
            remote(piece, piece, bs.at[j, k], br.at[j, k], source, wt).wait_recv()
            copy = remote(piece, piece, fs.at[j, k], fr.at[j, k], partner, wt)
            copy.start()
            sends.append(copy)

    for k in range(1, n):
        source = lax.rem(clip - k + n, n)
        remote(out_rows.at[k], in_rows.at[source], rs.at[k], rr.at[k], source, wt).wait_recv()
    total = None
    for source in range(n):
        hot = interleave(2 * seen_pad, cap, clip, source, held, seen, seen_pad, n, True)
        part = dg(hot, in_rows[source], 1, 0)
        total = part if total is None else total + part
    total = total.astype(BF16)
    seen_out[0] = total[:seen_pad]
    seen_out[1] = total[seen_pad:]

    for k in range(m):
        z = lax.rem(wt - k + m, m)
        for j in range(half):
            source = lax.rem(partner - 2 * j + n, n)
            piece = gath.at[source, z]
            sems = (fs.at[j, k], fr.at[j, k]) if j else (bs.at[0, k], br.at[0, k])
            remote(piece, piece, *sems, partner, wt).wait_recv()
    for z in range(m):
        for name, r, slot, at in plan:
            piece = gath[slot, z, at : at + SEG]
            if name == "wp":
                wp[z * wp_rows + r : z * wp_rows + r + SEG] = piece
            elif name == "vec":
                turned = piece.astype(F32).T
                small = vecs[0].shape[0]
                cols[z * small : (z + 1) * small] = turned[:small]
                large = vecs[BIAS_E].shape[0]
                be[z * large : (z + 1) * large] = turned[:large, BIAS_E : BIAS_E + 1]
            else:
                win[z * win_rows + r : z * win_rows + r + SEG, name * ROWS : (name + 1) * ROWS] = piece
    for copy in sends + row_sends:
        copy.wait_send()


def pack_kernel(wm, we, wr, out):
    rows = wm.shape[0]
    out[:rows] = wm[...]
    at = rows
    for j in range(we.shape[1] // ROWS):
        out[at : at + rows] = we[:, j * ROWS : (j + 1) * ROWS]
        at += rows
    out[at:] = wr[...]


def pack_mlp(wm, we, wr):
    rows = wm.shape[0] + wm.shape[0] * (we.shape[1] // ROWS) + wr.shape[0]
    whole = pl.BlockSpec(memory_space=pltpu.VMEM)
    return pl.pallas_call(
        pack_kernel,
        in_specs=[whole] * 3,
        out_specs=whole,
        out_shape=jax.ShapeDtypeStruct((rows, ROWS), BF16),
        compiler_params=params(),
        cost_estimate=cost(0, 1.3e6),
    )(wm, we, wr)


def enter(n, m, enc, vis, wp, win, vecs):
    held, e = enc.shape
    seen = vis.shape[1]
    seen_pad = up16(seen)
    d = wp.shape[1]
    cap = up16(-(-held // n))
    share = up16(-(-(wp.shape[0] + 3 * win.shape[0] + SEG) // n))
    whole = pl.BlockSpec(memory_space=pltpu.VMEM)
    shape = jax.ShapeDtypeStruct
    dma = pltpu.SemaphoreType.DMA
    ins = (enc, vis, wp, win, *vecs)
    return pl.pallas_call(
        functools.partial(enter_kernel, n, m, share, cap, seen_pad),
        in_specs=[whole] * len(ins),
        out_specs=[whole] * 6,
        out_shape=[
            shape((2, seen_pad, e), BF16), shape((2, seen_pad, 1), F32), shape((e, d), BF16),
            shape((d, 3 * d), BF16), shape((d, 16), F32), shape((vecs[BIAS_E].shape[0] * m, 1), F32),
        ],
        scratch_shapes=[
            pltpu.VMEM((n, share, ROWS), BF16), pltpu.VMEM((n, m, share, ROWS), BF16),
            pltpu.VMEM((n, cap, e), BF16), pltpu.VMEM((n, cap, e), BF16),
            pltpu.VMEM((SEG, ROWS), F32), pltpu.VMEM((8, 2 * LANES), F32),
            dma((m,)), dma((m,)), dma((n // 2, m)), dma((n // 2, m)), dma((n // 2, m)), dma((n // 2, m)),
            dma((n,)), dma((n,)),
        ],
        compiler_params=params(collective_id=0, has_side_effects=True),
        cost_estimate=cost(6e9, 4e6),
    )(*ins)


def front_kernel(seen, vis, wp, cols, pos, win, o_out, inv_out, e_out, stream_hbm, q_hbm, kt_hbm, v_hbm,
                 stream_s, q_s, k_s, v_s, k_rows, v_rows, v_aug, sems):
    copy = pl.program_id(0)
    step = pl.program_id(1)
    width = wp.shape[1]
    moves = [
        pltpu.make_async_copy(src, dst.at[copy], sems.at[i])
        for i, (src, dst) in enumerate(
            ((stream_s, stream_hbm), (q_s, q_hbm), (k_s, kt_hbm), (v_rows, v_hbm))
        )
    ]

    @pl.when(step == 0)
    def _():
        proj = dg(seen[0], wp[...], 1, 0).astype(BF16)
        hot = one_hot(vis[0], LP)
        covered = jnp.sum(hot, 0, keepdims=True)
        stream = dg(proj, hot.astype(BF16), 0, 0) + (1.0 - covered) * cols[:, TOKEN : TOKEN + 1] + pos[...]
        stream_s[...] = stream
        moves[0].start()
        scaled, _ = norm_stats(stream)
        normed = (scaled * cols[:, GAIN1 : GAIN1 + 1] + cols[:, SHIFT1 : SHIFT1 + 1]).astype(BF16)
        lane = lax.broadcasted_iota(jnp.int32, (L, LANES), 1)
        ones = (lane < HEAD + 3).astype(F32).astype(BF16)
        for part in (2, 1, 0):
            sl = slice(part * width, (part + 1) * width)
            mixed = dg(win[:, sl], normed, 0, 0)
            if part == 0:
                q_s[...] = ((mixed + cols[:, BIAS_Q : BIAS_Q + 1]) * Q_SCALE).astype(BF16)
                moves[1].start()
                continue
            if part == 2:
                mixed = mixed + cols[:, BIAS_V : BIAS_V + 1]
            mixed = mixed.astype(BF16)
            dst = k_s if part == 1 else v_s
            dst[:, :L] = mixed[:, :L]
            dst[:, L:] = jnp.zeros((width, LP - L), BF16)
            rows = k_rows if part == 1 else v_rows
            for h in range(H):
                if part == 2:
                    rows[h] = ones
                rows[h, :, :HEAD] = mixed[h * HEAD : (h + 1) * HEAD].T[:L]
            moves[2 if part == 1 else 3].start()

    @pl.when(step > 0)
    def _():
        head = pl.ds(pl.multiple_of((step - 1) * HEAD, HEAD), HEAD)
        row = lax.broadcasted_iota(jnp.int32, (16, L), 0)
        v_aug[:HEAD] = v_s[head, :L]
        v_aug[HEAD:] = (row == 0).astype(F32).astype(BF16)
        qf = q_s[head, :].astype(F32)
        kf = k_s[head, :].astype(F32)
        bound = jnp.max(jnp.sum(qf * qf, 0, keepdims=True)) * jnp.max(jnp.sum(kf * kf, 0, keepdims=True))
        safe = bound <= SAFE_EXPONENT * SAFE_EXPONENT

        def run(shift):
            for start, size in Q_BLOCKS:
                sl = slice(start, start + size)
                s = dg(k_rows[step - 1, :, :HEAD], q_s[head, sl], 1, 0)
                if shift:
                    s = s - jnp.max(s, 0, keepdims=True)
                e = jnp.exp2(s).astype(BF16)
                e_out[0, 0, :, sl] = e
                o = dg(v_aug[...], e, 1, 0)
                inv = 1.0 / o[HEAD : HEAD + 1]
                o_out[0, :, sl] = o[:HEAD] * inv
                inv_out[0, 0, :, sl] = inv

        pl.when(safe)(lambda: run(False))
        pl.when(jnp.logical_not(safe))(lambda: run(True))

    @pl.when(step == H)
    def _():
        for move in moves:
            move.wait()


def front(seen, vis, wp, cols, pos, win):
    _, a, e = seen.shape
    d = wp.shape[1]
    const = lambda *s: pl.BlockSpec(s, lambda c, i: (0,) * len(s), pipeline_mode=pl.Buffered(1))
    lead = lambda *s: pl.BlockSpec((1,) + s, lambda c, i: (c,) + (0,) * len(s))
    head = lambda c, i: (c, jnp.maximum(i - 1, 0), 0)
    wide = lambda c, i: (c, jnp.maximum(i - 1, 0), 0, 0)
    any_ = pl.BlockSpec(memory_space=pl.ANY)
    shape = jax.ShapeDtypeStruct
    vm = pltpu.VMEM
    return pl.pallas_call(
        front_kernel,
        grid=(2, H + 1),
        in_specs=[lead(a, e), lead(a, 1), const(e, d), const(d, 16), const(d, LP), const(d, 3 * d)],
        out_specs=[
            pl.BlockSpec((1, HEAD, LP), head), pl.BlockSpec((1, 1, 1, LP), wide), pl.BlockSpec((1, 1, L, LP), wide),
            any_, any_, any_, any_,
        ],
        out_shape=[
            shape((2, d, LP), F32), shape((2, H, 1, LP), F32), shape((2, H, L, LP), BF16),
            shape((2, d, LP), F32), shape((2, d, LP), BF16), shape((2, d, LP), BF16), shape((2, H, L, LANES), BF16),
        ],
        scratch_shapes=[
            vm((d, LP), F32), vm((d, LP), BF16), vm((d, LP), BF16), vm((d, LP), BF16),
            vm((H, L, LANES), BF16), vm((H, L, LANES), BF16), vm((HEAD + 16, L), BF16),
            pltpu.SemaphoreType.DMA((4,)),
        ],
        compiler_params=params(),
        cost_estimate=cost(4e10, 8e7),
    )(seen, vis, wp, cols, pos, win)


def mlp_parts(d, f, m):
    return [("wm", d // m)] + [(j, d // m) for j in range(f // ROWS)] + [("wr", f // m)]


def mid_kernel(n, m, share, o, inv, stream, up, wpack, be, cols,
               dec, ga_out, do_out, dsum_out, gpack, vec_out,
               wm, we, wr, dwm, dwe, dwr, dvec, dbe, drb, stats, n2, act_s, gl_s, g_s):
    copy = pl.program_id(0)
    ff = pl.program_id(1)
    last = pl.num_programs(1) - 1
    d = wm.shape[0]
    f = wr.shape[0]
    parts = mlp_parts(d, f, m)

    @pl.when((copy == 0) & (ff == 0))
    def _():
        for z in range(m):
            at = 0
            for name, rows in parts:
                piece = wpack[z, at : at + rows]
                dst = slice(z * rows, (z + 1) * rows)
                if name == "wm":
                    wm[dst] = piece
                elif name == "wr":
                    wr[dst] = piece
                else:
                    we[dst, name * ROWS : (name + 1) * ROWS] = piece
                at += rows
        dwm[...] = jnp.zeros_like(dwm)
        dwe[...] = jnp.zeros_like(dwe)
        dwr[...] = jnp.zeros_like(dwr)
        dvec[...] = jnp.zeros_like(dvec)
        dbe[...] = jnp.zeros_like(dbe)
        drb[...] = jnp.zeros_like(drb)

    @pl.when(ff == 0)
    def _():
        ctx = o[0].astype(BF16)
        x = stream[0] + dg(wm[...], ctx, 0, 0) + cols[:, BIAS_M : BIAS_M + 1]
        ga_out[0] = x
        mean = jnp.mean(x, 0, keepdims=True)
        center = x - mean
        recip = lax.rsqrt(jnp.mean(center * center, 0, keepdims=True) + EPSILON)
        stats[0:1] = mean
        stats[1:2] = recip
        n2[:d] = (center * recip * cols[:, GAIN2 : GAIN2 + 1] + cols[:, SHIFT2 : SHIFT2 + 1]).astype(BF16)
        row = lax.broadcasted_iota(jnp.int32, (16, LP), 0)
        n2[d:] = (row == 0).astype(F32).astype(BF16)
        g = (up[0].astype(F32) * 0.5).astype(BF16)
        g_s[:L] = g
        g_s[L:] = jnp.zeros((LP - L, d), BF16)
        drb[...] += dg(jnp.ones((8, L), BF16), g, 1, 0)

    rows = pl.ds(pl.multiple_of(ff * FFC, FFC), FFC)
    g = g_s[...]
    lifted = dg(we[:, rows], n2[:d], 0, 0) + be[rows, :]
    bell = jnp.exp(-0.5 * lifted * lifted)
    cdf = 0.5 * (1.0 + lax.erf(lifted * ROOT_HALF))
    act = (lifted * cdf).astype(BF16)
    slope = cdf + lifted * bell * INV_ROOT_TWO_PI
    gl = (dg(wr[rows, :], g, 1, 1) * slope).astype(BF16)
    act_s[rows, :] = act
    gl_s[rows, :] = gl

    @pl.when(ff == last)
    def _():
        x = ga_out[0]
        dwr[...] += dg(act_s[...], g_s[...], 1, 0)
        grad = dg(n2[...], gl_s[...], 1, 1)
        dwe[...] += grad[:d]
        dbe[...] += grad[d : d + 8]
        out = x + dg(wr[...], act_s[...], 0, 0) + cols[:, BIAS_R : BIAS_R + 1]
        dec[0] = out.astype(BF16).T[:L]
        scaled = (x - stats[0:1]) * stats[1:2]
        e = dg(we[...], gl_s[...], 1, 0)
        dvec[:, 0:1] += jnp.sum(e * scaled, 1, keepdims=True)
        dvec[:, 1:2] += jnp.sum(e, 1, keepdims=True)
        back = norm_back(e, scaled, stats[1:2], cols[:, GAIN2 : GAIN2 + 1])
        ga = g_s[...].T.astype(F32) + back
        ga_out[0] = ga
        gm = ga.astype(BF16)
        dvec[:, 2:3] += jnp.sum(gm.astype(F32), 1, keepdims=True)
        ctx = o[0]
        dwm[...] += dg(ctx.astype(BF16), gm, 1, 1)
        do = dg(wm[...], gm, 1, 0)
        for h in range(H):
            hs = slice(h * HEAD, (h + 1) * HEAD)
            part = (do[hs] * inv[0, h]).astype(BF16)
            do_out[0, hs] = part
            dsum_out[0, h] = aug_rows(-jnp.sum(part.astype(F32) * ctx[hs], 0, keepdims=True))

    @pl.when((ff == last) & (copy == 1))
    def _():
        plan = segments(parts, share)
        for z in range(m):
            for name, r, slot, at in plan:
                if name == "wm":
                    piece = dwm[z * (d // m) + r : z * (d // m) + r + SEG]
                elif name == "wr":
                    piece = dwr[z * (f // m) + r : z * (f // m) + r + SEG]
                else:
                    piece = dwe[z * (d // m) + r : z * (d // m) + r + SEG, name * ROWS : (name + 1) * ROWS]
                gpack[slot, z, at : at + SEG] = piece.astype(BF16)
            for at in range(len(plan) * SEG, n * share, SEG):
                gpack[at // share, z, at % share : at % share + SEG] = jnp.zeros((SEG, ROWS), BF16)
        turned = dvec[...].T
        vec_out[...] = jnp.zeros_like(vec_out)
        vec_out[BIAS_M : BIAS_M + 1] = turned[2:3]
        vec_out[GAIN2 : GAIN2 + 1] = turned[0:1]
        vec_out[SHIFT2 : SHIFT2 + 1] = turned[1:2]
        vec_out[BIAS_R : BIAS_R + 1] = drb[0:1]
        for j in range(f // ROWS):
            vec_out[BIAS_E + j : BIAS_E + j + 1] = dbe[0:1, j * ROWS : (j + 1) * ROWS]


def mid(n, m, share, o, inv, stream, up, wpack, be, cols):
    d = cols.shape[0]
    f = be.shape[0]
    once = pl.Buffered(1)
    const = lambda *s: pl.BlockSpec(s, lambda c, k: (0,) * len(s), pipeline_mode=once)
    lead = lambda *s: pl.BlockSpec((1,) + s, lambda c, k: (c,) + (0,) * len(s))
    shape = jax.ShapeDtypeStruct
    vm = pltpu.VMEM
    return pl.pallas_call(
        functools.partial(mid_kernel, n, m, share),
        grid=(2, f // FFC),
        in_specs=[lead(d, LP), lead(H, 1, LP), lead(d, LP), lead(L, d), const(*wpack.shape), const(f, 1), const(d, 16)],
        out_specs=[
            lead(L, d), lead(d, LP), lead(d, LP), lead(H, 16, LP), const(n, m, share, ROWS), const(16, d),
        ],
        out_shape=[
            shape((2, L, d), BF16), shape((2, d, LP), F32), shape((2, d, LP), BF16), shape((2, H, 16, LP), BF16),
            shape((n, m, share, ROWS), BF16), shape((16, d), F32),
        ],
        scratch_shapes=[
            vm((d, d), BF16), vm((d, f), BF16), vm((f, d), BF16),
            vm((d, d), F32), vm((d, f), F32), vm((f, d), F32), vm((d, LANES), F32), vm((8, f), F32), vm((8, d), F32),
            vm((8, LP), F32), vm((d + 16, LP), BF16),
            vm((f, LP), BF16), vm((f, LP), BF16), vm((LP, d), BF16),
        ],
        compiler_params=params(),
        cost_estimate=cost(5e10, 4e7),
    )(o, inv, stream, up, wpack, be, cols)


def back_kernel(n, m, share, held, seen_len, e, v_rows, q, do, dsum, kt, stream, ga, seen, vis, win, cols, vec_in,
                gpack, gp_out, do_aug, gm, kept, qtmp, dwin, dbin, dvec, dwp, n1, gp_s):
    copy = pl.program_id(0)
    step = pl.program_id(1)
    clip = lax.axis_index("clip")
    d = win.shape[0]
    e_width = dwp.shape[0]
    seen_pad = seen.shape[1]
    cap = gp_out.shape[1]

    @pl.when((copy == 0) & (step == 0))
    def _():
        dwin[...] = jnp.zeros_like(dwin)
        dbin[...] = jnp.zeros_like(dbin)
        dvec[...] = jnp.zeros_like(dvec)
        dwp[...] = jnp.zeros_like(dwp)
        do_aug[HEAD + 16 :] = jnp.zeros((LANES - HEAD - 16, LP), BF16)
        kept[...] = jnp.zeros_like(kept)

    @pl.when(step < H)
    def _():
        head = pl.ds(pl.multiple_of(step * HEAD, HEAD), HEAD)
        do_aug[:HEAD] = do[0]
        do_aug[HEAD : HEAD + 16] = dsum[0, 0]
        k_sum = None
        v_sum = None
        for start, size in Q_BLOCKS:
            sl = slice(start, start + size)
            p = e[0, 0, :, sl]
            dp = dg(v_rows[0, 0], do_aug[:, sl], 1, 0)
            ds = (p.astype(F32) * dp).astype(BF16)
            v_part = dg(do_aug[:HEAD, sl], p, 1, 1)
            k_part = dg(q[0, :, sl], ds, 1, 1)
            v_sum = v_part if v_sum is None else v_sum + v_part
            k_sum = k_part if k_sum is None else k_sum + k_part
            qtmp[:, sl] = (dg(kt[0, :, :L], ds, 1, 0) * (1.0 / math.sqrt(HEAD))).astype(BF16)
        gm[pl.ds(pl.multiple_of(step * HEAD, HEAD), HEAD), :] = qtmp[...]
        for part, total in ((1, k_sum * (1.0 / LOG2E)), (2, v_sum)):
            kept[:, :L] = total.astype(BF16)
            gm[pl.ds(pl.multiple_of(part * d + step * HEAD, HEAD), HEAD), :] = kept[...]

    @pl.when(step == H)
    def _():
        x = stream[0]
        scaled, recip = norm_stats(x)
        n1[:d] = (scaled * cols[:, GAIN1 : GAIN1 + 1] + cols[:, SHIFT1 : SHIFT1 + 1]).astype(BF16)
        row = lax.broadcasted_iota(jnp.int32, (16, LP), 0)
        n1[d:] = (row == 0).astype(F32).astype(BF16)
        e = None
        for part in range(3):
            sl = slice(part * d, (part + 1) * d)
            grad = dg(n1[...], gm[sl], 1, 1)
            dwin[:, sl] += grad[:d]
            dbin[:, sl] += grad[d : d + 8]
            term = dg(win[:, sl], gm[sl], 1, 0)
            e = term if e is None else e + term
        dvec[:, 0:1] += jnp.sum(e * scaled, 1, keepdims=True)
        dvec[:, 1:2] += jnp.sum(e, 1, keepdims=True)
        gs = ga[0] + norm_back(e, scaled, recip, cols[:, GAIN1 : GAIN1 + 1])
        hot = one_hot(vis[0], LP)
        token = lax.broadcasted_iota(jnp.int32, (1, LP), 1)
        masked = jnp.where(token < L, 1.0 - jnp.sum(hot, 0, keepdims=True), 0.0)
        dvec[:, 2:3] += jnp.sum(gs * masked, 1, keepdims=True)
        gp = dg(hot.astype(BF16), gs.astype(BF16), 1, 1).astype(BF16)
        gp_s[pl.ds(pl.multiple_of(copy * seen_pad, SEG), seen_pad), :] = gp
        dwp[...] += dg(seen[0], gp, 0, 0)

    @pl.when((copy == 1) & (step == H))
    def _():
        for source in range(n):
            pick = interleave(cap, 2 * seen_pad, clip, source, held, seen_len, seen_pad, n, False)
            gp_out[source] = dg(pick, gp_s[...], 1, 0).astype(BF16)
        turned = dvec[...].T
        row = lax.broadcasted_iota(jnp.int32, (16, d), 0)
        vec = vec_in[...]
        vec = jnp.where(row == TOKEN, turned[2:3], vec)
        vec = jnp.where(row == GAIN1, turned[0:1], vec)
        vec = jnp.where(row == SHIFT1, turned[1:2], vec)
        vec = jnp.where(row == BIAS_Q, dbin[0:1, :d], vec)
        vec = jnp.where(row == BIAS_V, dbin[0:1, 2 * d :], vec).astype(BF16)
        wp_rows = e_width // m
        win_rows = d // m
        plan = segments([("wp", wp_rows)] + [(j, win_rows) for j in range(3)] + [("vec", SEG)], share)
        for z in range(m):
            for name, r, slot, at in plan:
                if name == "wp":
                    piece = dwp[z * wp_rows + r : z * wp_rows + r + SEG].astype(BF16)
                elif name == "vec":
                    piece = vec
                else:
                    piece = dwin[
                        z * win_rows + r : z * win_rows + r + SEG, name * ROWS : (name + 1) * ROWS
                    ].astype(BF16)
                gpack[slot, z, at : at + SEG] = piece
            for at in range(len(plan) * SEG, n * share, SEG):
                gpack[at // share, z, at % share : at % share + SEG] = jnp.zeros((SEG, ROWS), BF16)


def back(n, m, share, held, seen_len, e, v_rows, q, do, dsum, kt, stream, ga, seen, vis, win, cols, vec_in):
    _, a, width = seen.shape
    d = win.shape[0]
    cap = up16(-(-held // n))
    const = lambda *s: pl.BlockSpec(s, lambda c, i: (0,) * len(s), pipeline_mode=pl.Buffered(1))
    lead = lambda *s: pl.BlockSpec((1,) + s, lambda c, i: (c,) + (0,) * len(s))
    head = lambda c, i: (c, jnp.minimum(i, H - 1), 0)
    wide = lambda c, i: (c, jnp.minimum(i, H - 1), 0, 0)
    shape = jax.ShapeDtypeStruct
    vm = pltpu.VMEM
    return pl.pallas_call(
        functools.partial(back_kernel, n, m, share, held, seen_len),
        grid=(2, H + 1),
        in_specs=[
            pl.BlockSpec((1, 1, L, LP), wide), pl.BlockSpec((1, 1, L, LANES), wide), pl.BlockSpec((1, HEAD, LP), head),
            pl.BlockSpec((1, HEAD, LP), head), pl.BlockSpec((1, 1, 16, LP), wide), pl.BlockSpec((1, HEAD, LP), head),
            lead(d, LP), lead(d, LP), lead(a, width), lead(a, 1), const(d, 3 * d), const(d, 16), const(16, d),
        ],
        out_specs=[const(n, m, share, ROWS), const(n, cap, d)],
        out_shape=[shape((n, m, share, ROWS), BF16), shape((n, cap, d), BF16)],
        scratch_shapes=[
            vm((LANES, LP), BF16), vm((3 * d, LP), BF16), vm((HEAD, LP), BF16), vm((HEAD, LP), BF16),
            vm((d, 3 * d), F32), vm((8, 3 * d), F32), vm((d, LANES), F32), vm((width, d), F32),
            vm((d + 16, LP), BF16), vm((2 * a, d), BF16),
        ],
        compiler_params=params(),
        cost_estimate=cost(1e11, 1e8),
    )(e, v_rows, q, do, dsum, kt, stream, ga, seen, vis, win, cols, vec_in)


def leave_kernel(n, m, gpack, gp, mlp, fin, ret, mlp_out, a1, a2s, a2r, tot, tot_b, brecv, fin_s, ret_s, mlp_s,
                 gs, gr, s1, r1, s2, r2, sb, rb, sc, rc, sm, rm, sf, rf):
    clip = lax.axis_index("clip")
    wt = lax.axis_index("wt")
    half = n // 2
    core = lax.rem(clip, 2)
    chip = clip // 2
    partner = clip + 1 - 2 * core
    mlp_s[clip] = mlp[...]
    greet(n, m, clip, wt)
    sends = []

    def send(*args):
        copy = remote(*args)
        copy.start()
        sends.append(copy)

    order = [*range(1, half), 0]
    turns = [*range(1, m), 0]
    for k in turns:
        zz = lax.rem(wt + k, m)
        for j in order:
            spot = lax.rem(chip + j, half)
            send(gpack.at[2 * spot + 1 - core, zz], a1.at[j, k], s1.at[j, k], r1.at[j, k], partner, wt)
    for k in turns:
        zz = lax.rem(wt + k, m)
        for j in order:
            mine = 2 * lax.rem(chip + j, half) + core
            remote(gpack.at[mine, zz], a1.at[j, k], s1.at[j, k], r1.at[j, k], partner, wt).wait_recv()
            both = gpack[mine, zz].astype(F32) + a1[j, k].astype(F32)
            if j == 0:
                tot[k] = both
            else:
                a2s[j, k] = both.astype(BF16)
                send(a2s.at[j, k], a2r.at[j, k], s2.at[j, k], r2.at[j, k], mine, wt)
    for k in [*range(2, n, 2), *range(1, n, 2)]:
        dest = lax.rem(clip + k, n)
        send(gp.at[dest], ret_s.at[clip], gs.at[k], gr.at[k], dest, wt)
    ret_s[clip] = gp[clip]
    for j in order:
        dest = lax.rem(clip + 2 * j, n) if j else partner
        send(mlp_s.at[clip], mlp_s.at[clip], sm.at[j], rm.at[j], dest, wt)
    for k in turns:
        zz = lax.rem(wt + k, m)
        total = tot[k]
        for j in range(1, half):
            source = lax.rem(clip - 2 * j + n, n)
            remote(a2s.at[j, k], a2r.at[j, k], s2.at[j, k], r2.at[j, k], source, wt).wait_recv()
            total = total + a2r[j, k].astype(F32)
        if k:
            tot_b[k] = total.astype(BF16)
            send(tot_b.at[k], brecv.at[k], sb.at[k], rb.at[k], clip, zz)
    for k in range(1, m):
        source = lax.rem(wt - k + m, m)
        remote(tot_b.at[k], brecv.at[k], sb.at[k], rb.at[k], clip, source).wait_recv()
        total = total + brecv[k].astype(F32)
    fin_s[clip] = total.astype(BF16)
    for k in [*range(2, n, 2), *range(1, n, 2)]:
        send(fin_s.at[clip], fin_s.at[clip], sc.at[k], rc.at[k], lax.rem(clip + k, n), wt)
    for j in range(1, half):
        source = lax.rem(clip - 2 * j + n, n)
        remote(mlp_s.at[source], mlp_s.at[source], sm.at[j], rm.at[j], source, wt).wait_recv()
        send(mlp_s.at[source], mlp_s.at[source], sf.at[j], rf.at[j], partner, wt)
    for k in range(1, n):
        source = lax.rem(clip - k + n, n)
        remote(gp.at[source], ret_s.at[source], gs.at[k], gr.at[k], source, wt).wait_recv()
    ret[...] = ret_s[...]
    for j in range(half):
        source = lax.rem(partner - 2 * j + n, n)
        sems = (sf.at[j], rf.at[j]) if j else (sm.at[0], rm.at[0])
        remote(mlp_s.at[source], mlp_s.at[source], *sems, partner, wt).wait_recv()
    mlp_out[...] = mlp_s[...]
    for k in range(1, n):
        source = lax.rem(clip - k + n, n)
        remote(fin_s.at[source], fin_s.at[source], sc.at[k], rc.at[k], source, wt).wait_recv()
    fin[...] = fin_s[...]
    for copy in sends:
        copy.wait_send()


def leave(n, m, gpack, gp, mlp):
    _, _, share, _ = gpack.shape
    _, cap, d = gp.shape
    whole = pl.BlockSpec(memory_space=pltpu.VMEM)
    shape = jax.ShapeDtypeStruct
    vm = pltpu.VMEM
    dma = pltpu.SemaphoreType.DMA
    half = n // 2
    return pl.pallas_call(
        functools.partial(leave_kernel, n, m),
        in_specs=[whole] * 3,
        out_specs=[whole] * 3,
        out_shape=[shape((n, share, ROWS), BF16), shape((n, cap, d), BF16), shape((n,) + mlp.shape, BF16)],
        scratch_shapes=[
            vm((half, m, share, ROWS), BF16), vm((half, m, share, ROWS), BF16), vm((half, m, share, ROWS), BF16),
            vm((m, share, ROWS), F32), vm((m, share, ROWS), BF16), vm((m, share, ROWS), BF16),
            vm((n, share, ROWS), BF16), vm((n, cap, d), BF16), vm((n,) + mlp.shape, BF16),
            dma((n,)), dma((n,)), dma((half, m)), dma((half, m)), dma((half, m)), dma((half, m)),
            dma((m,)), dma((m,)), dma((n,)), dma((n,)),
            dma((half,)), dma((half,)), dma((half,)), dma((half,)),
        ],
        compiler_params=params(collective_id=1, has_side_effects=True),
        cost_estimate=cost(4e9, 4e6),
    )(gpack, gp, mlp)


def finish_kernel(n, m, plan, mlp_plan, fin, ret, mlp, wp, egrad, dwp, dwin, dwm, dwe, dwr, *vecs):
    clip = lax.axis_index("clip")
    wt = lax.axis_index("wt")
    held = egrad.shape[0]
    cap = ret.shape[1]
    row = lax.broadcasted_iota(jnp.int32, (held, cap), 0)
    col = lax.broadcasted_iota(jnp.int32, (held, cap), 1)
    own = None
    for dest in range(n):
        start = first_slot(dest, held, clip, n)
        stop = first_slot(dest + 1, held, clip, n)
        hot = ((row - start == col) & (row < stop)).astype(F32).astype(BF16)
        part = dg(hot, ret[dest], 1, 0)
        own = part if own is None else own + part
    egrad[...] = dg(own.astype(BF16), wp[...], 1, 1).astype(BF16)
    for name, r, slot, at in plan:
        piece = fin[slot, at : at + SEG].astype(F32)
        if name == "wp":
            dwp[r : r + SEG] = piece
        elif name != "vec":
            dwin[r : r + SEG, name * ROWS : (name + 1) * ROWS] = piece
        else:
            for z in range(m):
                @pl.when(wt == z)
                def _():
                    for i, ref in enumerate(vecs[:BIAS_E]):
                        w = ref.shape[0]
                        ref[...] = piece[i, z * w : (z + 1) * w]
                    w = vecs[BIAS_E].shape[0]
                    line = BIAS_E + z * w // ROWS
                    vecs[BIAS_E][...] = piece[line, z * w % ROWS : z * w % ROWS + w]
    for name, r, slot, at in mlp_plan:
        piece = mlp[slot, at : at + SEG].astype(F32)
        if name == "wm":
            dwm[r : r + SEG] = piece
        elif name == "wr":
            dwr[r : r + SEG] = piece
        else:
            dwe[r : r + SEG, name * ROWS : (name + 1) * ROWS] = piece


def finish(n, m, held, fin, ret, mlp, wp, f):
    e, d = wp.shape
    whole = pl.BlockSpec(memory_space=pltpu.VMEM)
    shape = jax.ShapeDtypeStruct
    plan = segments([("wp", e // m)] + [(j, d // m) for j in range(3)] + [("vec", SEG)], fin.shape[1])
    mlp_plan = segments(mlp_parts(d, f, m), mlp.shape[1])
    outs = [shape((held, e), BF16)] + [
        shape((r // m, c), F32) for r, c in ((e, d), (d, 3 * d), (d, d), (d, f), (f, d))
    ] + [shape((d // m,), F32)] * BIAS_E + [shape((f // m,), F32)]
    return pl.pallas_call(
        functools.partial(finish_kernel, n, m, plan, mlp_plan),
        in_specs=[whole] * 4,
        out_specs=[whole] * len(outs),
        out_shape=outs,
        compiler_params=params(),
        cost_estimate=cost(1e9, 4e6),
    )(fin, ret, mlp, wp)


def core(n, m, held, seen_len, seen, vis, wp, win, cols, be, wpack, upstream, reduce_mlp=None):
    d = cols.shape[0]
    pos = jnp.asarray(position_table(d))
    o, inv, e, stream, q, kt, v_rows = front(seen, vis, wp, cols, pos, win)
    share = up16(-(-wpack.shape[1] // n))
    dec, ga, do, dsum, mlp, vec = mid(n, m, share, o, inv, stream, upstream.reshape(2, L, d), wpack, be, cols)
    if reduce_mlp is not None:
        mlp = reduce_mlp(mlp)
    share = up16(-(-(wp.shape[0] // m + 3 * (d // m) + SEG) // n))
    gpack, gp = back(n, m, share, held, seen_len, e, v_rows, q, do, dsum, kt, stream, ga, seen, vis, win, cols, vec)
    return dec, mlp, gpack, gp


def per_device(encoded, visible_at, wp, token, gain1, shift1, win, bq, bv, wm, bm, gain2, shift2, we, be, wr, br, upstream):
    n = lax.axis_size("clip")
    m = lax.axis_size("wt")
    held = encoded.shape[0]
    seen_len = visible_at.shape[1]
    d = wp.shape[1]
    f = be.shape[0] * m
    local = pack_mlp(wm, we, wr)
    wpack = lax.all_gather(local, "wt", axis=0, tiled=True).reshape(m, local.shape[0], ROWS)
    vecs = (token, gain1, shift1, bq, bv, bm, gain2, shift2, br, be)
    seen, vis, wp_full, win_full, cols, be_col = enter(n, m, encoded, visible_at, wp, win, vecs)

    def reduce_mlp(mlp):
        mlp = lax.psum_scatter(mlp.reshape(-1, ROWS), "clip", scatter_dimension=0, tiled=True)
        return lax.psum_scatter(mlp, "wt", scatter_dimension=0, tiled=True)

    dec, mlp, gpack, gp = core(
        n, m, held, seen_len, seen, vis, wp_full, win_full, cols, be_col, wpack, upstream, reduce_mlp
    )
    fin, ret, mlp = leave(n, m, gpack, gp, mlp)
    egrad, dwp, dwin, dwm, dwe, dwr, *small = finish(n, m, held, fin, ret, mlp, wp_full, f)
    t, g1, s1, vq, vv, vm, g2, s2, vr, ve = small
    return (
        dec.reshape(2 * L, d), egrad, dwp, t, g1, s1, dwin, vq, vv, dwm, vm, g2, s2, dwe, ve, dwr, vr,
    )


def solution(mesh):
    both, wt = P(("clip", "wt"), None), P("wt")
    mat = P("wt", None)
    params_in = (mat, wt, wt, wt, mat, wt, wt, mat, wt, wt, wt, mat, wt, mat, wt)
    return jax.shard_map(
        per_device,
        mesh=mesh,
        in_specs=(both, both) + params_in + (both,),
        out_specs=(both, both) + params_in,
        check_vma=False,
    )
```

```python
import functools
import math

import jax
import jax.numpy as jnp
import numpy as np
from jax import lax
from jax.experimental import pallas as pl
from jax.experimental.pallas import tpu as pltpu
from jax.sharding import PartitionSpec as P

H = 6
HEAD = 64
L = 1568
LANES = 128
LP = -(-L // LANES) * LANES
KP = L
EPSILON = 1e-06
LOG2E = math.log2(math.e)
Q_SCALE = LOG2E / math.sqrt(HEAD)
ROOT_HALF = math.sqrt(0.5)
INV_ROOT_TWO_PI = 1.0 / math.sqrt(2.0 * math.pi)
SAFE_EXPONENT = 60.0
VMEM_LIMIT = 60 * 2**20
FFC = 512
Q_BLOCKS = ((0, 896), (896, LP - 896))
F32 = jnp.float32
BF16 = jnp.bfloat16


SEG = 16
ROWS = 384
MESH = pl.DeviceIdType.MESH
TOKEN, GAIN1, SHIFT1, BIAS_Q, BIAS_V, BIAS_M, GAIN2, SHIFT2, BIAS_R, BIAS_E = range(10)


def params(**kw):
    return pltpu.CompilerParams(vmem_limit_bytes=VMEM_LIMIT, **kw)


def cost(flops, moved=0):
    return pl.CostEstimate(flops=int(flops), bytes_accessed=int(moved), transcendentals=0)


def up16(x):
    return -(-x // SEG) * SEG


def segments(parts, share):
    out = []
    at = 0
    for name, rows in parts:
        for r in range(0, rows, SEG):
            out.append((name, r, at // share, at % share))
            at += SEG
    return out


def dg(a, b, ca, cb):
    return lax.dot_general(a, b, (((ca,), (cb,)), ((), ())), preferred_element_type=F32)


def position_table(width):
    places = np.arange(LP, dtype=np.float64)[None, :]
    columns = np.arange(width)
    exponent = (2 * (columns // 2)).astype(np.float64) / width
    angles = places / np.power(10000.0, exponent)[:, None]
    return np.where(columns[:, None] % 2 == 0, np.sin(angles), np.cos(angles)).astype(np.float32)


def norm_stats(x):
    center = x - jnp.mean(x, 0, keepdims=True)
    recip = lax.rsqrt(jnp.mean(center * center, 0, keepdims=True) + EPSILON)
    return center * recip, recip


def norm_back(e, scaled, recip, gain):
    lifted = e * gain
    return recip * (
        lifted
        - jnp.mean(lifted, 0, keepdims=True)
        - scaled * jnp.mean(lifted * scaled, 0, keepdims=True)
    )


def split3(x):
    hi = x.astype(BF16)
    rest = x - hi.astype(F32)
    mid = rest.astype(BF16)
    low = (rest - mid.astype(F32)).astype(BF16)
    return hi, mid, low


def aug_rows(x):
    hi, mid, low = split3(x)
    row = lax.broadcasted_iota(jnp.int32, (16, x.shape[1]), 0)
    zero = jnp.zeros((16, x.shape[1]), F32)
    out = jnp.where(row == 0, hi.astype(F32), zero)
    out = jnp.where(row == 1, mid.astype(F32), out)
    out = jnp.where(row == 2, low.astype(F32), out)
    return out.astype(BF16)


def one_hot(vis, width):
    place = lax.broadcasted_iota(jnp.int32, (vis.shape[0], width), 1).astype(F32)
    return (vis == place).astype(F32)


def first_slot(dest, held, clip, n):
    return (dest * held - clip + n - 1) // n


def interleave(rows, cols, clip, source, held, seen, seen_pad, n, by_row):
    first = (clip * held - source + n - 1) // n
    base = source + n * first - clip * held
    place = lax.broadcasted_iota(jnp.int32, (rows, cols), 0 if by_row else 1)
    slot = lax.broadcasted_iota(jnp.int32, (rows, cols), 1 if by_row else 0)
    second = place >= seen_pad
    local = jnp.where(second, place - (seen_pad - seen), place)
    good = (place < seen) | (second & (place < seen_pad + seen))
    return (good & (local == base + n * slot)).astype(F32).astype(BF16)


def greet(n, m, clip, wt):
    barrier = pltpu.get_barrier_semaphore()
    for k in range(1, n):
        pl.semaphore_signal(barrier, inc=1, device_id=(lax.rem(clip + k, n), wt), device_id_type=MESH)
    for k in range(1, m):
        pl.semaphore_signal(barrier, inc=1, device_id=(clip, lax.rem(wt + k, m)), device_id_type=MESH)
    pl.semaphore_wait(barrier, n + m - 2)


def remote(src, dst, send, recv, clip, wt):
    return pltpu.make_async_remote_copy(
        src_ref=src, dst_ref=dst, send_sem=send, recv_sem=recv, device_id=(clip, wt), device_id_type=MESH
    )


def enter_kernel(n, m, share, cap, seen_pad, *refs):
    (enc, vis_in, wp_in, win_in, *vecs) = refs[:14]
    (seen_out, vis_out, wp, win, cols, be) = refs[14:20]
    (pack, gath, out_rows, in_rows, vec_s, vis_s, zs, zr, bs, br, fs, fr, rs, rr) = refs[20:]
    clip = lax.axis_index("clip")
    wt = lax.axis_index("wt")
    held = enc.shape[0]
    seen = vis_in.shape[1]
    wp_rows = wp_in.shape[0]
    win_rows = win_in.shape[0]
    half = n // 2
    plan = segments(
        [("wp", wp_rows)] + [(j, win_rows) for j in range(3)] + [("vec", SEG)], share
    )
    vec_s[...] = jnp.zeros_like(vec_s)
    for i, ref in enumerate(vecs):
        vec_s[i, : ref.shape[0]] = ref[...].astype(F32)
    for name, r, slot, at in plan:
        if name == "wp":
            piece = wp_in[r : r + SEG]
        elif name == "vec":
            piece = vec_s[...].astype(BF16)
        else:
            piece = win_in[r : r + SEG, name * ROWS : (name + 1) * ROWS]
        pack[slot, at : at + SEG] = piece
    for at in range(len(plan) * SEG, n * share, SEG):
        pack[at // share, at % share : at % share + SEG] = jnp.zeros((SEG, ROWS), BF16)
    greet(n, m, clip, wt)

    sends = []
    partner = clip + 1 - 2 * lax.rem(clip, 2)
    for k in range(1, m):
        copy = remote(pack.at[clip], gath.at[clip, wt], zs.at[k], zr.at[k], clip, lax.rem(wt + k, m))
        copy.start()
        sends.append(copy)
    gath[clip, wt] = pack[clip]

    def spread(k):
        z = lax.rem(wt - k + m, m)
        for j in [*range(1, half), 0]:
            piece = gath.at[clip, z]
            dest = lax.rem(clip + 2 * j, n) if j else partner
            copy = remote(piece, piece, bs.at[j, k], br.at[j, k], dest, wt)
            copy.start()
            sends.append(copy)

    spread(0)

    rows_at = lax.broadcasted_iota(jnp.int32, (cap, held), 0)
    cols_at = lax.broadcasted_iota(jnp.int32, (cap, held), 1)
    row_sends = []
    for k in [*range(2, n, 2), *range(3, n, 2), 1, 0] if n > 2 else range(n - 1, -1, -1):
        dest = lax.rem(clip + k, n)
        hot = (rows_at + first_slot(dest, held, clip, n) == cols_at).astype(F32).astype(BF16)
        rows = dg(hot, enc[...], 1, 0).astype(BF16)
        if k == 0:
            in_rows[clip] = rows
        else:
            out_rows[k] = rows
            copy = remote(out_rows.at[k], in_rows.at[clip], rs.at[k], rr.at[k], dest, wt)
            copy.start()
            row_sends.append(copy)

    for k in range(1, m):
        source = lax.rem(wt - k + m, m)
        remote(pack.at[clip], gath.at[clip, source], zs.at[k], zr.at[k], clip, source).wait_recv()
        spread(k)

    vis_s[...] = jnp.full(vis_s.shape, -1.0, F32)
    vis_s[0:2, :seen] = vis_in[...].astype(F32)
    turned = vis_s[...].T
    for copy_at in range(2):
        vis_out[copy_at] = turned[:seen_pad, copy_at : copy_at + 1]

    for k in range(m):
        z = lax.rem(wt - k + m, m)
        for j in range(1, half):
            source = lax.rem(clip - 2 * j + n, n)
            piece = gath.at[source, z]
            remote(piece, piece, bs.at[j, k], br.at[j, k], source, wt).wait_recv()
            copy = remote(piece, piece, fs.at[j, k], fr.at[j, k], partner, wt)
            copy.start()
            sends.append(copy)

    for k in range(1, n):
        source = lax.rem(clip - k + n, n)
        remote(out_rows.at[k], in_rows.at[source], rs.at[k], rr.at[k], source, wt).wait_recv()
    total = None
    for source in range(n):
        hot = interleave(2 * seen_pad, cap, clip, source, held, seen, seen_pad, n, True)
        part = dg(hot, in_rows[source], 1, 0)
        total = part if total is None else total + part
    total = total.astype(BF16)
    seen_out[0] = total[:seen_pad]
    seen_out[1] = total[seen_pad:]

    for k in range(m):
        z = lax.rem(wt - k + m, m)
        for j in range(half):
            source = lax.rem(partner - 2 * j + n, n)
            piece = gath.at[source, z]
            sems = (fs.at[j, k], fr.at[j, k]) if j else (bs.at[0, k], br.at[0, k])
            remote(piece, piece, *sems, partner, wt).wait_recv()
    for z in range(m):
        for name, r, slot, at in plan:
            piece = gath[slot, z, at : at + SEG]
            if name == "wp":
                wp[z * wp_rows + r : z * wp_rows + r + SEG] = piece
            elif name == "vec":
                turned = piece.astype(F32).T
                small = vecs[0].shape[0]
                cols[z * small : (z + 1) * small] = turned[:small]
                large = vecs[BIAS_E].shape[0]
                be[z * large : (z + 1) * large] = turned[:large, BIAS_E : BIAS_E + 1]
            else:
                win[z * win_rows + r : z * win_rows + r + SEG, name * ROWS : (name + 1) * ROWS] = piece
    for copy in sends + row_sends:
        copy.wait_send()


def pack_kernel(wm, we, wr, out):
    rows = wm.shape[0]
    out[:rows] = wm[...]
    at = rows
    for j in range(we.shape[1] // ROWS):
        out[at : at + rows] = we[:, j * ROWS : (j + 1) * ROWS]
        at += rows
    out[at:] = wr[...]


def pack_mlp(wm, we, wr):
    rows = wm.shape[0] + wm.shape[0] * (we.shape[1] // ROWS) + wr.shape[0]
    whole = pl.BlockSpec(memory_space=pltpu.VMEM)
    return pl.pallas_call(
        pack_kernel,
        in_specs=[whole] * 3,
        out_specs=whole,
        out_shape=jax.ShapeDtypeStruct((rows, ROWS), BF16),
        compiler_params=params(),
        cost_estimate=cost(0, 1.3e6),
    )(wm, we, wr)


def enter(n, m, enc, vis, wp, win, vecs):
    held, e = enc.shape
    seen = vis.shape[1]
    seen_pad = up16(seen)
    d = wp.shape[1]
    cap = up16(-(-held // n))
    share = up16(-(-(wp.shape[0] + 3 * win.shape[0] + SEG) // n))
    whole = pl.BlockSpec(memory_space=pltpu.VMEM)
    shape = jax.ShapeDtypeStruct
    dma = pltpu.SemaphoreType.DMA
    ins = (enc, vis, wp, win, *vecs)
    return pl.pallas_call(
        functools.partial(enter_kernel, n, m, share, cap, seen_pad),
        in_specs=[whole] * len(ins),
        out_specs=[whole] * 6,
        out_shape=[
            shape((2, seen_pad, e), BF16), shape((2, seen_pad, 1), F32), shape((e, d), BF16),
            shape((d, 3 * d), BF16), shape((d, 16), F32), shape((vecs[BIAS_E].shape[0] * m, 1), F32),
        ],
        scratch_shapes=[
            pltpu.VMEM((n, share, ROWS), BF16), pltpu.VMEM((n, m, share, ROWS), BF16),
            pltpu.VMEM((n, cap, e), BF16), pltpu.VMEM((n, cap, e), BF16),
            pltpu.VMEM((SEG, ROWS), F32), pltpu.VMEM((8, 2 * LANES), F32),
            dma((m,)), dma((m,)), dma((n // 2, m)), dma((n // 2, m)), dma((n // 2, m)), dma((n // 2, m)),
            dma((n,)), dma((n,)),
        ],
        compiler_params=params(collective_id=0, has_side_effects=True),
        cost_estimate=cost(6e9, 4e6),
    )(*ins)


def front_kernel(seen, vis, wp, cols, pos, win, o_out, inv_out, e_out, stream_hbm, q_hbm, kt_hbm, v_hbm,
                 stream_s, q_s, k_s, v_s, k_rows, v_rows, v_aug, sems):
    copy = pl.program_id(0)
    step = pl.program_id(1)
    width = wp.shape[1]
    moves = [
        pltpu.make_async_copy(src, dst.at[copy], sems.at[i])
        for i, (src, dst) in enumerate(
            ((stream_s, stream_hbm), (q_s, q_hbm), (k_s, kt_hbm), (v_rows, v_hbm))
        )
    ]

    @pl.when(step == 0)
    def _():
        proj = dg(seen[0], wp[...], 1, 0).astype(BF16)
        hot = one_hot(vis[0], LP)
        covered = jnp.sum(hot, 0, keepdims=True)
        stream = dg(proj, hot.astype(BF16), 0, 0) + (1.0 - covered) * cols[:, TOKEN : TOKEN + 1] + pos[...]
        stream_s[...] = stream
        moves[0].start()
        scaled, _ = norm_stats(stream)
        normed = (scaled * cols[:, GAIN1 : GAIN1 + 1] + cols[:, SHIFT1 : SHIFT1 + 1]).astype(BF16)
        lane = lax.broadcasted_iota(jnp.int32, (L, LANES), 1)
        ones = (lane < HEAD + 3).astype(F32).astype(BF16)
        for part in (2, 1, 0):
            sl = slice(part * width, (part + 1) * width)
            mixed = dg(win[:, sl], normed, 0, 0)
            if part == 0:
                q_s[...] = ((mixed + cols[:, BIAS_Q : BIAS_Q + 1]) * Q_SCALE).astype(BF16)
                moves[1].start()
                continue
            if part == 2:
                mixed = mixed + cols[:, BIAS_V : BIAS_V + 1]
            mixed = mixed.astype(BF16)
            dst = k_s if part == 1 else v_s
            dst[:, :L] = mixed[:, :L]
            dst[:, L:] = jnp.zeros((width, LP - L), BF16)
            rows = k_rows if part == 1 else v_rows
            for h in range(H):
                if part == 2:
                    rows[h] = ones
                rows[h, :, :HEAD] = mixed[h * HEAD : (h + 1) * HEAD].T[:L]
            moves[2 if part == 1 else 3].start()

    @pl.when(step > 0)
    def _():
        head = pl.ds(pl.multiple_of((step - 1) * HEAD, HEAD), HEAD)
        row = lax.broadcasted_iota(jnp.int32, (16, L), 0)
        v_aug[:HEAD] = v_s[head, :L]
        v_aug[HEAD:] = (row == 0).astype(F32).astype(BF16)
        qf = q_s[head, :].astype(F32)
        kf = k_s[head, :].astype(F32)
        bound = jnp.max(jnp.sum(qf * qf, 0, keepdims=True)) * jnp.max(jnp.sum(kf * kf, 0, keepdims=True))
        safe = bound <= SAFE_EXPONENT * SAFE_EXPONENT

        def run(shift):
            for start, size in Q_BLOCKS:
                sl = slice(start, start + size)
                s = dg(k_rows[step - 1, :, :HEAD], q_s[head, sl], 1, 0)
                if shift:
                    s = s - jnp.max(s, 0, keepdims=True)
                e = jnp.exp2(s).astype(BF16)
                e_out[0, 0, :, sl] = e
                o = dg(v_aug[...], e, 1, 0)
                inv = 1.0 / o[HEAD : HEAD + 1]
                o_out[0, :, sl] = o[:HEAD] * inv
                inv_out[0, 0, :, sl] = inv

        pl.when(safe)(lambda: run(False))
        pl.when(jnp.logical_not(safe))(lambda: run(True))

    @pl.when(step == H)
    def _():
        for move in moves:
            move.wait()


def front(seen, vis, wp, cols, pos, win):
    _, a, e = seen.shape
    d = wp.shape[1]
    const = lambda *s: pl.BlockSpec(s, lambda c, i: (0,) * len(s), pipeline_mode=pl.Buffered(1))
    lead = lambda *s: pl.BlockSpec((1,) + s, lambda c, i: (c,) + (0,) * len(s))
    head = lambda c, i: (c, jnp.maximum(i - 1, 0), 0)
    wide = lambda c, i: (c, jnp.maximum(i - 1, 0), 0, 0)
    any_ = pl.BlockSpec(memory_space=pl.ANY)
    shape = jax.ShapeDtypeStruct
    vm = pltpu.VMEM
    return pl.pallas_call(
        front_kernel,
        grid=(2, H + 1),
        in_specs=[lead(a, e), lead(a, 1), const(e, d), const(d, 16), const(d, LP), const(d, 3 * d)],
        out_specs=[
            pl.BlockSpec((1, HEAD, LP), head), pl.BlockSpec((1, 1, 1, LP), wide), pl.BlockSpec((1, 1, L, LP), wide),
            any_, any_, any_, any_,
        ],
        out_shape=[
            shape((2, d, LP), F32), shape((2, H, 1, LP), F32), shape((2, H, L, LP), BF16),
            shape((2, d, LP), F32), shape((2, d, LP), BF16), shape((2, d, LP), BF16), shape((2, H, L, LANES), BF16),
        ],
        scratch_shapes=[
            vm((d, LP), F32), vm((d, LP), BF16), vm((d, LP), BF16), vm((d, LP), BF16),
            vm((H, L, LANES), BF16), vm((H, L, LANES), BF16), vm((HEAD + 16, L), BF16),
            pltpu.SemaphoreType.DMA((4,)),
        ],
        compiler_params=params(),
        cost_estimate=cost(4e10, 8e7),
    )(seen, vis, wp, cols, pos, win)


def mlp_parts(d, f, m):
    return [("wm", d // m)] + [(j, d // m) for j in range(f // ROWS)] + [("wr", f // m)]


def mid_kernel(n, m, share, o, inv, stream, up, wpack, be, cols,
               dec, ga_out, do_out, dsum_out, gpack, vec_out,
               wm, we, wr, dwm, dwe, dwr, dvec, dbe, drb, stats, n2, act_s, gl_s, g_s):
    copy = pl.program_id(0)
    ff = pl.program_id(1)
    last = pl.num_programs(1) - 1
    d = wm.shape[0]
    f = wr.shape[0]
    parts = mlp_parts(d, f, m)

    @pl.when((copy == 0) & (ff == 0))
    def _():
        for z in range(m):
            at = 0
            for name, rows in parts:
                piece = wpack[z, at : at + rows]
                dst = slice(z * rows, (z + 1) * rows)
                if name == "wm":
                    wm[dst] = piece
                elif name == "wr":
                    wr[dst] = piece
                else:
                    we[dst, name * ROWS : (name + 1) * ROWS] = piece
                at += rows
        dwm[...] = jnp.zeros_like(dwm)
        dwe[...] = jnp.zeros_like(dwe)
        dwr[...] = jnp.zeros_like(dwr)
        dvec[...] = jnp.zeros_like(dvec)
        dbe[...] = jnp.zeros_like(dbe)
        drb[...] = jnp.zeros_like(drb)

    @pl.when(ff == 0)
    def _():
        ctx = o[0].astype(BF16)
        x = stream[0] + dg(wm[...], ctx, 0, 0) + cols[:, BIAS_M : BIAS_M + 1]
        ga_out[0] = x
        mean = jnp.mean(x, 0, keepdims=True)
        center = x - mean
        recip = lax.rsqrt(jnp.mean(center * center, 0, keepdims=True) + EPSILON)
        stats[0:1] = mean
        stats[1:2] = recip
        n2[:d] = (center * recip * cols[:, GAIN2 : GAIN2 + 1] + cols[:, SHIFT2 : SHIFT2 + 1]).astype(BF16)
        row = lax.broadcasted_iota(jnp.int32, (16, LP), 0)
        n2[d:] = (row == 0).astype(F32).astype(BF16)
        g = (up[0].astype(F32) * 0.5).astype(BF16)
        g_s[:L] = g
        g_s[L:] = jnp.zeros((LP - L, d), BF16)
        drb[...] += dg(jnp.ones((8, L), BF16), g, 1, 0)

    rows = pl.ds(pl.multiple_of(ff * FFC, FFC), FFC)
    g = g_s[...]
    lifted = dg(we[:, rows], n2[:d], 0, 0) + be[rows, :]
    bell = jnp.exp(-0.5 * lifted * lifted)
    cdf = 0.5 * (1.0 + lax.erf(lifted * ROOT_HALF))
    act = (lifted * cdf).astype(BF16)
    slope = cdf + lifted * bell * INV_ROOT_TWO_PI
    gl = (dg(wr[rows, :], g, 1, 1) * slope).astype(BF16)
    act_s[rows, :] = act
    gl_s[rows, :] = gl

    @pl.when(ff == last)
    def _():
        x = ga_out[0]
        dwr[...] += dg(act_s[...], g_s[...], 1, 0)
        grad = dg(n2[...], gl_s[...], 1, 1)
        dwe[...] += grad[:d]
        dbe[...] += grad[d : d + 8]
        out = x + dg(wr[...], act_s[...], 0, 0) + cols[:, BIAS_R : BIAS_R + 1]
        dec[0] = out.astype(BF16).T[:L]
        scaled = (x - stats[0:1]) * stats[1:2]
        e = dg(we[...], gl_s[...], 1, 0)
        dvec[:, 0:1] += jnp.sum(e * scaled, 1, keepdims=True)
        dvec[:, 1:2] += jnp.sum(e, 1, keepdims=True)
        back = norm_back(e, scaled, stats[1:2], cols[:, GAIN2 : GAIN2 + 1])
        ga = g_s[...].T.astype(F32) + back
        ga_out[0] = ga
        gm = ga.astype(BF16)
        dvec[:, 2:3] += jnp.sum(gm.astype(F32), 1, keepdims=True)
        ctx = o[0]
        dwm[...] += dg(ctx.astype(BF16), gm, 1, 1)
        do = dg(wm[...], gm, 1, 0)
        for h in range(H):
            hs = slice(h * HEAD, (h + 1) * HEAD)
            part = (do[hs] * inv[0, h]).astype(BF16)
            do_out[0, hs] = part
            dsum_out[0, h] = aug_rows(-jnp.sum(part.astype(F32) * ctx[hs], 0, keepdims=True))

    @pl.when((ff == last) & (copy == 1))
    def _():
        plan = segments(parts, share)
        for z in range(m):
            for name, r, slot, at in plan:
                if name == "wm":
                    piece = dwm[z * (d // m) + r : z * (d // m) + r + SEG]
                elif name == "wr":
                    piece = dwr[z * (f // m) + r : z * (f // m) + r + SEG]
                else:
                    piece = dwe[z * (d // m) + r : z * (d // m) + r + SEG, name * ROWS : (name + 1) * ROWS]
                gpack[slot, z, at : at + SEG] = piece.astype(BF16)
            for at in range(len(plan) * SEG, n * share, SEG):
                gpack[at // share, z, at % share : at % share + SEG] = jnp.zeros((SEG, ROWS), BF16)
        turned = dvec[...].T
        vec_out[...] = jnp.zeros_like(vec_out)
        vec_out[BIAS_M : BIAS_M + 1] = turned[2:3]
        vec_out[GAIN2 : GAIN2 + 1] = turned[0:1]
        vec_out[SHIFT2 : SHIFT2 + 1] = turned[1:2]
        vec_out[BIAS_R : BIAS_R + 1] = drb[0:1]
        for j in range(f // ROWS):
            vec_out[BIAS_E + j : BIAS_E + j + 1] = dbe[0:1, j * ROWS : (j + 1) * ROWS]


def mid(n, m, share, o, inv, stream, up, wpack, be, cols):
    d = cols.shape[0]
    f = be.shape[0]
    once = pl.Buffered(1)
    const = lambda *s: pl.BlockSpec(s, lambda c, k: (0,) * len(s), pipeline_mode=once)
    lead = lambda *s: pl.BlockSpec((1,) + s, lambda c, k: (c,) + (0,) * len(s))
    shape = jax.ShapeDtypeStruct
    vm = pltpu.VMEM
    return pl.pallas_call(
        functools.partial(mid_kernel, n, m, share),
        grid=(2, f // FFC),
        in_specs=[lead(d, LP), lead(H, 1, LP), lead(d, LP), lead(L, d), const(*wpack.shape), const(f, 1), const(d, 16)],
        out_specs=[
            lead(L, d), lead(d, LP), lead(d, LP), lead(H, 16, LP), const(n, m, share, ROWS), const(16, d),
        ],
        out_shape=[
            shape((2, L, d), BF16), shape((2, d, LP), F32), shape((2, d, LP), BF16), shape((2, H, 16, LP), BF16),
            shape((n, m, share, ROWS), BF16), shape((16, d), F32),
        ],
        scratch_shapes=[
            vm((d, d), BF16), vm((d, f), BF16), vm((f, d), BF16),
            vm((d, d), F32), vm((d, f), F32), vm((f, d), F32), vm((d, LANES), F32), vm((8, f), F32), vm((8, d), F32),
            vm((8, LP), F32), vm((d + 16, LP), BF16),
            vm((f, LP), BF16), vm((f, LP), BF16), vm((LP, d), BF16),
        ],
        compiler_params=params(),
        cost_estimate=cost(5e10, 4e7),
    )(o, inv, stream, up, wpack, be, cols)


def back_kernel(n, m, share, held, seen_len, e, v_rows, q, do, dsum, kt, stream, ga, seen, vis, win, cols, vec_in,
                gpack, gp_out, do_aug, gm, kept, qtmp, dwin, dbin, dvec, dwp, n1, gp_s):
    copy = pl.program_id(0)
    step = pl.program_id(1)
    clip = lax.axis_index("clip")
    d = win.shape[0]
    e_width = dwp.shape[0]
    seen_pad = seen.shape[1]
    cap = gp_out.shape[1]

    @pl.when((copy == 0) & (step == 0))
    def _():
        dwin[...] = jnp.zeros_like(dwin)
        dbin[...] = jnp.zeros_like(dbin)
        dvec[...] = jnp.zeros_like(dvec)
        dwp[...] = jnp.zeros_like(dwp)
        do_aug[HEAD + 16 :] = jnp.zeros((LANES - HEAD - 16, LP), BF16)
        kept[...] = jnp.zeros_like(kept)

    @pl.when(step < H)
    def _():
        head = pl.ds(pl.multiple_of(step * HEAD, HEAD), HEAD)
        do_aug[:HEAD] = do[0]
        do_aug[HEAD : HEAD + 16] = dsum[0, 0]
        k_sum = None
        v_sum = None
        for start, size in Q_BLOCKS:
            sl = slice(start, start + size)
            p = e[0, 0, :, sl]
            dp = dg(v_rows[0, 0], do_aug[:, sl], 1, 0)
            ds = (p.astype(F32) * dp).astype(BF16)
            v_part = dg(do_aug[:HEAD, sl], p, 1, 1)
            k_part = dg(q[0, :, sl], ds, 1, 1)
            v_sum = v_part if v_sum is None else v_sum + v_part
            k_sum = k_part if k_sum is None else k_sum + k_part
            qtmp[:, sl] = (dg(kt[0, :, :L], ds, 1, 0) * (1.0 / math.sqrt(HEAD))).astype(BF16)
        gm[pl.ds(pl.multiple_of(step * HEAD, HEAD), HEAD), :] = qtmp[...]
        for part, total in ((1, k_sum * (1.0 / LOG2E)), (2, v_sum)):
            kept[:, :L] = total.astype(BF16)
            gm[pl.ds(pl.multiple_of(part * d + step * HEAD, HEAD), HEAD), :] = kept[...]

    @pl.when(step == H)
    def _():
        x = stream[0]
        scaled, recip = norm_stats(x)
        n1[:d] = (scaled * cols[:, GAIN1 : GAIN1 + 1] + cols[:, SHIFT1 : SHIFT1 + 1]).astype(BF16)
        row = lax.broadcasted_iota(jnp.int32, (16, LP), 0)
        n1[d:] = (row == 0).astype(F32).astype(BF16)
        e = None
        for part in range(3):
            sl = slice(part * d, (part + 1) * d)
            grad = dg(n1[...], gm[sl], 1, 1)
            dwin[:, sl] += grad[:d]
            dbin[:, sl] += grad[d : d + 8]
            term = dg(win[:, sl], gm[sl], 1, 0)
            e = term if e is None else e + term
        dvec[:, 0:1] += jnp.sum(e * scaled, 1, keepdims=True)
        dvec[:, 1:2] += jnp.sum(e, 1, keepdims=True)
        gs = ga[0] + norm_back(e, scaled, recip, cols[:, GAIN1 : GAIN1 + 1])
        hot = one_hot(vis[0], LP)
        token = lax.broadcasted_iota(jnp.int32, (1, LP), 1)
        masked = jnp.where(token < L, 1.0 - jnp.sum(hot, 0, keepdims=True), 0.0)
        dvec[:, 2:3] += jnp.sum(gs * masked, 1, keepdims=True)
        gp = dg(hot.astype(BF16), gs.astype(BF16), 1, 1).astype(BF16)
        gp_s[pl.ds(pl.multiple_of(copy * seen_pad, SEG), seen_pad), :] = gp
        dwp[...] += dg(seen[0], gp, 0, 0)

    @pl.when((copy == 1) & (step == H))
    def _():
        for source in range(n):
            pick = interleave(cap, 2 * seen_pad, clip, source, held, seen_len, seen_pad, n, False)
            gp_out[source] = dg(pick, gp_s[...], 1, 0).astype(BF16)
        turned = dvec[...].T
        row = lax.broadcasted_iota(jnp.int32, (16, d), 0)
        vec = vec_in[...]
        vec = jnp.where(row == TOKEN, turned[2:3], vec)
        vec = jnp.where(row == GAIN1, turned[0:1], vec)
        vec = jnp.where(row == SHIFT1, turned[1:2], vec)
        vec = jnp.where(row == BIAS_Q, dbin[0:1, :d], vec)
        vec = jnp.where(row == BIAS_V, dbin[0:1, 2 * d :], vec).astype(BF16)
        wp_rows = e_width // m
        win_rows = d // m
        plan = segments([("wp", wp_rows)] + [(j, win_rows) for j in range(3)] + [("vec", SEG)], share)
        for z in range(m):
            for name, r, slot, at in plan:
                if name == "wp":
                    piece = dwp[z * wp_rows + r : z * wp_rows + r + SEG].astype(BF16)
                elif name == "vec":
                    piece = vec
                else:
                    piece = dwin[
                        z * win_rows + r : z * win_rows + r + SEG, name * ROWS : (name + 1) * ROWS
                    ].astype(BF16)
                gpack[slot, z, at : at + SEG] = piece
            for at in range(len(plan) * SEG, n * share, SEG):
                gpack[at // share, z, at % share : at % share + SEG] = jnp.zeros((SEG, ROWS), BF16)


def back(n, m, share, held, seen_len, e, v_rows, q, do, dsum, kt, stream, ga, seen, vis, win, cols, vec_in):
    _, a, width = seen.shape
    d = win.shape[0]
    cap = up16(-(-held // n))
    const = lambda *s: pl.BlockSpec(s, lambda c, i: (0,) * len(s), pipeline_mode=pl.Buffered(1))
    lead = lambda *s: pl.BlockSpec((1,) + s, lambda c, i: (c,) + (0,) * len(s))
    head = lambda c, i: (c, jnp.minimum(i, H - 1), 0)
    wide = lambda c, i: (c, jnp.minimum(i, H - 1), 0, 0)
    shape = jax.ShapeDtypeStruct
    vm = pltpu.VMEM
    return pl.pallas_call(
        functools.partial(back_kernel, n, m, share, held, seen_len),
        grid=(2, H + 1),
        in_specs=[
            pl.BlockSpec((1, 1, L, LP), wide), pl.BlockSpec((1, 1, L, LANES), wide), pl.BlockSpec((1, HEAD, LP), head),
            pl.BlockSpec((1, HEAD, LP), head), pl.BlockSpec((1, 1, 16, LP), wide), pl.BlockSpec((1, HEAD, LP), head),
            lead(d, LP), lead(d, LP), lead(a, width), lead(a, 1), const(d, 3 * d), const(d, 16), const(16, d),
        ],
        out_specs=[const(n, m, share, ROWS), const(n, cap, d)],
        out_shape=[shape((n, m, share, ROWS), BF16), shape((n, cap, d), BF16)],
        scratch_shapes=[
            vm((LANES, LP), BF16), vm((3 * d, LP), BF16), vm((HEAD, LP), BF16), vm((HEAD, LP), BF16),
            vm((d, 3 * d), F32), vm((8, 3 * d), F32), vm((d, LANES), F32), vm((width, d), F32),
            vm((d + 16, LP), BF16), vm((2 * a, d), BF16),
        ],
        compiler_params=params(),
        cost_estimate=cost(1e11, 1e8),
    )(e, v_rows, q, do, dsum, kt, stream, ga, seen, vis, win, cols, vec_in)


def leave_kernel(n, m, gpack, gp, mlp, fin, ret, mlp_out, a1, a2s, a2r, tot, tot_b, brecv, fin_s, ret_s, mlp_s, mlp_z,
                 gs, gr, s1, r1, s2, r2, sb, rb, sc, rc, sm, rm, sf, rf, sz, rz):
    clip = lax.axis_index("clip")
    wt = lax.axis_index("wt")
    half = n // 2
    core = lax.rem(clip, 2)
    chip = clip // 2
    partner = clip + 1 - 2 * core
    greet(n, m, clip, wt)
    sends = []

    def send(*args):
        copy = remote(*args)
        copy.start()
        sends.append(copy)

    order = [*range(1, half), 0]
    turns = [*range(1, m), 0]
    for k in range(1, m):
        zz = lax.rem(wt + k, m)
        send(mlp.at[zz], mlp_z.at[k], sz.at[k], rz.at[k], clip, zz)
    for k in turns:
        zz = lax.rem(wt + k, m)
        for j in order:
            spot = lax.rem(chip + j, half)
            send(gpack.at[2 * spot + 1 - core, zz], a1.at[j, k], s1.at[j, k], r1.at[j, k], partner, wt)
    for k in turns:
        zz = lax.rem(wt + k, m)
        for j in order:
            mine = 2 * lax.rem(chip + j, half) + core
            remote(gpack.at[mine, zz], a1.at[j, k], s1.at[j, k], r1.at[j, k], partner, wt).wait_recv()
            both = gpack[mine, zz].astype(F32) + a1[j, k].astype(F32)
            if j == 0:
                tot[k] = both
            else:
                a2s[j, k] = both.astype(BF16)
                send(a2s.at[j, k], a2r.at[j, k], s2.at[j, k], r2.at[j, k], mine, wt)
    for k in [*range(2, n, 2), *range(1, n, 2)]:
        dest = lax.rem(clip + k, n)
        send(gp.at[dest], ret_s.at[clip], gs.at[k], gr.at[k], dest, wt)
    ret_s[clip] = gp[clip]
    total = mlp[wt].astype(F32)
    for k in range(1, m):
        source = lax.rem(wt - k + m, m)
        remote(mlp.at[source], mlp_z.at[k], sz.at[k], rz.at[k], clip, source).wait_recv()
        total = total + mlp_z[k].astype(F32)
    mlp_s[clip] = total.astype(BF16)
    for j in order:
        dest = lax.rem(clip + 2 * j, n) if j else partner
        send(mlp_s.at[clip], mlp_s.at[clip], sm.at[j], rm.at[j], dest, wt)
    for k in turns:
        zz = lax.rem(wt + k, m)
        total = tot[k]
        for j in range(1, half):
            source = lax.rem(clip - 2 * j + n, n)
            remote(a2s.at[j, k], a2r.at[j, k], s2.at[j, k], r2.at[j, k], source, wt).wait_recv()
            total = total + a2r[j, k].astype(F32)
        if k:
            tot_b[k] = total.astype(BF16)
            send(tot_b.at[k], brecv.at[k], sb.at[k], rb.at[k], clip, zz)
    for k in range(1, m):
        source = lax.rem(wt - k + m, m)
        remote(tot_b.at[k], brecv.at[k], sb.at[k], rb.at[k], clip, source).wait_recv()
        total = total + brecv[k].astype(F32)
    fin_s[clip] = total.astype(BF16)
    for k in [*range(2, n, 2), *range(1, n, 2)]:
        send(fin_s.at[clip], fin_s.at[clip], sc.at[k], rc.at[k], lax.rem(clip + k, n), wt)
    for j in range(1, half):
        source = lax.rem(clip - 2 * j + n, n)
        remote(mlp_s.at[source], mlp_s.at[source], sm.at[j], rm.at[j], source, wt).wait_recv()
        send(mlp_s.at[source], mlp_s.at[source], sf.at[j], rf.at[j], partner, wt)
    for k in range(1, n):
        source = lax.rem(clip - k + n, n)
        remote(gp.at[source], ret_s.at[source], gs.at[k], gr.at[k], source, wt).wait_recv()
    ret[...] = ret_s[...]
    for j in range(half):
        source = lax.rem(partner - 2 * j + n, n)
        sems = (sf.at[j], rf.at[j]) if j else (sm.at[0], rm.at[0])
        remote(mlp_s.at[source], mlp_s.at[source], *sems, partner, wt).wait_recv()
    mlp_out[...] = mlp_s[...]
    for k in range(1, n):
        source = lax.rem(clip - k + n, n)
        remote(fin_s.at[source], fin_s.at[source], sc.at[k], rc.at[k], source, wt).wait_recv()
    fin[...] = fin_s[...]
    for copy in sends:
        copy.wait_send()


def leave(n, m, gpack, gp, mlp):
    _, _, share, _ = gpack.shape
    _, cap, d = gp.shape
    whole = pl.BlockSpec(memory_space=pltpu.VMEM)
    shape = jax.ShapeDtypeStruct
    vm = pltpu.VMEM
    dma = pltpu.SemaphoreType.DMA
    half = n // 2
    return pl.pallas_call(
        functools.partial(leave_kernel, n, m),
        in_specs=[whole] * 3,
        out_specs=[whole] * 3,
        out_shape=[shape((n, share, ROWS), BF16), shape((n, cap, d), BF16), shape((n,) + mlp.shape[1:], BF16)],
        scratch_shapes=[
            vm((half, m, share, ROWS), BF16), vm((half, m, share, ROWS), BF16), vm((half, m, share, ROWS), BF16),
            vm((m, share, ROWS), F32), vm((m, share, ROWS), BF16), vm((m, share, ROWS), BF16),
            vm((n, share, ROWS), BF16), vm((n, cap, d), BF16), vm((n,) + mlp.shape[1:], BF16), vm(mlp.shape, BF16),
            dma((n,)), dma((n,)), dma((half, m)), dma((half, m)), dma((half, m)), dma((half, m)),
            dma((m,)), dma((m,)), dma((n,)), dma((n,)),
            dma((half,)), dma((half,)), dma((half,)), dma((half,)), dma((m,)), dma((m,)),
        ],
        compiler_params=params(collective_id=1, has_side_effects=True),
        cost_estimate=cost(4e9, 4e6),
    )(gpack, gp, mlp)


def finish_kernel(n, m, plan, mlp_plan, fin, ret, mlp, wp, egrad, dwp, dwin, dwm, dwe, dwr, *vecs):
    clip = lax.axis_index("clip")
    wt = lax.axis_index("wt")
    held = egrad.shape[0]
    cap = ret.shape[1]
    row = lax.broadcasted_iota(jnp.int32, (held, cap), 0)
    col = lax.broadcasted_iota(jnp.int32, (held, cap), 1)
    own = None
    for dest in range(n):
        start = first_slot(dest, held, clip, n)
        stop = first_slot(dest + 1, held, clip, n)
        hot = ((row - start == col) & (row < stop)).astype(F32).astype(BF16)
        part = dg(hot, ret[dest], 1, 0)
        own = part if own is None else own + part
    egrad[...] = dg(own.astype(BF16), wp[...], 1, 1).astype(BF16)
    for name, r, slot, at in plan:
        piece = fin[slot, at : at + SEG].astype(F32)
        if name == "wp":
            dwp[r : r + SEG] = piece
        elif name != "vec":
            dwin[r : r + SEG, name * ROWS : (name + 1) * ROWS] = piece
        else:
            for z in range(m):
                @pl.when(wt == z)
                def _():
                    for i, ref in enumerate(vecs[:BIAS_E]):
                        w = ref.shape[0]
                        ref[...] = piece[i, z * w : (z + 1) * w]
                    w = vecs[BIAS_E].shape[0]
                    line = BIAS_E + z * w // ROWS
                    vecs[BIAS_E][...] = piece[line, z * w % ROWS : z * w % ROWS + w]
    for name, r, slot, at in mlp_plan:
        piece = mlp[slot, at : at + SEG].astype(F32)
        if name == "wm":
            dwm[r : r + SEG] = piece
        elif name == "wr":
            dwr[r : r + SEG] = piece
        else:
            dwe[r : r + SEG, name * ROWS : (name + 1) * ROWS] = piece


def finish(n, m, held, fin, ret, mlp, wp, f):
    e, d = wp.shape
    whole = pl.BlockSpec(memory_space=pltpu.VMEM)
    shape = jax.ShapeDtypeStruct
    plan = segments([("wp", e // m)] + [(j, d // m) for j in range(3)] + [("vec", SEG)], fin.shape[1])
    mlp_plan = segments(mlp_parts(d, f, m), mlp.shape[1])
    outs = [shape((held, e), BF16)] + [
        shape((r // m, c), F32) for r, c in ((e, d), (d, 3 * d), (d, d), (d, f), (f, d))
    ] + [shape((d // m,), F32)] * BIAS_E + [shape((f // m,), F32)]
    return pl.pallas_call(
        functools.partial(finish_kernel, n, m, plan, mlp_plan),
        in_specs=[whole] * 4,
        out_specs=[whole] * len(outs),
        out_shape=outs,
        compiler_params=params(),
        cost_estimate=cost(1e9, 4e6),
    )(fin, ret, mlp, wp)


def core(n, m, held, seen_len, seen, vis, wp, win, cols, be, wpack, upstream, reduce_mlp=None):
    d = cols.shape[0]
    pos = jnp.asarray(position_table(d))
    o, inv, e, stream, q, kt, v_rows = front(seen, vis, wp, cols, pos, win)
    share = up16(-(-wpack.shape[1] // n))
    dec, ga, do, dsum, mlp, vec = mid(n, m, share, o, inv, stream, upstream.reshape(2, L, d), wpack, be, cols)
    if reduce_mlp is not None:
        mlp = reduce_mlp(mlp)
    share = up16(-(-(wp.shape[0] // m + 3 * (d // m) + SEG) // n))
    gpack, gp = back(n, m, share, held, seen_len, e, v_rows, q, do, dsum, kt, stream, ga, seen, vis, win, cols, vec)
    return dec, mlp, gpack, gp


def per_device(encoded, visible_at, wp, token, gain1, shift1, win, bq, bv, wm, bm, gain2, shift2, we, be, wr, br, upstream):
    n = lax.axis_size("clip")
    m = lax.axis_size("wt")
    held = encoded.shape[0]
    seen_len = visible_at.shape[1]
    d = wp.shape[1]
    f = be.shape[0] * m
    local = pack_mlp(wm, we, wr)
    wpack = lax.all_gather(local, "wt", axis=0, tiled=True).reshape(m, local.shape[0], ROWS)
    vecs = (token, gain1, shift1, bq, bv, bm, gain2, shift2, br, be)
    seen, vis, wp_full, win_full, cols, be_col = enter(n, m, encoded, visible_at, wp, win, vecs)

    def reduce_mlp(mlp):
        part = lax.psum_scatter(mlp.reshape(-1, ROWS), "clip", scatter_dimension=0, tiled=True)
        return part.reshape(mlp.shape[1:])

    dec, mlp, gpack, gp = core(
        n, m, held, seen_len, seen, vis, wp_full, win_full, cols, be_col, wpack, upstream, reduce_mlp
    )
    fin, ret, mlp = leave(n, m, gpack, gp, mlp)
    egrad, dwp, dwin, dwm, dwe, dwr, *small = finish(n, m, held, fin, ret, mlp, wp_full, f)
    t, g1, s1, vq, vv, vm, g2, s2, vr, ve = small
    return (
        dec.reshape(2 * L, d), egrad, dwp, t, g1, s1, dwin, vq, vv, dwm, vm, g2, s2, dwe, ve, dwr, vr,
    )


def solution(mesh):
    both, wt = P(("clip", "wt"), None), P("wt")
    mat = P("wt", None)
    params_in = (mat, wt, wt, wt, mat, wt, wt, mat, wt, wt, wt, mat, wt, mat, wt)
    return jax.shard_map(
        per_device,
        mesh=mesh,
        in_specs=(both, both) + params_in + (both,),
        out_specs=(both, both) + params_in,
        check_vma=False,
    )
```

```python
import functools
import math

import jax
import jax.numpy as jnp
import numpy as np
from jax import lax
from jax.experimental import pallas as pl
from jax.experimental.pallas import tpu as pltpu
from jax.sharding import PartitionSpec as P

H = 6
HEAD = 64
L = 1568
LANES = 128
LP = -(-L // LANES) * LANES
KP = L
EPSILON = 1e-06
LOG2E = math.log2(math.e)
Q_SCALE = LOG2E / math.sqrt(HEAD)
ROOT_HALF = math.sqrt(0.5)
INV_ROOT_TWO_PI = 1.0 / math.sqrt(2.0 * math.pi)
SAFE_EXPONENT = 60.0
VMEM_LIMIT = 60 * 2**20
FFC = 512
Q_BLOCKS = ((0, 896), (896, LP - 896))
FRONT_BLOCKS = ((0, 1024), (1024, LP - 1024))
F32 = jnp.float32
BF16 = jnp.bfloat16


SEG = 16
ROWS = 384
MESH = pl.DeviceIdType.MESH
TOKEN, GAIN1, SHIFT1, BIAS_Q, BIAS_V, BIAS_M, GAIN2, SHIFT2, BIAS_R, BIAS_E = range(10)


def params(**kw):
    return pltpu.CompilerParams(vmem_limit_bytes=VMEM_LIMIT, **kw)


def cost(flops, moved=0):
    return pl.CostEstimate(flops=int(flops), bytes_accessed=int(moved), transcendentals=0)


def up16(x):
    return -(-x // SEG) * SEG


def segments(parts, share):
    out = []
    at = 0
    for name, rows in parts:
        for r in range(0, rows, SEG):
            out.append((name, r, at // share, at % share))
            at += SEG
    return out


def dg(a, b, ca, cb):
    return lax.dot_general(a, b, (((ca,), (cb,)), ((), ())), preferred_element_type=F32)


def position_table(width):
    places = np.arange(LP, dtype=np.float64)[None, :]
    columns = np.arange(width)
    exponent = (2 * (columns // 2)).astype(np.float64) / width
    angles = places / np.power(10000.0, exponent)[:, None]
    return np.where(columns[:, None] % 2 == 0, np.sin(angles), np.cos(angles)).astype(np.float32)


def norm_stats(x):
    center = x - jnp.mean(x, 0, keepdims=True)
    recip = lax.rsqrt(jnp.mean(center * center, 0, keepdims=True) + EPSILON)
    return center * recip, recip


def norm_back(e, scaled, recip, gain):
    lifted = e * gain
    return recip * (
        lifted
        - jnp.mean(lifted, 0, keepdims=True)
        - scaled * jnp.mean(lifted * scaled, 0, keepdims=True)
    )


def split3(x):
    hi = x.astype(BF16)
    rest = x - hi.astype(F32)
    mid = rest.astype(BF16)
    low = (rest - mid.astype(F32)).astype(BF16)
    return hi, mid, low


def aug_rows(x):
    hi, mid, low = split3(x)
    row = lax.broadcasted_iota(jnp.int32, (16, x.shape[1]), 0)
    zero = jnp.zeros((16, x.shape[1]), F32)
    out = jnp.where(row == 0, hi.astype(F32), zero)
    out = jnp.where(row == 1, mid.astype(F32), out)
    out = jnp.where(row == 2, low.astype(F32), out)
    return out.astype(BF16)


def one_hot(vis, width):
    place = lax.broadcasted_iota(jnp.int32, (vis.shape[0], width), 1).astype(F32)
    return (vis == place).astype(F32)


def first_slot(dest, held, clip, n):
    return (dest * held - clip + n - 1) // n


def interleave(rows, cols, clip, source, held, seen, seen_pad, n, by_row):
    first = (clip * held - source + n - 1) // n
    base = source + n * first - clip * held
    place = lax.broadcasted_iota(jnp.int32, (rows, cols), 0 if by_row else 1)
    slot = lax.broadcasted_iota(jnp.int32, (rows, cols), 1 if by_row else 0)
    second = place >= seen_pad
    local = jnp.where(second, place - (seen_pad - seen), place)
    good = (place < seen) | (second & (place < seen_pad + seen))
    return (good & (local == base + n * slot)).astype(F32).astype(BF16)


def greet(n, m, clip, wt):
    barrier = pltpu.get_barrier_semaphore()
    for k in range(1, n):
        pl.semaphore_signal(barrier, inc=1, device_id=(lax.rem(clip + k, n), wt), device_id_type=MESH)
    for k in range(1, m):
        pl.semaphore_signal(barrier, inc=1, device_id=(clip, lax.rem(wt + k, m)), device_id_type=MESH)
    pl.semaphore_wait(barrier, n + m - 2)


def remote(src, dst, send, recv, clip, wt):
    return pltpu.make_async_remote_copy(
        src_ref=src, dst_ref=dst, send_sem=send, recv_sem=recv, device_id=(clip, wt), device_id_type=MESH
    )


def enter_kernel(n, m, share, cap, seen_pad, *refs):
    (enc, vis_in, wp_in, win_in, *vecs) = refs[:14]
    (seen_out, vis_out, wp, win, cols, be) = refs[14:20]
    (pack, gath, out_rows, in_rows, vec_s, vis_s, zs, zr, bs, br, fs, fr, rs, rr) = refs[20:]
    clip = lax.axis_index("clip")
    wt = lax.axis_index("wt")
    held = enc.shape[0]
    seen = vis_in.shape[1]
    wp_rows = wp_in.shape[0]
    win_rows = win_in.shape[0]
    half = n // 2
    plan = segments(
        [("wp", wp_rows)] + [(j, win_rows) for j in range(3)] + [("vec", SEG)], share
    )
    vec_s[...] = jnp.zeros_like(vec_s)
    for i, ref in enumerate(vecs):
        vec_s[i, : ref.shape[0]] = ref[...].astype(F32)
    for name, r, slot, at in plan:
        if name == "wp":
            piece = wp_in[r : r + SEG]
        elif name == "vec":
            piece = vec_s[...].astype(BF16)
        else:
            piece = win_in[r : r + SEG, name * ROWS : (name + 1) * ROWS]
        pack[slot, at : at + SEG] = piece
    for at in range(len(plan) * SEG, n * share, SEG):
        pack[at // share, at % share : at % share + SEG] = jnp.zeros((SEG, ROWS), BF16)
    greet(n, m, clip, wt)

    sends = []
    partner = clip + 1 - 2 * lax.rem(clip, 2)
    for k in range(1, m):
        copy = remote(pack.at[clip], gath.at[clip, wt], zs.at[k], zr.at[k], clip, lax.rem(wt + k, m))
        copy.start()
        sends.append(copy)
    gath[clip, wt] = pack[clip]

    def spread(k):
        z = lax.rem(wt - k + m, m)
        for j in [*range(1, half), 0]:
            piece = gath.at[clip, z]
            dest = lax.rem(clip + 2 * j, n) if j else partner
            copy = remote(piece, piece, bs.at[j, k], br.at[j, k], dest, wt)
            copy.start()
            sends.append(copy)

    spread(0)

    rows_at = lax.broadcasted_iota(jnp.int32, (cap, held), 0)
    cols_at = lax.broadcasted_iota(jnp.int32, (cap, held), 1)
    row_sends = []
    for k in [*range(2, n, 2), *range(3, n, 2), 1, 0] if n > 2 else range(n - 1, -1, -1):
        dest = lax.rem(clip + k, n)
        hot = (rows_at + first_slot(dest, held, clip, n) == cols_at).astype(F32).astype(BF16)
        rows = dg(hot, enc[...], 1, 0).astype(BF16)
        if k == 0:
            in_rows[clip] = rows
        else:
            out_rows[k] = rows
            copy = remote(out_rows.at[k], in_rows.at[clip], rs.at[k], rr.at[k], dest, wt)
            copy.start()
            row_sends.append(copy)

    for k in range(1, m):
        source = lax.rem(wt - k + m, m)
        remote(pack.at[clip], gath.at[clip, source], zs.at[k], zr.at[k], clip, source).wait_recv()
        spread(k)

    vis_s[...] = jnp.full(vis_s.shape, -1.0, F32)
    vis_s[0:2, :seen] = vis_in[...].astype(F32)
    turned = vis_s[...].T
    for copy_at in range(2):
        vis_out[copy_at] = turned[:seen_pad, copy_at : copy_at + 1]

    for k in range(m):
        z = lax.rem(wt - k + m, m)
        for j in range(1, half):
            source = lax.rem(clip - 2 * j + n, n)
            piece = gath.at[source, z]
            remote(piece, piece, bs.at[j, k], br.at[j, k], source, wt).wait_recv()
            copy = remote(piece, piece, fs.at[j, k], fr.at[j, k], partner, wt)
            copy.start()
            sends.append(copy)

    for k in range(1, n):
        source = lax.rem(clip - k + n, n)
        remote(out_rows.at[k], in_rows.at[source], rs.at[k], rr.at[k], source, wt).wait_recv()
    total = None
    for source in range(n):
        hot = interleave(2 * seen_pad, cap, clip, source, held, seen, seen_pad, n, True)
        part = dg(hot, in_rows[source], 1, 0)
        total = part if total is None else total + part
    total = total.astype(BF16)
    seen_out[0] = total[:seen_pad]
    seen_out[1] = total[seen_pad:]

    for k in range(m):
        z = lax.rem(wt - k + m, m)
        for j in range(half):
            source = lax.rem(partner - 2 * j + n, n)
            piece = gath.at[source, z]
            sems = (fs.at[j, k], fr.at[j, k]) if j else (bs.at[0, k], br.at[0, k])
            remote(piece, piece, *sems, partner, wt).wait_recv()
    for z in range(m):
        for name, r, slot, at in plan:
            piece = gath[slot, z, at : at + SEG]
            if name == "wp":
                wp[z * wp_rows + r : z * wp_rows + r + SEG] = piece
            elif name == "vec":
                turned = piece.astype(F32).T
                small = vecs[0].shape[0]
                cols[z * small : (z + 1) * small] = turned[:small]
                large = vecs[BIAS_E].shape[0]
                be[z * large : (z + 1) * large] = turned[:large, BIAS_E : BIAS_E + 1]
            else:
                win[z * win_rows + r : z * win_rows + r + SEG, name * ROWS : (name + 1) * ROWS] = piece
    for copy in sends + row_sends:
        copy.wait_send()


def pack_kernel(wm, we, wr, out):
    rows = wm.shape[0]
    out[:rows] = wm[...]
    at = rows
    for j in range(we.shape[1] // ROWS):
        out[at : at + rows] = we[:, j * ROWS : (j + 1) * ROWS]
        at += rows
    out[at:] = wr[...]


def pack_mlp(wm, we, wr):
    rows = wm.shape[0] + wm.shape[0] * (we.shape[1] // ROWS) + wr.shape[0]
    whole = pl.BlockSpec(memory_space=pltpu.VMEM)
    return pl.pallas_call(
        pack_kernel,
        in_specs=[whole] * 3,
        out_specs=whole,
        out_shape=jax.ShapeDtypeStruct((rows, ROWS), BF16),
        compiler_params=params(),
        cost_estimate=cost(0, 1.3e6),
    )(wm, we, wr)


def enter(n, m, enc, vis, wp, win, vecs):
    held, e = enc.shape
    seen = vis.shape[1]
    seen_pad = up16(seen)
    d = wp.shape[1]
    cap = up16(-(-held // n))
    share = up16(-(-(wp.shape[0] + 3 * win.shape[0] + SEG) // n))
    whole = pl.BlockSpec(memory_space=pltpu.VMEM)
    shape = jax.ShapeDtypeStruct
    dma = pltpu.SemaphoreType.DMA
    ins = (enc, vis, wp, win, *vecs)
    return pl.pallas_call(
        functools.partial(enter_kernel, n, m, share, cap, seen_pad),
        in_specs=[whole] * len(ins),
        out_specs=[whole] * 6,
        out_shape=[
            shape((2, seen_pad, e), BF16), shape((2, seen_pad, 1), F32), shape((e, d), BF16),
            shape((d, 3 * d), BF16), shape((d, 16), F32), shape((vecs[BIAS_E].shape[0] * m, 1), F32),
        ],
        scratch_shapes=[
            pltpu.VMEM((n, share, ROWS), BF16), pltpu.VMEM((n, m, share, ROWS), BF16),
            pltpu.VMEM((n, cap, e), BF16), pltpu.VMEM((n, cap, e), BF16),
            pltpu.VMEM((SEG, ROWS), F32), pltpu.VMEM((8, 2 * LANES), F32),
            dma((m,)), dma((m,)), dma((n // 2, m)), dma((n // 2, m)), dma((n // 2, m)), dma((n // 2, m)),
            dma((n,)), dma((n,)),
        ],
        compiler_params=params(collective_id=0, has_side_effects=True),
        cost_estimate=cost(6e9, 4e6),
    )(*ins)


def front_kernel(seen, vis, wp, cols, pos, win, o_out, inv_out, e_out, stream_hbm, q_hbm, kt_hbm, v_hbm,
                 stream_s, q_s, k_s, v_s, k_rows, v_rows, v_aug, sems):
    copy = pl.program_id(0)
    step = pl.program_id(1)
    width = wp.shape[1]
    moves = [
        pltpu.make_async_copy(src, dst.at[copy], sems.at[i])
        for i, (src, dst) in enumerate(
            ((stream_s, stream_hbm), (q_s, q_hbm), (k_s, kt_hbm), (v_rows, v_hbm))
        )
    ]

    @pl.when(step == 0)
    def _():
        proj = dg(seen[0], wp[...], 1, 0).astype(BF16)
        hot = one_hot(vis[0], LP)
        covered = jnp.sum(hot, 0, keepdims=True)
        stream = dg(proj, hot.astype(BF16), 0, 0) + (1.0 - covered) * cols[:, TOKEN : TOKEN + 1] + pos[...]
        stream_s[...] = stream
        moves[0].start()
        scaled, _ = norm_stats(stream)
        normed = (scaled * cols[:, GAIN1 : GAIN1 + 1] + cols[:, SHIFT1 : SHIFT1 + 1]).astype(BF16)
        lane = lax.broadcasted_iota(jnp.int32, (L, LANES), 1)
        ones = (lane < HEAD + 3).astype(F32).astype(BF16)
        for part in (2, 1, 0):
            sl = slice(part * width, (part + 1) * width)
            mixed = dg(win[:, sl], normed, 0, 0)
            if part == 0:
                q_s[...] = ((mixed + cols[:, BIAS_Q : BIAS_Q + 1]) * Q_SCALE).astype(BF16)
                moves[1].start()
                continue
            if part == 2:
                mixed = mixed + cols[:, BIAS_V : BIAS_V + 1]
            mixed = mixed.astype(BF16)
            dst = k_s if part == 1 else v_s
            dst[:, :L] = mixed[:, :L]
            dst[:, L:] = jnp.zeros((width, LP - L), BF16)
            rows = k_rows if part == 1 else v_rows
            for h in range(H):
                if part == 2:
                    rows[h] = ones
                rows[h, :, :HEAD] = mixed[h * HEAD : (h + 1) * HEAD].T[:L]
            moves[2 if part == 1 else 3].start()

    @pl.when(step > 0)
    def _():
        head = pl.ds(pl.multiple_of((step - 1) * HEAD, HEAD), HEAD)
        row = lax.broadcasted_iota(jnp.int32, (16, L), 0)
        v_aug[:HEAD] = v_s[head, :L]
        v_aug[HEAD:] = (row == 0).astype(F32).astype(BF16)
        qf = q_s[head, :].astype(F32)
        kf = k_s[head, :].astype(F32)
        bound = jnp.max(jnp.sum(qf * qf, 0, keepdims=True)) * jnp.max(jnp.sum(kf * kf, 0, keepdims=True))
        safe = bound <= SAFE_EXPONENT * SAFE_EXPONENT

        def run(shift):
            for start, size in FRONT_BLOCKS:
                sl = slice(start, start + size)
                s = dg(k_rows[step - 1, :, :HEAD], q_s[head, sl], 1, 0)
                if shift:
                    s = s - jnp.max(s, 0, keepdims=True)
                e = jnp.exp2(s).astype(BF16)
                e_out[0, 0, :, sl] = e
                o = dg(v_aug[...], e, 1, 0)
                inv = 1.0 / o[HEAD : HEAD + 1]
                o_out[0, :, sl] = o[:HEAD] * inv
                inv_out[0, 0, :, sl] = inv

        pl.when(safe)(lambda: run(False))
        pl.when(jnp.logical_not(safe))(lambda: run(True))

    @pl.when(step == H)
    def _():
        for move in moves:
            move.wait()


def front(seen, vis, wp, cols, pos, win):
    _, a, e = seen.shape
    d = wp.shape[1]
    const = lambda *s: pl.BlockSpec(s, lambda c, i: (0,) * len(s), pipeline_mode=pl.Buffered(1))
    lead = lambda *s: pl.BlockSpec((1,) + s, lambda c, i: (c,) + (0,) * len(s))
    head = lambda c, i: (c, jnp.maximum(i - 1, 0), 0)
    wide = lambda c, i: (c, jnp.maximum(i - 1, 0), 0, 0)
    any_ = pl.BlockSpec(memory_space=pl.ANY)
    shape = jax.ShapeDtypeStruct
    vm = pltpu.VMEM
    return pl.pallas_call(
        front_kernel,
        grid=(2, H + 1),
        in_specs=[lead(a, e), lead(a, 1), const(e, d), const(d, 16), const(d, LP), const(d, 3 * d)],
        out_specs=[
            pl.BlockSpec((1, HEAD, LP), head), pl.BlockSpec((1, 1, 1, LP), wide), pl.BlockSpec((1, 1, L, LP), wide),
            any_, any_, any_, any_,
        ],
        out_shape=[
            shape((2, d, LP), F32), shape((2, H, 1, LP), F32), shape((2, H, L, LP), BF16),
            shape((2, d, LP), F32), shape((2, d, LP), BF16), shape((2, d, LP), BF16), shape((2, H, L, LANES), BF16),
        ],
        scratch_shapes=[
            vm((d, LP), F32), vm((d, LP), BF16), vm((d, LP), BF16), vm((d, LP), BF16),
            vm((H, L, LANES), BF16), vm((H, L, LANES), BF16), vm((HEAD + 16, L), BF16),
            pltpu.SemaphoreType.DMA((4,)),
        ],
        compiler_params=params(),
        cost_estimate=cost(4e10, 8e7),
    )(seen, vis, wp, cols, pos, win)


def mlp_parts(d, f, m):
    return [("wm", d // m)] + [(j, d // m) for j in range(f // ROWS)] + [("wr", f // m)]


def mid_kernel(n, m, share, o, inv, stream, up, wpack, be, cols,
               dec, ga_out, do_out, dsum_out, gpack, vec_out,
               wm, we, wr, dwm, dwe, dwr, dvec, dbe, drb, stats, n2, act_s, gl_s, g_s):
    copy = pl.program_id(0)
    ff = pl.program_id(1)
    last = pl.num_programs(1) - 1
    d = wm.shape[0]
    f = wr.shape[0]
    parts = mlp_parts(d, f, m)

    @pl.when((copy == 0) & (ff == 0))
    def _():
        for z in range(m):
            at = 0
            for name, rows in parts:
                piece = wpack[z, at : at + rows]
                dst = slice(z * rows, (z + 1) * rows)
                if name == "wm":
                    wm[dst] = piece
                elif name == "wr":
                    wr[dst] = piece
                else:
                    we[dst, name * ROWS : (name + 1) * ROWS] = piece
                at += rows
        dwm[...] = jnp.zeros_like(dwm)
        dwe[...] = jnp.zeros_like(dwe)
        dwr[...] = jnp.zeros_like(dwr)
        dvec[...] = jnp.zeros_like(dvec)
        dbe[...] = jnp.zeros_like(dbe)
        drb[...] = jnp.zeros_like(drb)

    @pl.when(ff == 0)
    def _():
        ctx = o[0].astype(BF16)
        x = stream[0] + dg(wm[...], ctx, 0, 0) + cols[:, BIAS_M : BIAS_M + 1]
        ga_out[0] = x
        mean = jnp.mean(x, 0, keepdims=True)
        center = x - mean
        recip = lax.rsqrt(jnp.mean(center * center, 0, keepdims=True) + EPSILON)
        stats[0:1] = mean
        stats[1:2] = recip
        n2[:d] = (center * recip * cols[:, GAIN2 : GAIN2 + 1] + cols[:, SHIFT2 : SHIFT2 + 1]).astype(BF16)
        row = lax.broadcasted_iota(jnp.int32, (16, LP), 0)
        n2[d:] = (row == 0).astype(F32).astype(BF16)
        g = (up[0].astype(F32) * 0.5).astype(BF16)
        g_s[:L] = g
        g_s[L:] = jnp.zeros((LP - L, d), BF16)
        drb[...] += dg(jnp.ones((8, L), BF16), g, 1, 0)

    rows = pl.ds(pl.multiple_of(ff * FFC, FFC), FFC)
    g = g_s[...]
    lifted = dg(we[:, rows], n2[:d], 0, 0) + be[rows, :]
    bell = jnp.exp(-0.5 * lifted * lifted)
    cdf = 0.5 * (1.0 + lax.erf(lifted * ROOT_HALF))
    act = (lifted * cdf).astype(BF16)
    slope = cdf + lifted * bell * INV_ROOT_TWO_PI
    gl = (dg(wr[rows, :], g, 1, 1) * slope).astype(BF16)
    act_s[rows, :] = act
    gl_s[rows, :] = gl

    @pl.when(ff == last)
    def _():
        x = ga_out[0]
        dwr[...] += dg(act_s[...], g_s[...], 1, 0)
        grad = dg(n2[...], gl_s[...], 1, 1)
        dwe[...] += grad[:d]
        dbe[...] += grad[d : d + 8]
        out = x + dg(wr[...], act_s[...], 0, 0) + cols[:, BIAS_R : BIAS_R + 1]
        dec[0] = out.astype(BF16).T[:L]
        scaled = (x - stats[0:1]) * stats[1:2]
        e = dg(we[...], gl_s[...], 1, 0)
        dvec[:, 0:1] += jnp.sum(e * scaled, 1, keepdims=True)
        dvec[:, 1:2] += jnp.sum(e, 1, keepdims=True)
        back = norm_back(e, scaled, stats[1:2], cols[:, GAIN2 : GAIN2 + 1])
        ga = g_s[...].T.astype(F32) + back
        ga_out[0] = ga
        gm = ga.astype(BF16)
        dvec[:, 2:3] += jnp.sum(gm.astype(F32), 1, keepdims=True)
        ctx = o[0]
        dwm[...] += dg(ctx.astype(BF16), gm, 1, 1)
        do = dg(wm[...], gm, 1, 0)
        for h in range(H):
            hs = slice(h * HEAD, (h + 1) * HEAD)
            part = (do[hs] * inv[0, h]).astype(BF16)
            do_out[0, hs] = part
            dsum_out[0, h] = aug_rows(-jnp.sum(part.astype(F32) * ctx[hs], 0, keepdims=True))

    @pl.when((ff == last) & (copy == 1))
    def _():
        plan = segments(parts, share)
        for z in range(m):
            for name, r, slot, at in plan:
                if name == "wm":
                    piece = dwm[z * (d // m) + r : z * (d // m) + r + SEG]
                elif name == "wr":
                    piece = dwr[z * (f // m) + r : z * (f // m) + r + SEG]
                else:
                    piece = dwe[z * (d // m) + r : z * (d // m) + r + SEG, name * ROWS : (name + 1) * ROWS]
                gpack[slot, z, at : at + SEG] = piece.astype(BF16)
            for at in range(len(plan) * SEG, n * share, SEG):
                gpack[at // share, z, at % share : at % share + SEG] = jnp.zeros((SEG, ROWS), BF16)
        turned = dvec[...].T
        vec_out[...] = jnp.zeros_like(vec_out)
        vec_out[BIAS_M : BIAS_M + 1] = turned[2:3]
        vec_out[GAIN2 : GAIN2 + 1] = turned[0:1]
        vec_out[SHIFT2 : SHIFT2 + 1] = turned[1:2]
        vec_out[BIAS_R : BIAS_R + 1] = drb[0:1]
        for j in range(f // ROWS):
            vec_out[BIAS_E + j : BIAS_E + j + 1] = dbe[0:1, j * ROWS : (j + 1) * ROWS]


def mid(n, m, share, o, inv, stream, up, wpack, be, cols):
    d = cols.shape[0]
    f = be.shape[0]
    once = pl.Buffered(1)
    const = lambda *s: pl.BlockSpec(s, lambda c, k: (0,) * len(s), pipeline_mode=once)
    lead = lambda *s: pl.BlockSpec((1,) + s, lambda c, k: (c,) + (0,) * len(s))
    shape = jax.ShapeDtypeStruct
    vm = pltpu.VMEM
    return pl.pallas_call(
        functools.partial(mid_kernel, n, m, share),
        grid=(2, f // FFC),
        in_specs=[lead(d, LP), lead(H, 1, LP), lead(d, LP), lead(L, d), const(*wpack.shape), const(f, 1), const(d, 16)],
        out_specs=[
            lead(L, d), lead(d, LP), lead(d, LP), lead(H, 16, LP), const(n, m, share, ROWS), const(16, d),
        ],
        out_shape=[
            shape((2, L, d), BF16), shape((2, d, LP), F32), shape((2, d, LP), BF16), shape((2, H, 16, LP), BF16),
            shape((n, m, share, ROWS), BF16), shape((16, d), F32),
        ],
        scratch_shapes=[
            vm((d, d), BF16), vm((d, f), BF16), vm((f, d), BF16),
            vm((d, d), F32), vm((d, f), F32), vm((f, d), F32), vm((d, LANES), F32), vm((8, f), F32), vm((8, d), F32),
            vm((8, LP), F32), vm((d + 16, LP), BF16),
            vm((f, LP), BF16), vm((f, LP), BF16), vm((LP, d), BF16),
        ],
        compiler_params=params(),
        cost_estimate=cost(5e10, 4e7),
    )(o, inv, stream, up, wpack, be, cols)


def back_kernel(n, m, share, held, seen_len, e, v_rows, q, do, dsum, kt, stream_hbm, ga_hbm, seen, vis, win_hbm, cols, vec_in,
                gpack, gp_out, do_aug, gm, kept, qtmp, dwin, dbin, dvec, dwp, n1, gp_s, stream, ga, win, sems):
    copy = pl.program_id(0)
    step = pl.program_id(1)
    clip = lax.axis_index("clip")
    d = cols.shape[0]
    e_width = dwp.shape[0]
    seen_pad = seen.shape[1]
    cap = gp_out.shape[1]

    @pl.when((copy == 0) & (step == 0))
    def _():
        dwin[...] = jnp.zeros_like(dwin)
        dbin[...] = jnp.zeros_like(dbin)
        dvec[...] = jnp.zeros_like(dvec)
        dwp[...] = jnp.zeros_like(dwp)
        do_aug[HEAD + 16 :] = jnp.zeros((LANES - HEAD - 16, LP), BF16)
        kept[...] = jnp.zeros_like(kept)

    loads = [
        pltpu.make_async_copy(stream_hbm.at[copy], stream, sems.at[0]),
        pltpu.make_async_copy(ga_hbm.at[copy], ga, sems.at[1]),
    ]
    load_win = pltpu.make_async_copy(win_hbm, win, sems.at[2])
    pl.when((copy == 0) & (step == 0))(load_win.start)

    @pl.when(step == 0)
    def _():
        for load in loads:
            load.start()

    @pl.when(step < H)
    def _():
        head = pl.ds(pl.multiple_of(step * HEAD, HEAD), HEAD)
        do_aug[:HEAD] = do[0]
        do_aug[HEAD : HEAD + 16] = dsum[0, 0]
        k_sum = None
        v_sum = None
        for start, size in Q_BLOCKS:
            sl = slice(start, start + size)
            p = e[0, 0, :, sl]
            dp = dg(v_rows[0, 0], do_aug[:, sl], 1, 0)
            ds = (p.astype(F32) * dp).astype(BF16)
            v_part = dg(do_aug[:HEAD, sl], p, 1, 1)
            k_part = dg(q[0, :, sl], ds, 1, 1)
            v_sum = v_part if v_sum is None else v_sum + v_part
            k_sum = k_part if k_sum is None else k_sum + k_part
            qtmp[:, sl] = (dg(kt[0, :, :L], ds, 1, 0) * (1.0 / math.sqrt(HEAD))).astype(BF16)
        gm[pl.ds(pl.multiple_of(step * HEAD, HEAD), HEAD), :] = qtmp[...]
        for part, total in ((1, k_sum * (1.0 / LOG2E)), (2, v_sum)):
            kept[:, :L] = total.astype(BF16)
            gm[pl.ds(pl.multiple_of(part * d + step * HEAD, HEAD), HEAD), :] = kept[...]

    @pl.when(step == H)
    def _():
        pl.when(copy == 0)(load_win.wait)
        for load in loads:
            load.wait()
        x = stream[...]
        scaled, recip = norm_stats(x)
        n1[:d] = (scaled * cols[:, GAIN1 : GAIN1 + 1] + cols[:, SHIFT1 : SHIFT1 + 1]).astype(BF16)
        row = lax.broadcasted_iota(jnp.int32, (16, LP), 0)
        n1[d:] = (row == 0).astype(F32).astype(BF16)
        e = None
        for part in range(3):
            sl = slice(part * d, (part + 1) * d)
            grad = dg(n1[...], gm[sl], 1, 1)
            dwin[:, sl] += grad[:d]
            dbin[:, sl] += grad[d : d + 8]
            term = dg(win[:, sl], gm[sl], 1, 0)
            e = term if e is None else e + term
        dvec[:, 0:1] += jnp.sum(e * scaled, 1, keepdims=True)
        dvec[:, 1:2] += jnp.sum(e, 1, keepdims=True)
        gs = ga[...] + norm_back(e, scaled, recip, cols[:, GAIN1 : GAIN1 + 1])
        hot = one_hot(vis[0], LP)
        token = lax.broadcasted_iota(jnp.int32, (1, LP), 1)
        masked = jnp.where(token < L, 1.0 - jnp.sum(hot, 0, keepdims=True), 0.0)
        dvec[:, 2:3] += jnp.sum(gs * masked, 1, keepdims=True)
        gp = dg(hot.astype(BF16), gs.astype(BF16), 1, 1).astype(BF16)
        gp_s[pl.ds(pl.multiple_of(copy * seen_pad, SEG), seen_pad), :] = gp
        dwp[...] += dg(seen[0], gp, 0, 0)

    @pl.when((copy == 1) & (step == H))
    def _():
        for source in range(n):
            pick = interleave(cap, 2 * seen_pad, clip, source, held, seen_len, seen_pad, n, False)
            gp_out[source] = dg(pick, gp_s[...], 1, 0).astype(BF16)
        turned = dvec[...].T
        row = lax.broadcasted_iota(jnp.int32, (16, d), 0)
        vec = vec_in[...]
        vec = jnp.where(row == TOKEN, turned[2:3], vec)
        vec = jnp.where(row == GAIN1, turned[0:1], vec)
        vec = jnp.where(row == SHIFT1, turned[1:2], vec)
        vec = jnp.where(row == BIAS_Q, dbin[0:1, :d], vec)
        vec = jnp.where(row == BIAS_V, dbin[0:1, 2 * d :], vec).astype(BF16)
        wp_rows = e_width // m
        win_rows = d // m
        plan = segments([("wp", wp_rows)] + [(j, win_rows) for j in range(3)] + [("vec", SEG)], share)
        for z in range(m):
            for name, r, slot, at in plan:
                if name == "wp":
                    piece = dwp[z * wp_rows + r : z * wp_rows + r + SEG].astype(BF16)
                elif name == "vec":
                    piece = vec
                else:
                    piece = dwin[
                        z * win_rows + r : z * win_rows + r + SEG, name * ROWS : (name + 1) * ROWS
                    ].astype(BF16)
                gpack[slot, z, at : at + SEG] = piece
            for at in range(len(plan) * SEG, n * share, SEG):
                gpack[at // share, z, at % share : at % share + SEG] = jnp.zeros((SEG, ROWS), BF16)


def back(n, m, share, held, seen_len, e, v_rows, q, do, dsum, kt, stream, ga, seen, vis, win, cols, vec_in):
    _, a, width = seen.shape
    d = win.shape[0]
    cap = up16(-(-held // n))
    const = lambda *s: pl.BlockSpec(s, lambda c, i: (0,) * len(s), pipeline_mode=pl.Buffered(1))
    lead = lambda *s: pl.BlockSpec((1,) + s, lambda c, i: (c,) + (0,) * len(s))
    head = lambda c, i: (c, jnp.minimum(i, H - 1), 0)
    wide = lambda c, i: (c, jnp.minimum(i, H - 1), 0, 0)
    any_ = pl.BlockSpec(memory_space=pl.ANY)
    shape = jax.ShapeDtypeStruct
    vm = pltpu.VMEM
    return pl.pallas_call(
        functools.partial(back_kernel, n, m, share, held, seen_len),
        grid=(2, H + 1),
        in_specs=[
            pl.BlockSpec((1, 1, L, LP), wide), pl.BlockSpec((1, 1, L, LANES), wide), pl.BlockSpec((1, HEAD, LP), head),
            pl.BlockSpec((1, HEAD, LP), head), pl.BlockSpec((1, 1, 16, LP), wide), pl.BlockSpec((1, HEAD, LP), head),
            any_, any_, lead(a, width), lead(a, 1), any_, const(d, 16), const(16, d),
        ],
        out_specs=[const(n, m, share, ROWS), const(n, cap, d)],
        out_shape=[shape((n, m, share, ROWS), BF16), shape((n, cap, d), BF16)],
        scratch_shapes=[
            vm((LANES, LP), BF16), vm((3 * d, LP), BF16), vm((HEAD, LP), BF16), vm((HEAD, LP), BF16),
            vm((d, 3 * d), F32), vm((8, 3 * d), F32), vm((d, LANES), F32), vm((width, d), F32),
            vm((d + 16, LP), BF16), vm((2 * a, d), BF16), vm((d, LP), F32), vm((d, LP), F32), vm((d, 3 * d), BF16),
            pltpu.SemaphoreType.DMA((3,)),
        ],
        compiler_params=params(),
        cost_estimate=cost(1e11, 1e8),
    )(e, v_rows, q, do, dsum, kt, stream, ga, seen, vis, win, cols, vec_in)


def leave_kernel(n, m, gpack, gp, mlp, fin, ret, mlp_out, a1, a2s, a2r, tot, tot_b, brecv, fin_s, ret_s, mlp_s, mlp_z,
                 gs, gr, s1, r1, s2, r2, sb, rb, sc, rc, sm, rm, sf, rf, sz, rz):
    clip = lax.axis_index("clip")
    wt = lax.axis_index("wt")
    half = n // 2
    core = lax.rem(clip, 2)
    chip = clip // 2
    partner = clip + 1 - 2 * core
    greet(n, m, clip, wt)
    sends = []

    def send(*args):
        copy = remote(*args)
        copy.start()
        sends.append(copy)

    order = [*range(1, half), 0]
    turns = [*range(1, m), 0]
    for k in range(1, m):
        zz = lax.rem(wt + k, m)
        send(mlp.at[zz], mlp_z.at[k], sz.at[k], rz.at[k], clip, zz)
    for k in turns:
        zz = lax.rem(wt + k, m)
        for j in order:
            spot = lax.rem(chip + j, half)
            send(gpack.at[2 * spot + 1 - core, zz], a1.at[j, k], s1.at[j, k], r1.at[j, k], partner, wt)
    for k in turns:
        zz = lax.rem(wt + k, m)
        for j in order:
            mine = 2 * lax.rem(chip + j, half) + core
            remote(gpack.at[mine, zz], a1.at[j, k], s1.at[j, k], r1.at[j, k], partner, wt).wait_recv()
            both = gpack[mine, zz].astype(F32) + a1[j, k].astype(F32)
            if j == 0:
                tot[k] = both
            else:
                a2s[j, k] = both.astype(BF16)
                send(a2s.at[j, k], a2r.at[j, k], s2.at[j, k], r2.at[j, k], mine, wt)
    for k in [*range(2, n, 2), *range(1, n, 2)]:
        dest = lax.rem(clip + k, n)
        send(gp.at[dest], ret_s.at[clip], gs.at[k], gr.at[k], dest, wt)
    ret_s[clip] = gp[clip]
    total = mlp[wt].astype(F32)
    for k in range(1, m):
        source = lax.rem(wt - k + m, m)
        remote(mlp.at[source], mlp_z.at[k], sz.at[k], rz.at[k], clip, source).wait_recv()
        total = total + mlp_z[k].astype(F32)
    mlp_s[clip] = total.astype(BF16)
    for j in order:
        dest = lax.rem(clip + 2 * j, n) if j else partner
        send(mlp_s.at[clip], mlp_s.at[clip], sm.at[j], rm.at[j], dest, wt)
    for k in turns:
        zz = lax.rem(wt + k, m)
        total = tot[k]
        for j in range(1, half):
            source = lax.rem(clip - 2 * j + n, n)
            remote(a2s.at[j, k], a2r.at[j, k], s2.at[j, k], r2.at[j, k], source, wt).wait_recv()
            total = total + a2r[j, k].astype(F32)
        if k:
            tot_b[k] = total.astype(BF16)
            send(tot_b.at[k], brecv.at[k], sb.at[k], rb.at[k], clip, zz)
    for k in range(1, m):
        source = lax.rem(wt - k + m, m)
        remote(tot_b.at[k], brecv.at[k], sb.at[k], rb.at[k], clip, source).wait_recv()
        total = total + brecv[k].astype(F32)
    fin_s[clip] = total.astype(BF16)
    for k in [*range(2, n, 2), *range(1, n, 2)]:
        send(fin_s.at[clip], fin_s.at[clip], sc.at[k], rc.at[k], lax.rem(clip + k, n), wt)
    for j in range(1, half):
        source = lax.rem(clip - 2 * j + n, n)
        remote(mlp_s.at[source], mlp_s.at[source], sm.at[j], rm.at[j], source, wt).wait_recv()
        send(mlp_s.at[source], mlp_s.at[source], sf.at[j], rf.at[j], partner, wt)
    for k in range(1, n):
        source = lax.rem(clip - k + n, n)
        remote(gp.at[source], ret_s.at[source], gs.at[k], gr.at[k], source, wt).wait_recv()
    ret[...] = ret_s[...]
    for j in range(half):
        source = lax.rem(partner - 2 * j + n, n)
        sems = (sf.at[j], rf.at[j]) if j else (sm.at[0], rm.at[0])
        remote(mlp_s.at[source], mlp_s.at[source], *sems, partner, wt).wait_recv()
    mlp_out[...] = mlp_s[...]
    for k in range(1, n):
        source = lax.rem(clip - k + n, n)
        remote(fin_s.at[source], fin_s.at[source], sc.at[k], rc.at[k], source, wt).wait_recv()
    fin[...] = fin_s[...]
    for copy in sends:
        copy.wait_send()


def leave(n, m, gpack, gp, mlp):
    _, _, share, _ = gpack.shape
    _, cap, d = gp.shape
    whole = pl.BlockSpec(memory_space=pltpu.VMEM)
    shape = jax.ShapeDtypeStruct
    vm = pltpu.VMEM
    dma = pltpu.SemaphoreType.DMA
    half = n // 2
    return pl.pallas_call(
        functools.partial(leave_kernel, n, m),
        in_specs=[whole] * 3,
        out_specs=[whole] * 3,
        out_shape=[shape((n, share, ROWS), BF16), shape((n, cap, d), BF16), shape((n,) + mlp.shape[1:], BF16)],
        scratch_shapes=[
            vm((half, m, share, ROWS), BF16), vm((half, m, share, ROWS), BF16), vm((half, m, share, ROWS), BF16),
            vm((m, share, ROWS), F32), vm((m, share, ROWS), BF16), vm((m, share, ROWS), BF16),
            vm((n, share, ROWS), BF16), vm((n, cap, d), BF16), vm((n,) + mlp.shape[1:], BF16), vm(mlp.shape, BF16),
            dma((n,)), dma((n,)), dma((half, m)), dma((half, m)), dma((half, m)), dma((half, m)),
            dma((m,)), dma((m,)), dma((n,)), dma((n,)),
            dma((half,)), dma((half,)), dma((half,)), dma((half,)), dma((m,)), dma((m,)),
        ],
        compiler_params=params(collective_id=1, has_side_effects=True),
        cost_estimate=cost(4e9, 4e6),
    )(gpack, gp, mlp)


def finish_kernel(n, m, plan, mlp_plan, fin, ret, mlp, wp, egrad, dwp, dwin, dwm, dwe, dwr, *vecs):
    clip = lax.axis_index("clip")
    wt = lax.axis_index("wt")
    held = egrad.shape[0]
    cap = ret.shape[1]
    row = lax.broadcasted_iota(jnp.int32, (held, cap), 0)
    col = lax.broadcasted_iota(jnp.int32, (held, cap), 1)
    own = None
    for dest in range(n):
        start = first_slot(dest, held, clip, n)
        stop = first_slot(dest + 1, held, clip, n)
        hot = ((row - start == col) & (row < stop)).astype(F32).astype(BF16)
        part = dg(hot, ret[dest], 1, 0)
        own = part if own is None else own + part
    egrad[...] = dg(own.astype(BF16), wp[...], 1, 1).astype(BF16)
    for name, r, slot, at in plan:
        piece = fin[slot, at : at + SEG].astype(F32)
        if name == "wp":
            dwp[r : r + SEG] = piece
        elif name != "vec":
            dwin[r : r + SEG, name * ROWS : (name + 1) * ROWS] = piece
        else:
            for z in range(m):
                @pl.when(wt == z)
                def _():
                    for i, ref in enumerate(vecs[:BIAS_E]):
                        w = ref.shape[0]
                        ref[...] = piece[i, z * w : (z + 1) * w]
                    w = vecs[BIAS_E].shape[0]
                    line = BIAS_E + z * w // ROWS
                    vecs[BIAS_E][...] = piece[line, z * w % ROWS : z * w % ROWS + w]
    for name, r, slot, at in mlp_plan:
        piece = mlp[slot, at : at + SEG].astype(F32)
        if name == "wm":
            dwm[r : r + SEG] = piece
        elif name == "wr":
            dwr[r : r + SEG] = piece
        else:
            dwe[r : r + SEG, name * ROWS : (name + 1) * ROWS] = piece


def finish(n, m, held, fin, ret, mlp, wp, f):
    e, d = wp.shape
    whole = pl.BlockSpec(memory_space=pltpu.VMEM)
    shape = jax.ShapeDtypeStruct
    plan = segments([("wp", e // m)] + [(j, d // m) for j in range(3)] + [("vec", SEG)], fin.shape[1])
    mlp_plan = segments(mlp_parts(d, f, m), mlp.shape[1])
    outs = [shape((held, e), BF16)] + [
        shape((r // m, c), F32) for r, c in ((e, d), (d, 3 * d), (d, d), (d, f), (f, d))
    ] + [shape((d // m,), F32)] * BIAS_E + [shape((f // m,), F32)]
    return pl.pallas_call(
        functools.partial(finish_kernel, n, m, plan, mlp_plan),
        in_specs=[whole] * 4,
        out_specs=[whole] * len(outs),
        out_shape=outs,
        compiler_params=params(),
        cost_estimate=cost(1e9, 4e6),
    )(fin, ret, mlp, wp)


def core(n, m, held, seen_len, seen, vis, wp, win, cols, be, wpack, upstream, reduce_mlp=None):
    d = cols.shape[0]
    pos = jnp.asarray(position_table(d))
    o, inv, e, stream, q, kt, v_rows = front(seen, vis, wp, cols, pos, win)
    share = up16(-(-wpack.shape[1] // n))
    dec, ga, do, dsum, mlp, vec = mid(n, m, share, o, inv, stream, upstream.reshape(2, L, d), wpack, be, cols)
    if reduce_mlp is not None:
        mlp = reduce_mlp(mlp)
    share = up16(-(-(wp.shape[0] // m + 3 * (d // m) + SEG) // n))
    gpack, gp = back(n, m, share, held, seen_len, e, v_rows, q, do, dsum, kt, stream, ga, seen, vis, win, cols, vec)
    return dec, mlp, gpack, gp


def per_device(encoded, visible_at, wp, token, gain1, shift1, win, bq, bv, wm, bm, gain2, shift2, we, be, wr, br, upstream):
    n = lax.axis_size("clip")
    m = lax.axis_size("wt")
    held = encoded.shape[0]
    seen_len = visible_at.shape[1]
    d = wp.shape[1]
    f = be.shape[0] * m
    local = pack_mlp(wm, we, wr)
    wpack = lax.all_gather(local, "wt", axis=0, tiled=True).reshape(m, local.shape[0], ROWS)
    vecs = (token, gain1, shift1, bq, bv, bm, gain2, shift2, br, be)
    seen, vis, wp_full, win_full, cols, be_col = enter(n, m, encoded, visible_at, wp, win, vecs)

    def reduce_mlp(mlp):
        part = lax.psum_scatter(mlp.reshape(-1, ROWS), "clip", scatter_dimension=0, tiled=True)
        return part.reshape(mlp.shape[1:])

    dec, mlp, gpack, gp = core(
        n, m, held, seen_len, seen, vis, wp_full, win_full, cols, be_col, wpack, upstream, reduce_mlp
    )
    fin, ret, mlp = leave(n, m, gpack, gp, mlp)
    egrad, dwp, dwin, dwm, dwe, dwr, *small = finish(n, m, held, fin, ret, mlp, wp_full, f)
    t, g1, s1, vq, vv, vm, g2, s2, vr, ve = small
    return (
        dec.reshape(2 * L, d), egrad, dwp, t, g1, s1, dwin, vq, vv, dwm, vm, g2, s2, dwe, ve, dwr, vr,
    )


def solution(mesh):
    both, wt = P(("clip", "wt"), None), P("wt")
    mat = P("wt", None)
    params_in = (mat, wt, wt, wt, mat, wt, wt, mat, wt, wt, wt, mat, wt, mat, wt)
    return jax.shard_map(
        per_device,
        mesh=mesh,
        in_specs=(both, both) + params_in + (both,),
        out_specs=(both, both) + params_in,
        check_vma=False,
    )
```

```python
import functools
import math

import jax
import jax.numpy as jnp
import numpy as np
from jax import lax
from jax.experimental import pallas as pl
from jax.experimental.pallas import tpu as pltpu
from jax.sharding import PartitionSpec as P

H = 6
HEAD = 64
L = 1568
LANES = 128
LP = -(-L // LANES) * LANES
KP = L
EPSILON = 1e-06
LOG2E = math.log2(math.e)
Q_SCALE = LOG2E / math.sqrt(HEAD)
ROOT_HALF = math.sqrt(0.5)
INV_ROOT_TWO_PI = 1.0 / math.sqrt(2.0 * math.pi)
SAFE_EXPONENT = 60.0
VMEM_LIMIT = 60 * 2**20
FFC = 512
Q_BLOCKS = ((0, 896), (896, LP - 896))
FRONT_BLOCKS = ((0, 1024), (1024, LP - 1024))
F32 = jnp.float32
BF16 = jnp.bfloat16


SEG = 16
ROWS = 384
MESH = pl.DeviceIdType.MESH
TOKEN, GAIN1, SHIFT1, BIAS_Q, BIAS_V, BIAS_M, GAIN2, SHIFT2, BIAS_R, BIAS_E = range(10)


def params(**kw):
    return pltpu.CompilerParams(vmem_limit_bytes=VMEM_LIMIT, **kw)


def cost(flops, moved=0):
    return pl.CostEstimate(flops=int(flops), bytes_accessed=int(moved), transcendentals=0)


def up16(x):
    return -(-x // SEG) * SEG


def segments(parts, share):
    out = []
    at = 0
    for name, rows in parts:
        for r in range(0, rows, SEG):
            out.append((name, r, at // share, at % share))
            at += SEG
    return out


def dg(a, b, ca, cb):
    return lax.dot_general(a, b, (((ca,), (cb,)), ((), ())), preferred_element_type=F32)


def position_table(width):
    places = np.arange(LP, dtype=np.float64)[None, :]
    columns = np.arange(width)
    exponent = (2 * (columns // 2)).astype(np.float64) / width
    angles = places / np.power(10000.0, exponent)[:, None]
    return np.where(columns[:, None] % 2 == 0, np.sin(angles), np.cos(angles)).astype(np.float32)


def norm_stats(x):
    center = x - jnp.mean(x, 0, keepdims=True)
    recip = lax.rsqrt(jnp.mean(center * center, 0, keepdims=True) + EPSILON)
    return center * recip, recip


def norm_back(e, scaled, recip, gain):
    lifted = e * gain
    return recip * (
        lifted
        - jnp.mean(lifted, 0, keepdims=True)
        - scaled * jnp.mean(lifted * scaled, 0, keepdims=True)
    )


def split3(x):
    hi = x.astype(BF16)
    rest = x - hi.astype(F32)
    mid = rest.astype(BF16)
    low = (rest - mid.astype(F32)).astype(BF16)
    return hi, mid, low


def aug_rows(x):
    hi, mid, low = split3(x)
    row = lax.broadcasted_iota(jnp.int32, (16, x.shape[1]), 0)
    zero = jnp.zeros((16, x.shape[1]), F32)
    out = jnp.where(row == 0, hi.astype(F32), zero)
    out = jnp.where(row == 1, mid.astype(F32), out)
    out = jnp.where(row == 2, low.astype(F32), out)
    return out.astype(BF16)


def one_hot(vis, width):
    place = lax.broadcasted_iota(jnp.int32, (vis.shape[0], width), 1).astype(F32)
    return (vis == place).astype(F32)


def first_slot(dest, held, clip, n):
    return (dest * held - clip + n - 1) // n


def interleave(rows, cols, clip, source, held, seen, seen_pad, n, by_row):
    first = (clip * held - source + n - 1) // n
    base = source + n * first - clip * held
    place = lax.broadcasted_iota(jnp.int32, (rows, cols), 0 if by_row else 1)
    slot = lax.broadcasted_iota(jnp.int32, (rows, cols), 1 if by_row else 0)
    second = place >= seen_pad
    local = jnp.where(second, place - (seen_pad - seen), place)
    good = (place < seen) | (second & (place < seen_pad + seen))
    return (good & (local == base + n * slot)).astype(F32).astype(BF16)


def greet(n, m, clip, wt):
    barrier = pltpu.get_barrier_semaphore()
    for k in range(1, n):
        pl.semaphore_signal(barrier, inc=1, device_id=(lax.rem(clip + k, n), wt), device_id_type=MESH)
    for k in range(1, m):
        pl.semaphore_signal(barrier, inc=1, device_id=(clip, lax.rem(wt + k, m)), device_id_type=MESH)
    pl.semaphore_wait(barrier, n + m - 2)


def remote(src, dst, send, recv, clip, wt):
    return pltpu.make_async_remote_copy(
        src_ref=src, dst_ref=dst, send_sem=send, recv_sem=recv, device_id=(clip, wt), device_id_type=MESH
    )


def enter_kernel(n, m, share, cap, seen_pad, *refs):
    (enc, vis_in, wp_in, win_in, *vecs) = refs[:14]
    (seen_out, vis_out, wp, win, cols, be) = refs[14:20]
    (pack, gath, out_rows, in_rows, vec_s, vis_s, zs, zr, bs, br, fs, fr, rs, rr) = refs[20:]
    clip = lax.axis_index("clip")
    wt = lax.axis_index("wt")
    held = enc.shape[0]
    seen = vis_in.shape[1]
    wp_rows = wp_in.shape[0]
    win_rows = win_in.shape[0]
    half = n // 2
    plan = segments(
        [("wp", wp_rows)] + [(j, win_rows) for j in range(3)] + [("vec", SEG)], share
    )
    vec_s[...] = jnp.zeros_like(vec_s)
    for i, ref in enumerate(vecs):
        vec_s[i, : ref.shape[0]] = ref[...].astype(F32)
    for name, r, slot, at in plan:
        if name == "wp":
            piece = wp_in[r : r + SEG]
        elif name == "vec":
            piece = vec_s[...].astype(BF16)
        else:
            piece = win_in[r : r + SEG, name * ROWS : (name + 1) * ROWS]
        pack[slot, at : at + SEG] = piece
    for at in range(len(plan) * SEG, n * share, SEG):
        pack[at // share, at % share : at % share + SEG] = jnp.zeros((SEG, ROWS), BF16)
    greet(n, m, clip, wt)

    sends = []
    partner = clip + 1 - 2 * lax.rem(clip, 2)
    for k in range(1, m):
        copy = remote(pack.at[clip], gath.at[clip, wt], zs.at[k], zr.at[k], clip, lax.rem(wt + k, m))
        copy.start()
        sends.append(copy)
    gath[clip, wt] = pack[clip]

    def spread(k):
        z = lax.rem(wt - k + m, m)
        for j in [*range(1, half), 0]:
            piece = gath.at[clip, z]
            dest = lax.rem(clip + 2 * j, n) if j else partner
            copy = remote(piece, piece, bs.at[j, k], br.at[j, k], dest, wt)
            copy.start()
            sends.append(copy)

    spread(0)

    rows_at = lax.broadcasted_iota(jnp.int32, (cap, held), 0)
    cols_at = lax.broadcasted_iota(jnp.int32, (cap, held), 1)
    row_sends = []
    for k in [*range(2, n, 2), *range(3, n, 2), 1, 0] if n > 2 else range(n - 1, -1, -1):
        dest = lax.rem(clip + k, n)
        hot = (rows_at + first_slot(dest, held, clip, n) == cols_at).astype(F32).astype(BF16)
        rows = dg(hot, enc[...], 1, 0).astype(BF16)
        if k == 0:
            in_rows[clip] = rows
        else:
            out_rows[k] = rows
            copy = remote(out_rows.at[k], in_rows.at[clip], rs.at[k], rr.at[k], dest, wt)
            copy.start()
            row_sends.append(copy)

    for k in range(1, m):
        source = lax.rem(wt - k + m, m)
        remote(pack.at[clip], gath.at[clip, source], zs.at[k], zr.at[k], clip, source).wait_recv()
        spread(k)

    vis_s[...] = jnp.full(vis_s.shape, -1.0, F32)
    vis_s[0:2, :seen] = vis_in[...].astype(F32)
    turned = vis_s[...].T
    for copy_at in range(2):
        vis_out[copy_at] = turned[:seen_pad, copy_at : copy_at + 1]

    for k in range(m):
        z = lax.rem(wt - k + m, m)
        for j in range(1, half):
            source = lax.rem(clip - 2 * j + n, n)
            piece = gath.at[source, z]
            remote(piece, piece, bs.at[j, k], br.at[j, k], source, wt).wait_recv()
            copy = remote(piece, piece, fs.at[j, k], fr.at[j, k], partner, wt)
            copy.start()
            sends.append(copy)

    for k in range(1, n):
        source = lax.rem(clip - k + n, n)
        remote(out_rows.at[k], in_rows.at[source], rs.at[k], rr.at[k], source, wt).wait_recv()
    total = None
    for source in range(n):
        hot = interleave(2 * seen_pad, cap, clip, source, held, seen, seen_pad, n, True)
        part = dg(hot, in_rows[source], 1, 0)
        total = part if total is None else total + part
    total = total.astype(BF16)
    seen_out[0] = total[:seen_pad]
    seen_out[1] = total[seen_pad:]

    for k in range(m):
        z = lax.rem(wt - k + m, m)
        for j in range(half):
            source = lax.rem(partner - 2 * j + n, n)
            piece = gath.at[source, z]
            sems = (fs.at[j, k], fr.at[j, k]) if j else (bs.at[0, k], br.at[0, k])
            remote(piece, piece, *sems, partner, wt).wait_recv()
    for z in range(m):
        for name, r, slot, at in plan:
            piece = gath[slot, z, at : at + SEG]
            if name == "wp":
                wp[z * wp_rows + r : z * wp_rows + r + SEG] = piece
            elif name == "vec":
                turned = piece.astype(F32).T
                small = vecs[0].shape[0]
                cols[z * small : (z + 1) * small] = turned[:small]
                large = vecs[BIAS_E].shape[0]
                be[z * large : (z + 1) * large] = turned[:large, BIAS_E : BIAS_E + 1]
            else:
                win[z * win_rows + r : z * win_rows + r + SEG, name * ROWS : (name + 1) * ROWS] = piece
    for copy in sends + row_sends:
        copy.wait_send()


def pack_kernel(wm, we, wr, out):
    rows = wm.shape[0]
    out[:rows] = wm[...]
    at = rows
    for j in range(we.shape[1] // ROWS):
        out[at : at + rows] = we[:, j * ROWS : (j + 1) * ROWS]
        at += rows
    out[at:] = wr[...]


def pack_mlp(wm, we, wr):
    rows = wm.shape[0] + wm.shape[0] * (we.shape[1] // ROWS) + wr.shape[0]
    whole = pl.BlockSpec(memory_space=pltpu.VMEM)
    return pl.pallas_call(
        pack_kernel,
        in_specs=[whole] * 3,
        out_specs=whole,
        out_shape=jax.ShapeDtypeStruct((rows, ROWS), BF16),
        compiler_params=params(),
        cost_estimate=cost(0, 1.3e6),
    )(wm, we, wr)


def enter(n, m, enc, vis, wp, win, vecs):
    held, e = enc.shape
    seen = vis.shape[1]
    seen_pad = up16(seen)
    d = wp.shape[1]
    cap = up16(-(-held // n))
    share = up16(-(-(wp.shape[0] + 3 * win.shape[0] + SEG) // n))
    whole = pl.BlockSpec(memory_space=pltpu.VMEM)
    shape = jax.ShapeDtypeStruct
    dma = pltpu.SemaphoreType.DMA
    ins = (enc, vis, wp, win, *vecs)
    return pl.pallas_call(
        functools.partial(enter_kernel, n, m, share, cap, seen_pad),
        in_specs=[whole] * len(ins),
        out_specs=[whole] * 6,
        out_shape=[
            shape((2, seen_pad, e), BF16), shape((2, seen_pad, 1), F32), shape((e, d), BF16),
            shape((d, 3 * d), BF16), shape((d, 16), F32), shape((vecs[BIAS_E].shape[0] * m, 1), F32),
        ],
        scratch_shapes=[
            pltpu.VMEM((n, share, ROWS), BF16), pltpu.VMEM((n, m, share, ROWS), BF16),
            pltpu.VMEM((n, cap, e), BF16), pltpu.VMEM((n, cap, e), BF16),
            pltpu.VMEM((SEG, ROWS), F32), pltpu.VMEM((8, 2 * LANES), F32),
            dma((m,)), dma((m,)), dma((n // 2, m)), dma((n // 2, m)), dma((n // 2, m)), dma((n // 2, m)),
            dma((n,)), dma((n,)),
        ],
        compiler_params=params(collective_id=0, has_side_effects=True),
        cost_estimate=cost(6e9, 4e6),
    )(*ins)


def front_kernel(seen, vis, wp, cols, pos, win, o_out, inv_out, e_out, stream_hbm, q_hbm, kt_hbm, v_hbm,
                 stream_s, q_s, k_s, v_s, k_rows, v_rows, v_aug, sems):
    copy = pl.program_id(0)
    step = pl.program_id(1)
    width = wp.shape[1]
    moves = [
        pltpu.make_async_copy(src, dst.at[copy], sems.at[i])
        for i, (src, dst) in enumerate(
            ((stream_s, stream_hbm), (q_s, q_hbm), (k_s, kt_hbm), (v_rows, v_hbm))
        )
    ]

    @pl.when(step == 0)
    def _():
        proj = dg(seen[0], wp[...], 1, 0).astype(BF16)
        hot = one_hot(vis[0], LP)
        covered = jnp.sum(hot, 0, keepdims=True)
        stream = dg(proj, hot.astype(BF16), 0, 0) + (1.0 - covered) * cols[:, TOKEN : TOKEN + 1] + pos[...]
        stream_s[...] = stream
        moves[0].start()
        scaled, _ = norm_stats(stream)
        normed = (scaled * cols[:, GAIN1 : GAIN1 + 1] + cols[:, SHIFT1 : SHIFT1 + 1]).astype(BF16)
        lane = lax.broadcasted_iota(jnp.int32, (L, LANES), 1)
        ones = (lane < HEAD + 3).astype(F32).astype(BF16)
        for part in (2, 1, 0):
            sl = slice(part * width, (part + 1) * width)
            mixed = dg(win[:, sl], normed, 0, 0)
            if part == 0:
                q_s[...] = (mixed + cols[:, BIAS_Q : BIAS_Q + 1]).astype(BF16)
                moves[1].start()
                continue
            if part == 2:
                mixed = mixed + cols[:, BIAS_V : BIAS_V + 1]
            mixed = mixed.astype(BF16)
            dst = k_s if part == 1 else v_s
            dst[:, :L] = mixed[:, :L]
            dst[:, L:] = jnp.zeros((width, LP - L), BF16)
            rows = k_rows if part == 1 else v_rows
            for h in range(H):
                if part == 2:
                    rows[h] = ones
                rows[h, :, :HEAD] = mixed[h * HEAD : (h + 1) * HEAD].T[:L]
            moves[2 if part == 1 else 3].start()

    @pl.when(step > 0)
    def _():
        head = pl.ds(pl.multiple_of((step - 1) * HEAD, HEAD), HEAD)
        row = lax.broadcasted_iota(jnp.int32, (16, L), 0)
        v_aug[:HEAD] = v_s[head, :L]
        v_aug[HEAD:] = (row == 0).astype(F32).astype(BF16)
        qf = q_s[head, :].astype(F32)
        kf = k_s[head, :].astype(F32)
        bound = jnp.max(jnp.sum(qf * qf, 0, keepdims=True)) * jnp.max(jnp.sum(kf * kf, 0, keepdims=True))
        safe = bound * (Q_SCALE * Q_SCALE) <= SAFE_EXPONENT * SAFE_EXPONENT

        def run(shift):
            for start, size in FRONT_BLOCKS:
                sl = slice(start, start + size)
                s = dg(k_rows[step - 1, :, :HEAD], q_s[head, sl], 1, 0)
                if shift:
                    s = s - jnp.max(s, 0, keepdims=True)
                e = jnp.exp2(s * Q_SCALE).astype(BF16)
                e_out[0, 0, :, sl] = e
                o = dg(v_aug[...], e, 1, 0)
                inv = 1.0 / o[HEAD : HEAD + 1]
                o_out[0, :, sl] = o[:HEAD] * inv
                inv_out[0, 0, :, sl] = inv

        pl.when(safe)(lambda: run(False))
        pl.when(jnp.logical_not(safe))(lambda: run(True))

    @pl.when(step == H)
    def _():
        for move in moves:
            move.wait()


def front(seen, vis, wp, cols, pos, win):
    _, a, e = seen.shape
    d = wp.shape[1]
    const = lambda *s: pl.BlockSpec(s, lambda c, i: (0,) * len(s), pipeline_mode=pl.Buffered(1))
    lead = lambda *s: pl.BlockSpec((1,) + s, lambda c, i: (c,) + (0,) * len(s))
    head = lambda c, i: (c, jnp.maximum(i - 1, 0), 0)
    wide = lambda c, i: (c, jnp.maximum(i - 1, 0), 0, 0)
    any_ = pl.BlockSpec(memory_space=pl.ANY)
    shape = jax.ShapeDtypeStruct
    vm = pltpu.VMEM
    return pl.pallas_call(
        front_kernel,
        grid=(2, H + 1),
        in_specs=[lead(a, e), lead(a, 1), const(e, d), const(d, 16), const(d, LP), const(d, 3 * d)],
        out_specs=[
            pl.BlockSpec((1, HEAD, LP), head), pl.BlockSpec((1, 1, 1, LP), wide), pl.BlockSpec((1, 1, L, LP), wide),
            any_, any_, any_, any_,
        ],
        out_shape=[
            shape((2, d, LP), F32), shape((2, H, 1, LP), F32), shape((2, H, L, LP), BF16),
            shape((2, d, LP), F32), shape((2, d, LP), BF16), shape((2, d, LP), BF16), shape((2, H, L, LANES), BF16),
        ],
        scratch_shapes=[
            vm((d, LP), F32), vm((d, LP), BF16), vm((d, LP), BF16), vm((d, LP), BF16),
            vm((H, L, LANES), BF16), vm((H, L, LANES), BF16), vm((HEAD + 16, L), BF16),
            pltpu.SemaphoreType.DMA((4,)),
        ],
        compiler_params=params(),
        cost_estimate=cost(4e10, 8e7),
    )(seen, vis, wp, cols, pos, win)


def mlp_parts(d, f, m):
    return [("wm", d // m)] + [(j, d // m) for j in range(f // ROWS)] + [("wr", f // m)]


def mid_kernel(n, m, share, o, inv, stream, up, wpack, be, cols,
               dec, ga_out, do_out, dsum_out, gpack, vec_out,
               wm, we, wr, dwm, dwe, dwr, dvec, dbe, drb, stats, n2, act_s, gl_s, g_s):
    copy = pl.program_id(0)
    ff = pl.program_id(1)
    last = pl.num_programs(1) - 1
    d = wm.shape[0]
    f = wr.shape[0]
    parts = mlp_parts(d, f, m)

    @pl.when((copy == 0) & (ff == 0))
    def _():
        for z in range(m):
            at = 0
            for name, rows in parts:
                piece = wpack[z, at : at + rows]
                dst = slice(z * rows, (z + 1) * rows)
                if name == "wm":
                    wm[dst] = piece
                elif name == "wr":
                    wr[dst] = piece
                else:
                    we[dst, name * ROWS : (name + 1) * ROWS] = piece
                at += rows
        dwm[...] = jnp.zeros_like(dwm)
        dwe[...] = jnp.zeros_like(dwe)
        dwr[...] = jnp.zeros_like(dwr)
        dvec[...] = jnp.zeros_like(dvec)
        dbe[...] = jnp.zeros_like(dbe)
        drb[...] = jnp.zeros_like(drb)

    @pl.when(ff == 0)
    def _():
        ctx = o[0].astype(BF16)
        x = stream[0] + dg(wm[...], ctx, 0, 0) + cols[:, BIAS_M : BIAS_M + 1]
        ga_out[0] = x
        mean = jnp.mean(x, 0, keepdims=True)
        center = x - mean
        recip = lax.rsqrt(jnp.mean(center * center, 0, keepdims=True) + EPSILON)
        stats[0:1] = mean
        stats[1:2] = recip
        n2[:d] = (center * recip * cols[:, GAIN2 : GAIN2 + 1] + cols[:, SHIFT2 : SHIFT2 + 1]).astype(BF16)
        row = lax.broadcasted_iota(jnp.int32, (16, LP), 0)
        n2[d:] = (row == 0).astype(F32).astype(BF16)
        g = (up[0].astype(F32) * 0.5).astype(BF16)
        g_s[:L] = g
        g_s[L:] = jnp.zeros((LP - L, d), BF16)
        drb[...] += dg(jnp.ones((8, L), BF16), g, 1, 0)

    rows = pl.ds(pl.multiple_of(ff * FFC, FFC), FFC)
    g = g_s[...]
    lifted = dg(we[:, rows], n2[:d], 0, 0) + be[rows, :]
    bell = jnp.exp(-0.5 * lifted * lifted)
    cdf = 0.5 * (1.0 + lax.erf(lifted * ROOT_HALF))
    act = (lifted * cdf).astype(BF16)
    slope = cdf + lifted * bell * INV_ROOT_TWO_PI
    gl = (dg(wr[rows, :], g, 1, 1) * slope).astype(BF16)
    act_s[rows, :] = act
    gl_s[rows, :] = gl

    @pl.when(ff == last)
    def _():
        x = ga_out[0]
        dwr[...] += dg(act_s[...], g_s[...], 1, 0)
        grad = dg(n2[...], gl_s[...], 1, 1)
        dwe[...] += grad[:d]
        dbe[...] += grad[d : d + 8]
        out = x + dg(wr[...], act_s[...], 0, 0) + cols[:, BIAS_R : BIAS_R + 1]
        dec[0] = out.astype(BF16).T[:L]
        scaled = (x - stats[0:1]) * stats[1:2]
        e = dg(we[...], gl_s[...], 1, 0)
        dvec[:, 0:1] += jnp.sum(e * scaled, 1, keepdims=True)
        dvec[:, 1:2] += jnp.sum(e, 1, keepdims=True)
        back = norm_back(e, scaled, stats[1:2], cols[:, GAIN2 : GAIN2 + 1])
        ga = g_s[...].T.astype(F32) + back
        ga_out[0] = ga
        gm = ga.astype(BF16)
        dvec[:, 2:3] += jnp.sum(gm.astype(F32), 1, keepdims=True)
        ctx = o[0]
        dwm[...] += dg(ctx.astype(BF16), gm, 1, 1)
        do = dg(wm[...], gm, 1, 0)
        for h in range(H):
            hs = slice(h * HEAD, (h + 1) * HEAD)
            part = (do[hs] * inv[0, h]).astype(BF16)
            do_out[0, hs] = part
            dsum_out[0, h] = aug_rows(-jnp.sum(part.astype(F32) * ctx[hs], 0, keepdims=True))

    @pl.when((ff == last) & (copy == 1))
    def _():
        plan = segments(parts, share)
        for z in range(m):
            for name, r, slot, at in plan:
                if name == "wm":
                    piece = dwm[z * (d // m) + r : z * (d // m) + r + SEG]
                elif name == "wr":
                    piece = dwr[z * (f // m) + r : z * (f // m) + r + SEG]
                else:
                    piece = dwe[z * (d // m) + r : z * (d // m) + r + SEG, name * ROWS : (name + 1) * ROWS]
                gpack[slot, z, at : at + SEG] = piece.astype(BF16)
            for at in range(len(plan) * SEG, n * share, SEG):
                gpack[at // share, z, at % share : at % share + SEG] = jnp.zeros((SEG, ROWS), BF16)
        turned = dvec[...].T
        vec_out[...] = jnp.zeros_like(vec_out)
        vec_out[BIAS_M : BIAS_M + 1] = turned[2:3]
        vec_out[GAIN2 : GAIN2 + 1] = turned[0:1]
        vec_out[SHIFT2 : SHIFT2 + 1] = turned[1:2]
        vec_out[BIAS_R : BIAS_R + 1] = drb[0:1]
        for j in range(f // ROWS):
            vec_out[BIAS_E + j : BIAS_E + j + 1] = dbe[0:1, j * ROWS : (j + 1) * ROWS]


def mid(n, m, share, o, inv, stream, up, wpack, be, cols):
    d = cols.shape[0]
    f = be.shape[0]
    once = pl.Buffered(1)
    const = lambda *s: pl.BlockSpec(s, lambda c, k: (0,) * len(s), pipeline_mode=once)
    lead = lambda *s: pl.BlockSpec((1,) + s, lambda c, k: (c,) + (0,) * len(s))
    shape = jax.ShapeDtypeStruct
    vm = pltpu.VMEM
    return pl.pallas_call(
        functools.partial(mid_kernel, n, m, share),
        grid=(2, f // FFC),
        in_specs=[lead(d, LP), lead(H, 1, LP), lead(d, LP), lead(L, d), const(*wpack.shape), const(f, 1), const(d, 16)],
        out_specs=[
            lead(L, d), lead(d, LP), lead(d, LP), lead(H, 16, LP), const(n, m, share, ROWS), const(16, d),
        ],
        out_shape=[
            shape((2, L, d), BF16), shape((2, d, LP), F32), shape((2, d, LP), BF16), shape((2, H, 16, LP), BF16),
            shape((n, m, share, ROWS), BF16), shape((16, d), F32),
        ],
        scratch_shapes=[
            vm((d, d), BF16), vm((d, f), BF16), vm((f, d), BF16),
            vm((d, d), F32), vm((d, f), F32), vm((f, d), F32), vm((d, LANES), F32), vm((8, f), F32), vm((8, d), F32),
            vm((8, LP), F32), vm((d + 16, LP), BF16),
            vm((f, LP), BF16), vm((f, LP), BF16), vm((LP, d), BF16),
        ],
        compiler_params=params(),
        cost_estimate=cost(5e10, 4e7),
    )(o, inv, stream, up, wpack, be, cols)


def back_kernel(n, m, share, held, seen_len, e, v_rows, q, do, dsum, kt, stream_hbm, ga_hbm, seen, vis, win_hbm, cols, vec_in,
                gpack, gp_out, do_aug, gm, kept, qtmp, dwin, dbin, dvec, dwp, n1, gp_s, stream, ga, win, sems):
    copy = pl.program_id(0)
    step = pl.program_id(1)
    clip = lax.axis_index("clip")
    d = cols.shape[0]
    e_width = dwp.shape[0]
    seen_pad = seen.shape[1]
    cap = gp_out.shape[1]

    @pl.when((copy == 0) & (step == 0))
    def _():
        dwin[...] = jnp.zeros_like(dwin)
        dbin[...] = jnp.zeros_like(dbin)
        dvec[...] = jnp.zeros_like(dvec)
        dwp[...] = jnp.zeros_like(dwp)
        do_aug[HEAD + 16 :] = jnp.zeros((LANES - HEAD - 16, LP), BF16)
        kept[...] = jnp.zeros_like(kept)

    loads = [
        pltpu.make_async_copy(stream_hbm.at[copy], stream, sems.at[0]),
        pltpu.make_async_copy(ga_hbm.at[copy], ga, sems.at[1]),
    ]
    load_win = pltpu.make_async_copy(win_hbm, win, sems.at[2])
    pl.when((copy == 0) & (step == 0))(load_win.start)

    @pl.when(step == 0)
    def _():
        for load in loads:
            load.start()

    @pl.when(step < H)
    def _():
        head = pl.ds(pl.multiple_of(step * HEAD, HEAD), HEAD)
        do_aug[:HEAD] = do[0]
        do_aug[HEAD : HEAD + 16] = dsum[0, 0]
        k_sum = None
        v_sum = None
        for start, size in Q_BLOCKS:
            sl = slice(start, start + size)
            p = e[0, 0, :, sl]
            dp = dg(v_rows[0, 0], do_aug[:, sl], 1, 0)
            ds = (p.astype(F32) * dp).astype(BF16)
            v_part = dg(do_aug[:HEAD, sl], p, 1, 1)
            k_part = dg(q[0, :, sl], ds, 1, 1)
            v_sum = v_part if v_sum is None else v_sum + v_part
            k_sum = k_part if k_sum is None else k_sum + k_part
            qtmp[:, sl] = (dg(kt[0, :, :L], ds, 1, 0) * (1.0 / math.sqrt(HEAD))).astype(BF16)
        gm[pl.ds(pl.multiple_of(step * HEAD, HEAD), HEAD), :] = qtmp[...]
        for part, total in ((1, k_sum * (1.0 / math.sqrt(HEAD))), (2, v_sum)):
            kept[:, :L] = total.astype(BF16)
            gm[pl.ds(pl.multiple_of(part * d + step * HEAD, HEAD), HEAD), :] = kept[...]

    @pl.when(step == H)
    def _():
        pl.when(copy == 0)(load_win.wait)
        for load in loads:
            load.wait()
        x = stream[...]
        scaled, recip = norm_stats(x)
        n1[:d] = (scaled * cols[:, GAIN1 : GAIN1 + 1] + cols[:, SHIFT1 : SHIFT1 + 1]).astype(BF16)
        row = lax.broadcasted_iota(jnp.int32, (16, LP), 0)
        n1[d:] = (row == 0).astype(F32).astype(BF16)
        e = None
        for part in range(3):
            sl = slice(part * d, (part + 1) * d)
            grad = dg(n1[...], gm[sl], 1, 1)
            dwin[:, sl] += grad[:d]
            dbin[:, sl] += grad[d : d + 8]
            term = dg(win[:, sl], gm[sl], 1, 0)
            e = term if e is None else e + term
        dvec[:, 0:1] += jnp.sum(e * scaled, 1, keepdims=True)
        dvec[:, 1:2] += jnp.sum(e, 1, keepdims=True)
        gs = ga[...] + norm_back(e, scaled, recip, cols[:, GAIN1 : GAIN1 + 1])
        hot = one_hot(vis[0], LP)
        token = lax.broadcasted_iota(jnp.int32, (1, LP), 1)
        masked = jnp.where(token < L, 1.0 - jnp.sum(hot, 0, keepdims=True), 0.0)
        dvec[:, 2:3] += jnp.sum(gs * masked, 1, keepdims=True)
        gp = dg(hot.astype(BF16), gs.astype(BF16), 1, 1).astype(BF16)
        gp_s[pl.ds(pl.multiple_of(copy * seen_pad, SEG), seen_pad), :] = gp
        dwp[...] += dg(seen[0], gp, 0, 0)

    @pl.when((copy == 1) & (step == H))
    def _():
        for source in range(n):
            pick = interleave(cap, 2 * seen_pad, clip, source, held, seen_len, seen_pad, n, False)
            gp_out[source] = dg(pick, gp_s[...], 1, 0).astype(BF16)
        turned = dvec[...].T
        row = lax.broadcasted_iota(jnp.int32, (16, d), 0)
        vec = vec_in[...]
        vec = jnp.where(row == TOKEN, turned[2:3], vec)
        vec = jnp.where(row == GAIN1, turned[0:1], vec)
        vec = jnp.where(row == SHIFT1, turned[1:2], vec)
        vec = jnp.where(row == BIAS_Q, dbin[0:1, :d], vec)
        vec = jnp.where(row == BIAS_V, dbin[0:1, 2 * d :], vec).astype(BF16)
        wp_rows = e_width // m
        win_rows = d // m
        plan = segments([("wp", wp_rows)] + [(j, win_rows) for j in range(3)] + [("vec", SEG)], share)
        for z in range(m):
            for name, r, slot, at in plan:
                if name == "wp":
                    piece = dwp[z * wp_rows + r : z * wp_rows + r + SEG].astype(BF16)
                elif name == "vec":
                    piece = vec
                else:
                    piece = dwin[
                        z * win_rows + r : z * win_rows + r + SEG, name * ROWS : (name + 1) * ROWS
                    ].astype(BF16)
                gpack[slot, z, at : at + SEG] = piece
            for at in range(len(plan) * SEG, n * share, SEG):
                gpack[at // share, z, at % share : at % share + SEG] = jnp.zeros((SEG, ROWS), BF16)


def back(n, m, share, held, seen_len, e, v_rows, q, do, dsum, kt, stream, ga, seen, vis, win, cols, vec_in):
    _, a, width = seen.shape
    d = win.shape[0]
    cap = up16(-(-held // n))
    const = lambda *s: pl.BlockSpec(s, lambda c, i: (0,) * len(s), pipeline_mode=pl.Buffered(1))
    lead = lambda *s: pl.BlockSpec((1,) + s, lambda c, i: (c,) + (0,) * len(s))
    head = lambda c, i: (c, jnp.minimum(i, H - 1), 0)
    wide = lambda c, i: (c, jnp.minimum(i, H - 1), 0, 0)
    any_ = pl.BlockSpec(memory_space=pl.ANY)
    shape = jax.ShapeDtypeStruct
    vm = pltpu.VMEM
    return pl.pallas_call(
        functools.partial(back_kernel, n, m, share, held, seen_len),
        grid=(2, H + 1),
        in_specs=[
            pl.BlockSpec((1, 1, L, LP), wide), pl.BlockSpec((1, 1, L, LANES), wide), pl.BlockSpec((1, HEAD, LP), head),
            pl.BlockSpec((1, HEAD, LP), head), pl.BlockSpec((1, 1, 16, LP), wide), pl.BlockSpec((1, HEAD, LP), head),
            any_, any_, lead(a, width), lead(a, 1), any_, const(d, 16), const(16, d),
        ],
        out_specs=[const(n, m, share, ROWS), const(n, cap, d)],
        out_shape=[shape((n, m, share, ROWS), BF16), shape((n, cap, d), BF16)],
        scratch_shapes=[
            vm((LANES, LP), BF16), vm((3 * d, LP), BF16), vm((HEAD, LP), BF16), vm((HEAD, LP), BF16),
            vm((d, 3 * d), F32), vm((8, 3 * d), F32), vm((d, LANES), F32), vm((width, d), F32),
            vm((d + 16, LP), BF16), vm((2 * a, d), BF16), vm((d, LP), F32), vm((d, LP), F32), vm((d, 3 * d), BF16),
            pltpu.SemaphoreType.DMA((3,)),
        ],
        compiler_params=params(),
        cost_estimate=cost(1e11, 1e8),
    )(e, v_rows, q, do, dsum, kt, stream, ga, seen, vis, win, cols, vec_in)


def leave_kernel(n, m, gpack, gp, mlp, fin, ret, mlp_out, a1, a2s, a2r, tot, tot_b, brecv, fin_s, ret_s, mlp_s, mlp_z,
                 gs, gr, s1, r1, s2, r2, sb, rb, sc, rc, sm, rm, sf, rf, sz, rz):
    clip = lax.axis_index("clip")
    wt = lax.axis_index("wt")
    half = n // 2
    core = lax.rem(clip, 2)
    chip = clip // 2
    partner = clip + 1 - 2 * core
    greet(n, m, clip, wt)
    sends = []

    def send(*args):
        copy = remote(*args)
        copy.start()
        sends.append(copy)

    order = [*range(1, half), 0]
    turns = [*range(1, m), 0]
    for k in range(1, m):
        zz = lax.rem(wt + k, m)
        send(mlp.at[zz], mlp_z.at[k], sz.at[k], rz.at[k], clip, zz)
    for k in turns:
        zz = lax.rem(wt + k, m)
        for j in order:
            spot = lax.rem(chip + j, half)
            send(gpack.at[2 * spot + 1 - core, zz], a1.at[j, k], s1.at[j, k], r1.at[j, k], partner, wt)
    for k in turns:
        zz = lax.rem(wt + k, m)
        for j in order:
            mine = 2 * lax.rem(chip + j, half) + core
            remote(gpack.at[mine, zz], a1.at[j, k], s1.at[j, k], r1.at[j, k], partner, wt).wait_recv()
            both = gpack[mine, zz].astype(F32) + a1[j, k].astype(F32)
            if j == 0:
                tot[k] = both
            else:
                a2s[j, k] = both.astype(BF16)
                send(a2s.at[j, k], a2r.at[j, k], s2.at[j, k], r2.at[j, k], mine, wt)
    for k in [*range(2, n, 2), *range(1, n, 2)]:
        dest = lax.rem(clip + k, n)
        send(gp.at[dest], ret_s.at[clip], gs.at[k], gr.at[k], dest, wt)
    ret_s[clip] = gp[clip]
    total = mlp[wt].astype(F32)
    for k in range(1, m):
        source = lax.rem(wt - k + m, m)
        remote(mlp.at[source], mlp_z.at[k], sz.at[k], rz.at[k], clip, source).wait_recv()
        total = total + mlp_z[k].astype(F32)
    mlp_s[clip] = total.astype(BF16)
    for j in order:
        dest = lax.rem(clip + 2 * j, n) if j else partner
        send(mlp_s.at[clip], mlp_s.at[clip], sm.at[j], rm.at[j], dest, wt)
    for k in turns:
        zz = lax.rem(wt + k, m)
        total = tot[k]
        for j in range(1, half):
            source = lax.rem(clip - 2 * j + n, n)
            remote(a2s.at[j, k], a2r.at[j, k], s2.at[j, k], r2.at[j, k], source, wt).wait_recv()
            total = total + a2r[j, k].astype(F32)
        if k:
            tot_b[k] = total.astype(BF16)
            send(tot_b.at[k], brecv.at[k], sb.at[k], rb.at[k], clip, zz)
    for k in range(1, m):
        source = lax.rem(wt - k + m, m)
        remote(tot_b.at[k], brecv.at[k], sb.at[k], rb.at[k], clip, source).wait_recv()
        total = total + brecv[k].astype(F32)
    fin_s[clip] = total.astype(BF16)
    for j in order:
        dest = lax.rem(clip + 2 * j, n) if j else partner
        send(fin_s.at[clip], fin_s.at[clip], sc.at[j], rc.at[j], dest, wt)
    for j in range(1, half):
        source = lax.rem(clip - 2 * j + n, n)
        remote(mlp_s.at[source], mlp_s.at[source], sm.at[j], rm.at[j], source, wt).wait_recv()
        send(mlp_s.at[source], mlp_s.at[source], sf.at[j], rf.at[j], partner, wt)
    for j in range(1, half):
        source = lax.rem(clip - 2 * j + n, n)
        remote(fin_s.at[source], fin_s.at[source], sc.at[j], rc.at[j], source, wt).wait_recv()
        send(fin_s.at[source], fin_s.at[source], sc.at[half + j], rc.at[half + j], partner, wt)
    for k in range(1, n):
        source = lax.rem(clip - k + n, n)
        remote(gp.at[source], ret_s.at[source], gs.at[k], gr.at[k], source, wt).wait_recv()
    ret[...] = ret_s[...]
    for j in range(half):
        source = lax.rem(partner - 2 * j + n, n)
        sems = (sf.at[j], rf.at[j]) if j else (sm.at[0], rm.at[0])
        remote(mlp_s.at[source], mlp_s.at[source], *sems, partner, wt).wait_recv()
    mlp_out[...] = mlp_s[...]
    for j in range(half):
        source = lax.rem(partner - 2 * j + n, n)
        at = half + j if j else 0
        remote(fin_s.at[source], fin_s.at[source], sc.at[at], rc.at[at], partner, wt).wait_recv()
    fin[...] = fin_s[...]
    for copy in sends:
        copy.wait_send()


def leave(n, m, gpack, gp, mlp):
    _, _, share, _ = gpack.shape
    _, cap, d = gp.shape
    whole = pl.BlockSpec(memory_space=pltpu.VMEM)
    shape = jax.ShapeDtypeStruct
    vm = pltpu.VMEM
    dma = pltpu.SemaphoreType.DMA
    half = n // 2
    return pl.pallas_call(
        functools.partial(leave_kernel, n, m),
        in_specs=[whole] * 3,
        out_specs=[whole] * 3,
        out_shape=[shape((n, share, ROWS), BF16), shape((n, cap, d), BF16), shape((n,) + mlp.shape[1:], BF16)],
        scratch_shapes=[
            vm((half, m, share, ROWS), BF16), vm((half, m, share, ROWS), BF16), vm((half, m, share, ROWS), BF16),
            vm((m, share, ROWS), F32), vm((m, share, ROWS), BF16), vm((m, share, ROWS), BF16),
            vm((n, share, ROWS), BF16), vm((n, cap, d), BF16), vm((n,) + mlp.shape[1:], BF16), vm(mlp.shape, BF16),
            dma((n,)), dma((n,)), dma((half, m)), dma((half, m)), dma((half, m)), dma((half, m)),
            dma((m,)), dma((m,)), dma((n,)), dma((n,)),
            dma((half,)), dma((half,)), dma((half,)), dma((half,)), dma((m,)), dma((m,)),
        ],
        compiler_params=params(collective_id=1, has_side_effects=True),
        cost_estimate=cost(4e9, 4e6),
    )(gpack, gp, mlp)


def finish_kernel(n, m, plan, mlp_plan, fin, ret, mlp, wp, egrad, dwp, dwin, dwm, dwe, dwr, *vecs):
    clip = lax.axis_index("clip")
    wt = lax.axis_index("wt")
    held = egrad.shape[0]
    cap = ret.shape[1]
    row = lax.broadcasted_iota(jnp.int32, (held, cap), 0)
    col = lax.broadcasted_iota(jnp.int32, (held, cap), 1)
    own = None
    for dest in range(n):
        start = first_slot(dest, held, clip, n)
        stop = first_slot(dest + 1, held, clip, n)
        hot = ((row - start == col) & (row < stop)).astype(F32).astype(BF16)
        part = dg(hot, ret[dest], 1, 0)
        own = part if own is None else own + part
    egrad[...] = dg(own.astype(BF16), wp[...], 1, 1).astype(BF16)
    for name, r, slot, at in plan:
        piece = fin[slot, at : at + SEG].astype(F32)
        if name == "wp":
            dwp[r : r + SEG] = piece
        elif name != "vec":
            dwin[r : r + SEG, name * ROWS : (name + 1) * ROWS] = piece
        else:
            for z in range(m):
                @pl.when(wt == z)
                def _():
                    for i, ref in enumerate(vecs[:BIAS_E]):
                        w = ref.shape[0]
                        ref[...] = piece[i, z * w : (z + 1) * w]
                    w = vecs[BIAS_E].shape[0]
                    line = BIAS_E + z * w // ROWS
                    vecs[BIAS_E][...] = piece[line, z * w % ROWS : z * w % ROWS + w]
    for name, r, slot, at in mlp_plan:
        piece = mlp[slot, at : at + SEG].astype(F32)
        if name == "wm":
            dwm[r : r + SEG] = piece
        elif name == "wr":
            dwr[r : r + SEG] = piece
        else:
            dwe[r : r + SEG, name * ROWS : (name + 1) * ROWS] = piece


def finish(n, m, held, fin, ret, mlp, wp, f):
    e, d = wp.shape
    whole = pl.BlockSpec(memory_space=pltpu.VMEM)
    shape = jax.ShapeDtypeStruct
    plan = segments([("wp", e // m)] + [(j, d // m) for j in range(3)] + [("vec", SEG)], fin.shape[1])
    mlp_plan = segments(mlp_parts(d, f, m), mlp.shape[1])
    outs = [shape((held, e), BF16)] + [
        shape((r // m, c), F32) for r, c in ((e, d), (d, 3 * d), (d, d), (d, f), (f, d))
    ] + [shape((d // m,), F32)] * BIAS_E + [shape((f // m,), F32)]
    return pl.pallas_call(
        functools.partial(finish_kernel, n, m, plan, mlp_plan),
        in_specs=[whole] * 4,
        out_specs=[whole] * len(outs),
        out_shape=outs,
        compiler_params=params(),
        cost_estimate=cost(1e9, 4e6),
    )(fin, ret, mlp, wp)


def core(n, m, held, seen_len, seen, vis, wp, win, cols, be, wpack, upstream, reduce_mlp=None):
    d = cols.shape[0]
    pos = jnp.asarray(position_table(d))
    o, inv, e, stream, q, kt, v_rows = front(seen, vis, wp, cols, pos, win)
    share = up16(-(-wpack.shape[1] // n))
    dec, ga, do, dsum, mlp, vec = mid(n, m, share, o, inv, stream, upstream.reshape(2, L, d), wpack, be, cols)
    if reduce_mlp is not None:
        mlp = reduce_mlp(mlp)
    share = up16(-(-(wp.shape[0] // m + 3 * (d // m) + SEG) // n))
    gpack, gp = back(n, m, share, held, seen_len, e, v_rows, q, do, dsum, kt, stream, ga, seen, vis, win, cols, vec)
    return dec, mlp, gpack, gp


def per_device(encoded, visible_at, wp, token, gain1, shift1, win, bq, bv, wm, bm, gain2, shift2, we, be, wr, br, upstream):
    n = lax.axis_size("clip")
    m = lax.axis_size("wt")
    held = encoded.shape[0]
    seen_len = visible_at.shape[1]
    d = wp.shape[1]
    f = be.shape[0] * m
    local = pack_mlp(wm, we, wr)
    wpack = lax.all_gather(local, "wt", axis=0, tiled=True).reshape(m, local.shape[0], ROWS)
    vecs = (token, gain1, shift1, bq, bv, bm, gain2, shift2, br, be)
    seen, vis, wp_full, win_full, cols, be_col = enter(n, m, encoded, visible_at, wp, win, vecs)

    def reduce_mlp(mlp):
        part = lax.psum_scatter(mlp.reshape(-1, ROWS), "clip", scatter_dimension=0, tiled=True)
        return part.reshape(mlp.shape[1:])

    dec, mlp, gpack, gp = core(
        n, m, held, seen_len, seen, vis, wp_full, win_full, cols, be_col, wpack, upstream, reduce_mlp
    )
    fin, ret, mlp = leave(n, m, gpack, gp, mlp)
    egrad, dwp, dwin, dwm, dwe, dwr, *small = finish(n, m, held, fin, ret, mlp, wp_full, f)
    t, g1, s1, vq, vv, vm, g2, s2, vr, ve = small
    return (
        dec.reshape(2 * L, d), egrad, dwp, t, g1, s1, dwin, vq, vv, dwm, vm, g2, s2, dwe, ve, dwr, vr,
    )


def solution(mesh):
    both, wt = P(("clip", "wt"), None), P("wt")
    mat = P("wt", None)
    params_in = (mat, wt, wt, wt, mat, wt, wt, mat, wt, wt, wt, mat, wt, mat, wt)
    return jax.shard_map(
        per_device,
        mesh=mesh,
        in_specs=(both, both) + params_in + (both,),
        out_specs=(both, both) + params_in,
        check_vma=False,
    )
```

```python
import functools
import math

import jax
import jax.numpy as jnp
import numpy as np
from jax import lax
from jax.experimental import pallas as pl
from jax.experimental.pallas import tpu as pltpu
from jax.sharding import PartitionSpec as P

H = 6
HEAD = 64
L = 1568
LANES = 128
LP = -(-L // LANES) * LANES
KP = L
EPSILON = 1e-06
LOG2E = math.log2(math.e)
Q_SCALE = LOG2E / math.sqrt(HEAD)
ROOT_HALF = math.sqrt(0.5)
INV_ROOT_TWO_PI = 1.0 / math.sqrt(2.0 * math.pi)
SAFE_EXPONENT = 60.0
VMEM_LIMIT = 60 * 2**20
FFC = 512
Q_BLOCKS = ((0, 896), (896, LP - 896))
FRONT_BLOCKS = ((0, 1024), (1024, LP - 1024))
F32 = jnp.float32
BF16 = jnp.bfloat16


SEG = 16
ROWS = 384
MESH = pl.DeviceIdType.MESH
TOKEN, GAIN1, SHIFT1, BIAS_Q, BIAS_V, BIAS_M, GAIN2, SHIFT2, BIAS_R, BIAS_E = range(10)


def params(**kw):
    return pltpu.CompilerParams(vmem_limit_bytes=VMEM_LIMIT, **kw)


def cost(flops, moved=0):
    return pl.CostEstimate(flops=int(flops), bytes_accessed=int(moved), transcendentals=0)


def up16(x):
    return -(-x // SEG) * SEG


def segments(parts, share):
    out = []
    at = 0
    for name, rows in parts:
        for r in range(0, rows, SEG):
            out.append((name, r, at // share, at % share))
            at += SEG
    return out


def dg(a, b, ca, cb):
    return lax.dot_general(a, b, (((ca,), (cb,)), ((), ())), preferred_element_type=F32)


def position_table(width):
    places = np.arange(LP, dtype=np.float64)[None, :]
    columns = np.arange(width)
    exponent = (2 * (columns // 2)).astype(np.float64) / width
    angles = places / np.power(10000.0, exponent)[:, None]
    return np.where(columns[:, None] % 2 == 0, np.sin(angles), np.cos(angles)).astype(np.float32)


def norm_stats(x):
    center = x - jnp.mean(x, 0, keepdims=True)
    recip = lax.rsqrt(jnp.mean(center * center, 0, keepdims=True) + EPSILON)
    return center * recip, recip


def norm_back(e, scaled, recip, gain):
    lifted = e * gain
    return recip * (
        lifted
        - jnp.mean(lifted, 0, keepdims=True)
        - scaled * jnp.mean(lifted * scaled, 0, keepdims=True)
    )


def split3(x):
    hi = x.astype(BF16)
    rest = x - hi.astype(F32)
    mid = rest.astype(BF16)
    low = (rest - mid.astype(F32)).astype(BF16)
    return hi, mid, low


def aug_rows(x):
    hi, mid, low = split3(x)
    row = lax.broadcasted_iota(jnp.int32, (16, x.shape[1]), 0)
    zero = jnp.zeros((16, x.shape[1]), F32)
    out = jnp.where(row == 0, hi.astype(F32), zero)
    out = jnp.where(row == 1, mid.astype(F32), out)
    out = jnp.where(row == 2, low.astype(F32), out)
    return out.astype(BF16)


def one_hot(vis, width):
    place = lax.broadcasted_iota(jnp.int32, (vis.shape[0], width), 1).astype(F32)
    return (vis == place).astype(F32)


def first_slot(dest, held, clip, n):
    return (dest * held - clip + n - 1) // n


def interleave(rows, cols, clip, source, held, seen, seen_pad, n, by_row):
    first = (clip * held - source + n - 1) // n
    base = source + n * first - clip * held
    place = lax.broadcasted_iota(jnp.int32, (rows, cols), 0 if by_row else 1)
    slot = lax.broadcasted_iota(jnp.int32, (rows, cols), 1 if by_row else 0)
    second = place >= seen_pad
    local = jnp.where(second, place - (seen_pad - seen), place)
    good = (place < seen) | (second & (place < seen_pad + seen))
    return (good & (local == base + n * slot)).astype(F32).astype(BF16)


def greet(n, m, clip, wt):
    barrier = pltpu.get_barrier_semaphore()
    for k in range(1, n):
        pl.semaphore_signal(barrier, inc=1, device_id=(lax.rem(clip + k, n), wt), device_id_type=MESH)
    for k in range(1, m):
        pl.semaphore_signal(barrier, inc=1, device_id=(clip, lax.rem(wt + k, m)), device_id_type=MESH)
    pl.semaphore_wait(barrier, n + m - 2)


def remote(src, dst, send, recv, clip, wt):
    return pltpu.make_async_remote_copy(
        src_ref=src, dst_ref=dst, send_sem=send, recv_sem=recv, device_id=(clip, wt), device_id_type=MESH
    )


def enter_kernel(n, m, share, cap, seen_pad, *refs):
    (enc, vis_in, wp_in, win_in, *vecs) = refs[:14]
    (seen_out, vis_out, wp, win, cols, be) = refs[14:20]
    (pack, gath, out_rows, in_rows, vec_s, vis_s, zs, zr, bs, br, fs, fr, rs, rr) = refs[20:]
    clip = lax.axis_index("clip")
    wt = lax.axis_index("wt")
    held = enc.shape[0]
    seen = vis_in.shape[1]
    wp_rows = wp_in.shape[0]
    win_rows = win_in.shape[0]
    half = n // 2
    plan = segments(
        [("wp", wp_rows)] + [(j, win_rows) for j in range(3)] + [("vec", SEG)], share
    )
    vec_s[...] = jnp.zeros_like(vec_s)
    for i, ref in enumerate(vecs):
        vec_s[i, : ref.shape[0]] = ref[...].astype(F32)
    for name, r, slot, at in plan:
        if name == "wp":
            piece = wp_in[r : r + SEG]
        elif name == "vec":
            piece = vec_s[...].astype(BF16)
        else:
            piece = win_in[r : r + SEG, name * ROWS : (name + 1) * ROWS]
        pack[slot, at : at + SEG] = piece
    for at in range(len(plan) * SEG, n * share, SEG):
        pack[at // share, at % share : at % share + SEG] = jnp.zeros((SEG, ROWS), BF16)
    greet(n, m, clip, wt)

    sends = []
    partner = clip + 1 - 2 * lax.rem(clip, 2)
    for k in range(1, m):
        copy = remote(pack.at[clip], gath.at[clip, wt], zs.at[k], zr.at[k], clip, lax.rem(wt + k, m))
        copy.start()
        sends.append(copy)
    gath[clip, wt] = pack[clip]

    def spread(k):
        z = lax.rem(wt - k + m, m)
        for j in [*range(1, half), 0]:
            piece = gath.at[clip, z]
            dest = lax.rem(clip + 2 * j, n) if j else partner
            copy = remote(piece, piece, bs.at[j, k], br.at[j, k], dest, wt)
            copy.start()
            sends.append(copy)

    spread(0)

    rows_at = lax.broadcasted_iota(jnp.int32, (cap, held), 0)
    cols_at = lax.broadcasted_iota(jnp.int32, (cap, held), 1)
    row_sends = []
    for k in [*range(2, n, 2), *range(3, n, 2), 1, 0] if n > 2 else range(n - 1, -1, -1):
        dest = lax.rem(clip + k, n)
        hot = (rows_at + first_slot(dest, held, clip, n) == cols_at).astype(F32).astype(BF16)
        rows = dg(hot, enc[...], 1, 0).astype(BF16)
        if k == 0:
            in_rows[clip] = rows
        else:
            out_rows[k] = rows
            copy = remote(out_rows.at[k], in_rows.at[clip], rs.at[k], rr.at[k], dest, wt)
            copy.start()
            row_sends.append(copy)

    for k in range(1, m):
        source = lax.rem(wt - k + m, m)
        remote(pack.at[clip], gath.at[clip, source], zs.at[k], zr.at[k], clip, source).wait_recv()
        spread(k)

    vis_s[...] = jnp.full(vis_s.shape, -1.0, F32)
    vis_s[0:2, :seen] = vis_in[...].astype(F32)
    turned = vis_s[...].T
    for copy_at in range(2):
        vis_out[copy_at] = turned[:seen_pad, copy_at : copy_at + 1]

    for k in range(m):
        z = lax.rem(wt - k + m, m)
        for j in range(1, half):
            source = lax.rem(clip - 2 * j + n, n)
            piece = gath.at[source, z]
            remote(piece, piece, bs.at[j, k], br.at[j, k], source, wt).wait_recv()
            copy = remote(piece, piece, fs.at[j, k], fr.at[j, k], partner, wt)
            copy.start()
            sends.append(copy)

    for k in range(1, n):
        source = lax.rem(clip - k + n, n)
        remote(out_rows.at[k], in_rows.at[source], rs.at[k], rr.at[k], source, wt).wait_recv()
    total = None
    for source in range(n):
        hot = interleave(2 * seen_pad, cap, clip, source, held, seen, seen_pad, n, True)
        part = dg(hot, in_rows[source], 1, 0)
        total = part if total is None else total + part
    total = total.astype(BF16)
    seen_out[0] = total[:seen_pad]
    seen_out[1] = total[seen_pad:]

    for k in range(m):
        z = lax.rem(wt - k + m, m)
        for j in range(half):
            source = lax.rem(partner - 2 * j + n, n)
            piece = gath.at[source, z]
            sems = (fs.at[j, k], fr.at[j, k]) if j else (bs.at[0, k], br.at[0, k])
            remote(piece, piece, *sems, partner, wt).wait_recv()
    for z in range(m):
        for name, r, slot, at in plan:
            piece = gath[slot, z, at : at + SEG]
            if name == "wp":
                wp[z * wp_rows + r : z * wp_rows + r + SEG] = piece
            elif name == "vec":
                turned = piece.astype(F32).T
                small = vecs[0].shape[0]
                cols[z * small : (z + 1) * small] = turned[:small]
                large = vecs[BIAS_E].shape[0]
                be[z * large : (z + 1) * large] = turned[:large, BIAS_E : BIAS_E + 1]
            else:
                win[z * win_rows + r : z * win_rows + r + SEG, name * ROWS : (name + 1) * ROWS] = piece
    for copy in sends + row_sends:
        copy.wait_send()


def pack_kernel(wm, we, wr, out):
    rows = wm.shape[0]
    out[:rows] = wm[...]
    at = rows
    for j in range(we.shape[1] // ROWS):
        out[at : at + rows] = we[:, j * ROWS : (j + 1) * ROWS]
        at += rows
    out[at:] = wr[...]


def pack_mlp(wm, we, wr):
    rows = wm.shape[0] + wm.shape[0] * (we.shape[1] // ROWS) + wr.shape[0]
    whole = pl.BlockSpec(memory_space=pltpu.VMEM)
    return pl.pallas_call(
        pack_kernel,
        in_specs=[whole] * 3,
        out_specs=whole,
        out_shape=jax.ShapeDtypeStruct((rows, ROWS), BF16),
        compiler_params=params(),
        cost_estimate=cost(0, 1.3e6),
    )(wm, we, wr)


def enter(n, m, enc, vis, wp, win, vecs):
    held, e = enc.shape
    seen = vis.shape[1]
    seen_pad = up16(seen)
    d = wp.shape[1]
    cap = up16(-(-held // n))
    share = up16(-(-(wp.shape[0] + 3 * win.shape[0] + SEG) // n))
    whole = pl.BlockSpec(memory_space=pltpu.VMEM)
    shape = jax.ShapeDtypeStruct
    dma = pltpu.SemaphoreType.DMA
    ins = (enc, vis, wp, win, *vecs)
    return pl.pallas_call(
        functools.partial(enter_kernel, n, m, share, cap, seen_pad),
        in_specs=[whole] * len(ins),
        out_specs=[whole] * 6,
        out_shape=[
            shape((2, seen_pad, e), BF16), shape((2, seen_pad, 1), F32), shape((e, d), BF16),
            shape((d, 3 * d), BF16), shape((d, 16), F32), shape((vecs[BIAS_E].shape[0] * m, 1), F32),
        ],
        scratch_shapes=[
            pltpu.VMEM((n, share, ROWS), BF16), pltpu.VMEM((n, m, share, ROWS), BF16),
            pltpu.VMEM((n, cap, e), BF16), pltpu.VMEM((n, cap, e), BF16),
            pltpu.VMEM((SEG, ROWS), F32), pltpu.VMEM((8, 2 * LANES), F32),
            dma((m,)), dma((m,)), dma((n // 2, m)), dma((n // 2, m)), dma((n // 2, m)), dma((n // 2, m)),
            dma((n,)), dma((n,)),
        ],
        compiler_params=params(collective_id=0, has_side_effects=True),
        cost_estimate=cost(6e9, 4e6),
    )(*ins)


def front_kernel(seen, vis, wp, cols, pos, win, o_out, inv_out, e_out, stream_hbm, q_hbm, kt_hbm, v_hbm,
                 stream_s, q_s, k_s, v_s, k_rows, v_rows, v_aug, sems):
    copy = pl.program_id(0)
    step = pl.program_id(1)
    width = wp.shape[1]
    moves = [
        pltpu.make_async_copy(src, dst.at[copy], sems.at[i])
        for i, (src, dst) in enumerate(
            ((stream_s, stream_hbm), (q_s, q_hbm), (k_s, kt_hbm), (v_rows, v_hbm))
        )
    ]

    @pl.when(step == 0)
    def _():
        proj = dg(seen[0], wp[...], 1, 0).astype(BF16)
        hot = one_hot(vis[0], LP)
        covered = jnp.sum(hot, 0, keepdims=True)
        stream = dg(proj, hot.astype(BF16), 0, 0) + (1.0 - covered) * cols[:, TOKEN : TOKEN + 1] + pos[...]
        stream_s[...] = stream
        moves[0].start()
        scaled, _ = norm_stats(stream)
        normed = (scaled * cols[:, GAIN1 : GAIN1 + 1] + cols[:, SHIFT1 : SHIFT1 + 1]).astype(BF16)

        @pl.when(copy == 0)
        def _():
            lane = lax.broadcasted_iota(jnp.int32, (L, LANES), 1)
            ones = (lane < HEAD + 3).astype(F32).astype(BF16)
            for h in range(H):
                v_rows[h] = ones

        for part in (2, 1, 0):
            sl = slice(part * width, (part + 1) * width)
            mixed = dg(win[:, sl], normed, 0, 0)
            if part == 0:
                q_s[...] = (mixed + cols[:, BIAS_Q : BIAS_Q + 1]).astype(BF16)
                moves[1].start()
                continue
            if part == 2:
                mixed = mixed + cols[:, BIAS_V : BIAS_V + 1]
            mixed = mixed.astype(BF16)
            dst = k_s if part == 1 else v_s
            dst[:, :L] = mixed[:, :L]
            dst[:, L:] = jnp.zeros((width, LP - L), BF16)
            rows = k_rows if part == 1 else v_rows
            for h in range(H):
                rows[h, :, :HEAD] = mixed[h * HEAD : (h + 1) * HEAD].T[:L]
            moves[2 if part == 1 else 3].start()

    @pl.when(step > 0)
    def _():
        head = pl.ds(pl.multiple_of((step - 1) * HEAD, HEAD), HEAD)
        row = lax.broadcasted_iota(jnp.int32, (16, L), 0)
        v_aug[:HEAD] = v_s[head, :L]
        v_aug[HEAD:] = (row == 0).astype(F32).astype(BF16)
        qf = q_s[head, :].astype(F32)
        kf = k_s[head, :].astype(F32)
        bound = jnp.max(jnp.sum(qf * qf, 0, keepdims=True)) * jnp.max(jnp.sum(kf * kf, 0, keepdims=True))
        safe = bound * (Q_SCALE * Q_SCALE) <= SAFE_EXPONENT * SAFE_EXPONENT

        def run(shift):
            for start, size in FRONT_BLOCKS:
                sl = slice(start, start + size)
                s = dg(k_rows[step - 1, :, :HEAD], q_s[head, sl], 1, 0)
                if shift:
                    s = s - jnp.max(s, 0, keepdims=True)
                e = jnp.exp2(s * Q_SCALE).astype(BF16)
                e_out[0, 0, :, sl] = e
                o = dg(v_aug[...], e, 1, 0)
                inv = 1.0 / o[HEAD : HEAD + 1]
                o_out[0, :, sl] = o[:HEAD] * inv
                inv_out[0, 0, :, sl] = inv

        pl.when(safe)(lambda: run(False))
        pl.when(jnp.logical_not(safe))(lambda: run(True))

    @pl.when(step == H)
    def _():
        for move in moves:
            move.wait()


def front(seen, vis, wp, cols, pos, win):
    _, a, e = seen.shape
    d = wp.shape[1]
    const = lambda *s: pl.BlockSpec(s, lambda c, i: (0,) * len(s), pipeline_mode=pl.Buffered(1))
    lead = lambda *s: pl.BlockSpec((1,) + s, lambda c, i: (c,) + (0,) * len(s))
    head = lambda c, i: (c, jnp.maximum(i - 1, 0), 0)
    wide = lambda c, i: (c, jnp.maximum(i - 1, 0), 0, 0)
    any_ = pl.BlockSpec(memory_space=pl.ANY)
    shape = jax.ShapeDtypeStruct
    vm = pltpu.VMEM
    return pl.pallas_call(
        front_kernel,
        grid=(2, H + 1),
        in_specs=[lead(a, e), lead(a, 1), const(e, d), const(d, 16), const(d, LP), const(d, 3 * d)],
        out_specs=[
            pl.BlockSpec((1, HEAD, LP), head), pl.BlockSpec((1, 1, 1, LP), wide), pl.BlockSpec((1, 1, L, LP), wide),
            any_, any_, any_, any_,
        ],
        out_shape=[
            shape((2, d, LP), F32), shape((2, H, 1, LP), F32), shape((2, H, L, LP), BF16),
            shape((2, d, LP), F32), shape((2, d, LP), BF16), shape((2, d, LP), BF16), shape((2, H, L, LANES), BF16),
        ],
        scratch_shapes=[
            vm((d, LP), F32), vm((d, LP), BF16), vm((d, LP), BF16), vm((d, LP), BF16),
            vm((H, L, LANES), BF16), vm((H, L, LANES), BF16), vm((HEAD + 16, L), BF16),
            pltpu.SemaphoreType.DMA((4,)),
        ],
        compiler_params=params(),
        cost_estimate=cost(4e10, 8e7),
    )(seen, vis, wp, cols, pos, win)


def mlp_parts(d, f, m):
    return [("wm", d // m)] + [(j, d // m) for j in range(f // ROWS)] + [("wr", f // m)]


def mid_kernel(n, m, share, o, inv, stream, up, wpack, be, cols,
               dec, ga_out, do_out, dsum_out, gpack, vec_out,
               wm, we, wr, dwm, dwe, dwr, dvec, dbe, drb, stats, n2, act_s, gl_s, g_s):
    copy = pl.program_id(0)
    ff = pl.program_id(1)
    last = pl.num_programs(1) - 1
    d = wm.shape[0]
    f = wr.shape[0]
    parts = mlp_parts(d, f, m)

    @pl.when((copy == 0) & (ff == 0))
    def _():
        for z in range(m):
            at = 0
            for name, rows in parts:
                piece = wpack[z, at : at + rows]
                dst = slice(z * rows, (z + 1) * rows)
                if name == "wm":
                    wm[dst] = piece
                elif name == "wr":
                    wr[dst] = piece
                else:
                    we[dst, name * ROWS : (name + 1) * ROWS] = piece
                at += rows
        dwm[...] = jnp.zeros_like(dwm)
        dwe[...] = jnp.zeros_like(dwe)
        dwr[...] = jnp.zeros_like(dwr)
        dvec[...] = jnp.zeros_like(dvec)
        dbe[...] = jnp.zeros_like(dbe)
        drb[...] = jnp.zeros_like(drb)

    @pl.when(ff == 0)
    def _():
        ctx = o[0].astype(BF16)
        x = stream[0] + dg(wm[...], ctx, 0, 0) + cols[:, BIAS_M : BIAS_M + 1]
        ga_out[0] = x
        mean = jnp.mean(x, 0, keepdims=True)
        center = x - mean
        recip = lax.rsqrt(jnp.mean(center * center, 0, keepdims=True) + EPSILON)
        stats[0:1] = mean
        stats[1:2] = recip
        n2[:d] = (center * recip * cols[:, GAIN2 : GAIN2 + 1] + cols[:, SHIFT2 : SHIFT2 + 1]).astype(BF16)
        row = lax.broadcasted_iota(jnp.int32, (16, LP), 0)
        n2[d:] = (row == 0).astype(F32).astype(BF16)
        g = (up[0].astype(F32) * 0.5).astype(BF16)
        g_s[:L] = g
        g_s[L:] = jnp.zeros((LP - L, d), BF16)
        drb[...] += dg(jnp.ones((8, L), BF16), g, 1, 0)

    rows = pl.ds(pl.multiple_of(ff * FFC, FFC), FFC)
    g = g_s[...]
    lifted = dg(we[:, rows], n2[:d], 0, 0) + be[rows, :]
    bell = jnp.exp(-0.5 * lifted * lifted)
    cdf = 0.5 * (1.0 + lax.erf(lifted * ROOT_HALF))
    act = (lifted * cdf).astype(BF16)
    slope = cdf + lifted * bell * INV_ROOT_TWO_PI
    gl = (dg(wr[rows, :], g, 1, 1) * slope).astype(BF16)
    act_s[rows, :] = act
    gl_s[rows, :] = gl

    @pl.when(ff == last)
    def _():
        x = ga_out[0]
        dwr[...] += dg(act_s[...], g_s[...], 1, 0)
        grad = dg(n2[...], gl_s[...], 1, 1)
        dwe[...] += grad[:d]
        dbe[...] += grad[d : d + 8]
        out = x + dg(wr[...], act_s[...], 0, 0) + cols[:, BIAS_R : BIAS_R + 1]
        dec[0] = out.astype(BF16).T[:L]
        scaled = (x - stats[0:1]) * stats[1:2]
        e = dg(we[...], gl_s[...], 1, 0)
        dvec[:, 0:1] += jnp.sum(e * scaled, 1, keepdims=True)
        dvec[:, 1:2] += jnp.sum(e, 1, keepdims=True)
        back = norm_back(e, scaled, stats[1:2], cols[:, GAIN2 : GAIN2 + 1])
        ga = g_s[...].T.astype(F32) + back
        ga_out[0] = ga
        gm = ga.astype(BF16)
        dvec[:, 2:3] += jnp.sum(gm.astype(F32), 1, keepdims=True)
        ctx = o[0]
        dwm[...] += dg(ctx.astype(BF16), gm, 1, 1)
        do = dg(wm[...], gm, 1, 0)
        for h in range(H):
            hs = slice(h * HEAD, (h + 1) * HEAD)
            part = (do[hs] * inv[0, h]).astype(BF16)
            do_out[0, hs] = part
            dsum_out[0, h] = aug_rows(-jnp.sum(part.astype(F32) * ctx[hs], 0, keepdims=True))

    @pl.when((ff == last) & (copy == 1))
    def _():
        plan = segments(parts, share)
        for z in range(m):
            for name, r, slot, at in plan:
                if name == "wm":
                    piece = dwm[z * (d // m) + r : z * (d // m) + r + SEG]
                elif name == "wr":
                    piece = dwr[z * (f // m) + r : z * (f // m) + r + SEG]
                else:
                    piece = dwe[z * (d // m) + r : z * (d // m) + r + SEG, name * ROWS : (name + 1) * ROWS]
                gpack[slot, z, at : at + SEG] = piece.astype(BF16)
            for at in range(len(plan) * SEG, n * share, SEG):
                gpack[at // share, z, at % share : at % share + SEG] = jnp.zeros((SEG, ROWS), BF16)
        turned = dvec[...].T
        vec_out[...] = jnp.zeros_like(vec_out)
        vec_out[BIAS_M : BIAS_M + 1] = turned[2:3]
        vec_out[GAIN2 : GAIN2 + 1] = turned[0:1]
        vec_out[SHIFT2 : SHIFT2 + 1] = turned[1:2]
        vec_out[BIAS_R : BIAS_R + 1] = drb[0:1]
        for j in range(f // ROWS):
            vec_out[BIAS_E + j : BIAS_E + j + 1] = dbe[0:1, j * ROWS : (j + 1) * ROWS]


def mid(n, m, share, o, inv, stream, up, wpack, be, cols):
    d = cols.shape[0]
    f = be.shape[0]
    once = pl.Buffered(1)
    const = lambda *s: pl.BlockSpec(s, lambda c, k: (0,) * len(s), pipeline_mode=once)
    lead = lambda *s: pl.BlockSpec((1,) + s, lambda c, k: (c,) + (0,) * len(s))
    shape = jax.ShapeDtypeStruct
    vm = pltpu.VMEM
    return pl.pallas_call(
        functools.partial(mid_kernel, n, m, share),
        grid=(2, f // FFC),
        in_specs=[lead(d, LP), lead(H, 1, LP), lead(d, LP), lead(L, d), const(*wpack.shape), const(f, 1), const(d, 16)],
        out_specs=[
            lead(L, d), lead(d, LP), lead(d, LP), lead(H, 16, LP), const(n, m, share, ROWS), const(16, d),
        ],
        out_shape=[
            shape((2, L, d), BF16), shape((2, d, LP), F32), shape((2, d, LP), BF16), shape((2, H, 16, LP), BF16),
            shape((n, m, share, ROWS), BF16), shape((16, d), F32),
        ],
        scratch_shapes=[
            vm((d, d), BF16), vm((d, f), BF16), vm((f, d), BF16),
            vm((d, d), F32), vm((d, f), F32), vm((f, d), F32), vm((d, LANES), F32), vm((8, f), F32), vm((8, d), F32),
            vm((8, LP), F32), vm((d + 16, LP), BF16),
            vm((f, LP), BF16), vm((f, LP), BF16), vm((LP, d), BF16),
        ],
        compiler_params=params(),
        cost_estimate=cost(5e10, 4e7),
    )(o, inv, stream, up, wpack, be, cols)


def back_kernel(n, m, share, held, seen_len, e, v_rows, q, do, dsum, kt, stream_hbm, ga_hbm, seen, vis, win_hbm, cols, vec_in,
                gpack, gp_out, do_aug, gm, kept, qtmp, dwin, dbin, dvec, dwp, n1, gp_s, stream, ga, win, sems):
    copy = pl.program_id(0)
    step = pl.program_id(1)
    clip = lax.axis_index("clip")
    d = cols.shape[0]
    e_width = dwp.shape[0]
    seen_pad = seen.shape[1]
    cap = gp_out.shape[1]

    @pl.when((copy == 0) & (step == 0))
    def _():
        dwin[...] = jnp.zeros_like(dwin)
        dbin[...] = jnp.zeros_like(dbin)
        dvec[...] = jnp.zeros_like(dvec)
        dwp[...] = jnp.zeros_like(dwp)
        do_aug[HEAD + 16 :] = jnp.zeros((LANES - HEAD - 16, LP), BF16)
        kept[...] = jnp.zeros_like(kept)

    loads = [
        pltpu.make_async_copy(stream_hbm.at[copy], stream, sems.at[0]),
        pltpu.make_async_copy(ga_hbm.at[copy], ga, sems.at[1]),
    ]
    load_win = pltpu.make_async_copy(win_hbm, win, sems.at[2])
    pl.when((copy == 0) & (step == 0))(load_win.start)

    @pl.when(step == 0)
    def _():
        for load in loads:
            load.start()

    @pl.when(step < H)
    def _():
        head = pl.ds(pl.multiple_of(step * HEAD, HEAD), HEAD)
        do_aug[:HEAD] = do[0]
        do_aug[HEAD : HEAD + 16] = dsum[0, 0]
        k_sum = None
        v_sum = None
        for start, size in Q_BLOCKS:
            sl = slice(start, start + size)
            p = e[0, 0, :, sl]
            dp = dg(v_rows[0, 0], do_aug[:, sl], 1, 0)
            ds = (p.astype(F32) * dp).astype(BF16)
            v_part = dg(do_aug[:HEAD, sl], p, 1, 1)
            k_part = dg(q[0, :, sl], ds, 1, 1)
            v_sum = v_part if v_sum is None else v_sum + v_part
            k_sum = k_part if k_sum is None else k_sum + k_part
            qtmp[:, sl] = (dg(kt[0, :, :L], ds, 1, 0) * (1.0 / math.sqrt(HEAD))).astype(BF16)
        gm[pl.ds(pl.multiple_of(step * HEAD, HEAD), HEAD), :] = qtmp[...]
        for part, total in ((1, k_sum * (1.0 / math.sqrt(HEAD))), (2, v_sum)):
            kept[:, :L] = total.astype(BF16)
            gm[pl.ds(pl.multiple_of(part * d + step * HEAD, HEAD), HEAD), :] = kept[...]

    @pl.when(step == H)
    def _():
        pl.when(copy == 0)(load_win.wait)
        for load in loads:
            load.wait()
        x = stream[...]
        scaled, recip = norm_stats(x)
        n1[:d] = (scaled * cols[:, GAIN1 : GAIN1 + 1] + cols[:, SHIFT1 : SHIFT1 + 1]).astype(BF16)
        row = lax.broadcasted_iota(jnp.int32, (16, LP), 0)
        n1[d:] = (row == 0).astype(F32).astype(BF16)
        e = None
        for part in range(3):
            sl = slice(part * d, (part + 1) * d)
            grad = dg(n1[...], gm[sl], 1, 1)
            dwin[:, sl] += grad[:d]
            dbin[:, sl] += grad[d : d + 8]
            term = dg(win[:, sl], gm[sl], 1, 0)
            e = term if e is None else e + term
        dvec[:, 0:1] += jnp.sum(e * scaled, 1, keepdims=True)
        dvec[:, 1:2] += jnp.sum(e, 1, keepdims=True)
        gs = ga[...] + norm_back(e, scaled, recip, cols[:, GAIN1 : GAIN1 + 1])
        hot = one_hot(vis[0], LP)
        token = lax.broadcasted_iota(jnp.int32, (1, LP), 1)
        masked = jnp.where(token < L, 1.0 - jnp.sum(hot, 0, keepdims=True), 0.0)
        dvec[:, 2:3] += jnp.sum(gs * masked, 1, keepdims=True)
        gp = dg(hot.astype(BF16), gs.astype(BF16), 1, 1).astype(BF16)
        gp_s[pl.ds(pl.multiple_of(copy * seen_pad, SEG), seen_pad), :] = gp
        dwp[...] += dg(seen[0], gp, 0, 0)

    @pl.when((copy == 1) & (step == H))
    def _():
        for source in range(n):
            pick = interleave(cap, 2 * seen_pad, clip, source, held, seen_len, seen_pad, n, False)
            gp_out[source] = dg(pick, gp_s[...], 1, 0).astype(BF16)
        turned = dvec[...].T
        row = lax.broadcasted_iota(jnp.int32, (16, d), 0)
        vec = vec_in[...]
        vec = jnp.where(row == TOKEN, turned[2:3], vec)
        vec = jnp.where(row == GAIN1, turned[0:1], vec)
        vec = jnp.where(row == SHIFT1, turned[1:2], vec)
        vec = jnp.where(row == BIAS_Q, dbin[0:1, :d], vec)
        vec = jnp.where(row == BIAS_V, dbin[0:1, 2 * d :], vec).astype(BF16)
        wp_rows = e_width // m
        win_rows = d // m
        plan = segments([("wp", wp_rows)] + [(j, win_rows) for j in range(3)] + [("vec", SEG)], share)
        for z in range(m):
            for name, r, slot, at in plan:
                if name == "wp":
                    piece = dwp[z * wp_rows + r : z * wp_rows + r + SEG].astype(BF16)
                elif name == "vec":
                    piece = vec
                else:
                    piece = dwin[
                        z * win_rows + r : z * win_rows + r + SEG, name * ROWS : (name + 1) * ROWS
                    ].astype(BF16)
                gpack[slot, z, at : at + SEG] = piece
            for at in range(len(plan) * SEG, n * share, SEG):
                gpack[at // share, z, at % share : at % share + SEG] = jnp.zeros((SEG, ROWS), BF16)


def back(n, m, share, held, seen_len, e, v_rows, q, do, dsum, kt, stream, ga, seen, vis, win, cols, vec_in):
    _, a, width = seen.shape
    d = win.shape[0]
    cap = up16(-(-held // n))
    const = lambda *s: pl.BlockSpec(s, lambda c, i: (0,) * len(s), pipeline_mode=pl.Buffered(1))
    lead = lambda *s: pl.BlockSpec((1,) + s, lambda c, i: (c,) + (0,) * len(s))
    head = lambda c, i: (c, jnp.minimum(i, H - 1), 0)
    wide = lambda c, i: (c, jnp.minimum(i, H - 1), 0, 0)
    any_ = pl.BlockSpec(memory_space=pl.ANY)
    shape = jax.ShapeDtypeStruct
    vm = pltpu.VMEM
    return pl.pallas_call(
        functools.partial(back_kernel, n, m, share, held, seen_len),
        grid=(2, H + 1),
        in_specs=[
            pl.BlockSpec((1, 1, L, LP), wide), pl.BlockSpec((1, 1, L, LANES), wide), pl.BlockSpec((1, HEAD, LP), head),
            pl.BlockSpec((1, HEAD, LP), head), pl.BlockSpec((1, 1, 16, LP), wide), pl.BlockSpec((1, HEAD, LP), head),
            any_, any_, lead(a, width), lead(a, 1), any_, const(d, 16), const(16, d),
        ],
        out_specs=[const(n, m, share, ROWS), const(n, cap, d)],
        out_shape=[shape((n, m, share, ROWS), BF16), shape((n, cap, d), BF16)],
        scratch_shapes=[
            vm((LANES, LP), BF16), vm((3 * d, LP), BF16), vm((HEAD, LP), BF16), vm((HEAD, LP), BF16),
            vm((d, 3 * d), F32), vm((8, 3 * d), F32), vm((d, LANES), F32), vm((width, d), F32),
            vm((d + 16, LP), BF16), vm((2 * a, d), BF16), vm((d, LP), F32), vm((d, LP), F32), vm((d, 3 * d), BF16),
            pltpu.SemaphoreType.DMA((3,)),
        ],
        compiler_params=params(),
        cost_estimate=cost(1e11, 1e8),
    )(e, v_rows, q, do, dsum, kt, stream, ga, seen, vis, win, cols, vec_in)


def leave_kernel(n, m, gpack, gp, mlp, fin, ret, mlp_out, a1, a2s, a2r, tot, tot_b, brecv, fin_s, ret_s, mlp_s, mlp_z,
                 gs, gr, s1, r1, s2, r2, sb, rb, sc, rc, sm, rm, sf, rf, sz, rz):
    clip = lax.axis_index("clip")
    wt = lax.axis_index("wt")
    half = n // 2
    core = lax.rem(clip, 2)
    chip = clip // 2
    partner = clip + 1 - 2 * core
    greet(n, m, clip, wt)
    sends = []

    def send(*args):
        copy = remote(*args)
        copy.start()
        sends.append(copy)

    order = [*range(1, half), 0]
    turns = [*range(1, m), 0]
    for k in range(1, m):
        zz = lax.rem(wt + k, m)
        send(mlp.at[zz], mlp_z.at[k], sz.at[k], rz.at[k], clip, zz)
    for k in turns:
        zz = lax.rem(wt + k, m)
        for j in order:
            spot = lax.rem(chip + j, half)
            send(gpack.at[2 * spot + 1 - core, zz], a1.at[j, k], s1.at[j, k], r1.at[j, k], partner, wt)
    for k in turns:
        zz = lax.rem(wt + k, m)
        for j in order:
            mine = 2 * lax.rem(chip + j, half) + core
            remote(gpack.at[mine, zz], a1.at[j, k], s1.at[j, k], r1.at[j, k], partner, wt).wait_recv()
            both = gpack[mine, zz].astype(F32) + a1[j, k].astype(F32)
            if j == 0:
                tot[k] = both
            else:
                a2s[j, k] = both.astype(BF16)
                send(a2s.at[j, k], a2r.at[j, k], s2.at[j, k], r2.at[j, k], mine, wt)
    for k in [*range(2, n, 2), *range(1, n, 2)]:
        dest = lax.rem(clip + k, n)
        send(gp.at[dest], ret_s.at[clip], gs.at[k], gr.at[k], dest, wt)
    ret_s[clip] = gp[clip]
    total = mlp[wt].astype(F32)
    for k in range(1, m):
        source = lax.rem(wt - k + m, m)
        remote(mlp.at[source], mlp_z.at[k], sz.at[k], rz.at[k], clip, source).wait_recv()
        total = total + mlp_z[k].astype(F32)
    mlp_s[clip] = total.astype(BF16)
    for j in order:
        dest = lax.rem(clip + 2 * j, n) if j else partner
        send(mlp_s.at[clip], mlp_s.at[clip], sm.at[j], rm.at[j], dest, wt)
    for k in turns:
        zz = lax.rem(wt + k, m)
        total = tot[k]
        for j in range(1, half):
            source = lax.rem(clip - 2 * j + n, n)
            remote(a2s.at[j, k], a2r.at[j, k], s2.at[j, k], r2.at[j, k], source, wt).wait_recv()
            total = total + a2r[j, k].astype(F32)
        if k:
            tot_b[k] = total.astype(BF16)
            send(tot_b.at[k], brecv.at[k], sb.at[k], rb.at[k], clip, zz)
    for k in range(1, m):
        source = lax.rem(wt - k + m, m)
        remote(tot_b.at[k], brecv.at[k], sb.at[k], rb.at[k], clip, source).wait_recv()
        total = total + brecv[k].astype(F32)
    fin_s[clip] = total.astype(BF16)
    for j in order:
        dest = lax.rem(clip + 2 * j, n) if j else partner
        send(fin_s.at[clip], fin_s.at[clip], sc.at[j], rc.at[j], dest, wt)
    for j in range(1, half):
        source = lax.rem(clip - 2 * j + n, n)
        remote(mlp_s.at[source], mlp_s.at[source], sm.at[j], rm.at[j], source, wt).wait_recv()
        send(mlp_s.at[source], mlp_s.at[source], sf.at[j], rf.at[j], partner, wt)
    for j in range(1, half):
        source = lax.rem(clip - 2 * j + n, n)
        remote(fin_s.at[source], fin_s.at[source], sc.at[j], rc.at[j], source, wt).wait_recv()
        send(fin_s.at[source], fin_s.at[source], sc.at[half + j], rc.at[half + j], partner, wt)
    for k in range(1, n):
        source = lax.rem(clip - k + n, n)
        remote(gp.at[source], ret_s.at[source], gs.at[k], gr.at[k], source, wt).wait_recv()
    ret[...] = ret_s[...]
    for j in range(half):
        source = lax.rem(partner - 2 * j + n, n)
        sems = (sf.at[j], rf.at[j]) if j else (sm.at[0], rm.at[0])
        remote(mlp_s.at[source], mlp_s.at[source], *sems, partner, wt).wait_recv()
    mlp_out[...] = mlp_s[...]
    for j in range(half):
        source = lax.rem(partner - 2 * j + n, n)
        at = half + j if j else 0
        remote(fin_s.at[source], fin_s.at[source], sc.at[at], rc.at[at], partner, wt).wait_recv()
    fin[...] = fin_s[...]
    for copy in sends:
        copy.wait_send()


def leave(n, m, gpack, gp, mlp):
    _, _, share, _ = gpack.shape
    _, cap, d = gp.shape
    whole = pl.BlockSpec(memory_space=pltpu.VMEM)
    shape = jax.ShapeDtypeStruct
    vm = pltpu.VMEM
    dma = pltpu.SemaphoreType.DMA
    half = n // 2
    return pl.pallas_call(
        functools.partial(leave_kernel, n, m),
        in_specs=[whole] * 3,
        out_specs=[whole] * 3,
        out_shape=[shape((n, share, ROWS), BF16), shape((n, cap, d), BF16), shape((n,) + mlp.shape[1:], BF16)],
        scratch_shapes=[
            vm((half, m, share, ROWS), BF16), vm((half, m, share, ROWS), BF16), vm((half, m, share, ROWS), BF16),
            vm((m, share, ROWS), F32), vm((m, share, ROWS), BF16), vm((m, share, ROWS), BF16),
            vm((n, share, ROWS), BF16), vm((n, cap, d), BF16), vm((n,) + mlp.shape[1:], BF16), vm(mlp.shape, BF16),
            dma((n,)), dma((n,)), dma((half, m)), dma((half, m)), dma((half, m)), dma((half, m)),
            dma((m,)), dma((m,)), dma((n,)), dma((n,)),
            dma((half,)), dma((half,)), dma((half,)), dma((half,)), dma((m,)), dma((m,)),
        ],
        compiler_params=params(collective_id=1, has_side_effects=True),
        cost_estimate=cost(4e9, 4e6),
    )(gpack, gp, mlp)


def finish_kernel(n, m, plan, mlp_plan, fin, ret, mlp, wp, egrad, dwp, dwin, dwm, dwe, dwr, *vecs):
    clip = lax.axis_index("clip")
    wt = lax.axis_index("wt")
    held = egrad.shape[0]
    cap = ret.shape[1]
    row = lax.broadcasted_iota(jnp.int32, (held, cap), 0)
    col = lax.broadcasted_iota(jnp.int32, (held, cap), 1)
    own = None
    for dest in range(n):
        start = first_slot(dest, held, clip, n)
        stop = first_slot(dest + 1, held, clip, n)
        hot = ((row - start == col) & (row < stop)).astype(F32).astype(BF16)
        part = dg(hot, ret[dest], 1, 0)
        own = part if own is None else own + part
    egrad[...] = dg(own.astype(BF16), wp[...], 1, 1).astype(BF16)
    for name, r, slot, at in plan:
        piece = fin[slot, at : at + SEG].astype(F32)
        if name == "wp":
            dwp[r : r + SEG] = piece
        elif name != "vec":
            dwin[r : r + SEG, name * ROWS : (name + 1) * ROWS] = piece
        else:
            for z in range(m):
                @pl.when(wt == z)
                def _():
                    for i, ref in enumerate(vecs[:BIAS_E]):
                        w = ref.shape[0]
                        ref[...] = piece[i, z * w : (z + 1) * w]
                    w = vecs[BIAS_E].shape[0]
                    line = BIAS_E + z * w // ROWS
                    vecs[BIAS_E][...] = piece[line, z * w % ROWS : z * w % ROWS + w]
    for name, r, slot, at in mlp_plan:
        piece = mlp[slot, at : at + SEG].astype(F32)
        if name == "wm":
            dwm[r : r + SEG] = piece
        elif name == "wr":
            dwr[r : r + SEG] = piece
        else:
            dwe[r : r + SEG, name * ROWS : (name + 1) * ROWS] = piece


def finish(n, m, held, fin, ret, mlp, wp, f):
    e, d = wp.shape
    whole = pl.BlockSpec(memory_space=pltpu.VMEM)
    shape = jax.ShapeDtypeStruct
    plan = segments([("wp", e // m)] + [(j, d // m) for j in range(3)] + [("vec", SEG)], fin.shape[1])
    mlp_plan = segments(mlp_parts(d, f, m), mlp.shape[1])
    outs = [shape((held, e), BF16)] + [
        shape((r // m, c), F32) for r, c in ((e, d), (d, 3 * d), (d, d), (d, f), (f, d))
    ] + [shape((d // m,), F32)] * BIAS_E + [shape((f // m,), F32)]
    return pl.pallas_call(
        functools.partial(finish_kernel, n, m, plan, mlp_plan),
        in_specs=[whole] * 4,
        out_specs=[whole] * len(outs),
        out_shape=outs,
        compiler_params=params(),
        cost_estimate=cost(1e9, 4e6),
    )(fin, ret, mlp, wp)


def core(n, m, held, seen_len, seen, vis, wp, win, cols, be, wpack, upstream, reduce_mlp=None):
    d = cols.shape[0]
    pos = jnp.asarray(position_table(d))
    o, inv, e, stream, q, kt, v_rows = front(seen, vis, wp, cols, pos, win)
    share = up16(-(-wpack.shape[1] // n))
    dec, ga, do, dsum, mlp, vec = mid(n, m, share, o, inv, stream, upstream.reshape(2, L, d), wpack, be, cols)
    if reduce_mlp is not None:
        mlp = reduce_mlp(mlp)
    share = up16(-(-(wp.shape[0] // m + 3 * (d // m) + SEG) // n))
    gpack, gp = back(n, m, share, held, seen_len, e, v_rows, q, do, dsum, kt, stream, ga, seen, vis, win, cols, vec)
    return dec, mlp, gpack, gp


def per_device(encoded, visible_at, wp, token, gain1, shift1, win, bq, bv, wm, bm, gain2, shift2, we, be, wr, br, upstream):
    n = lax.axis_size("clip")
    m = lax.axis_size("wt")
    held = encoded.shape[0]
    seen_len = visible_at.shape[1]
    d = wp.shape[1]
    f = be.shape[0] * m
    local = pack_mlp(wm, we, wr)
    wpack = lax.all_gather(local, "wt", axis=0, tiled=True).reshape(m, local.shape[0], ROWS)
    vecs = (token, gain1, shift1, bq, bv, bm, gain2, shift2, br, be)
    seen, vis, wp_full, win_full, cols, be_col = enter(n, m, encoded, visible_at, wp, win, vecs)

    def reduce_mlp(mlp):
        part = lax.psum_scatter(mlp.reshape(-1, ROWS), "clip", scatter_dimension=0, tiled=True)
        return part.reshape(mlp.shape[1:])

    dec, mlp, gpack, gp = core(
        n, m, held, seen_len, seen, vis, wp_full, win_full, cols, be_col, wpack, upstream, reduce_mlp
    )
    fin, ret, mlp = leave(n, m, gpack, gp, mlp)
    egrad, dwp, dwin, dwm, dwe, dwr, *small = finish(n, m, held, fin, ret, mlp, wp_full, f)
    t, g1, s1, vq, vv, vm, g2, s2, vr, ve = small
    return (
        dec.reshape(2 * L, d), egrad, dwp, t, g1, s1, dwin, vq, vv, dwm, vm, g2, s2, dwe, ve, dwr, vr,
    )


def solution(mesh):
    both, wt = P(("clip", "wt"), None), P("wt")
    mat = P("wt", None)
    params_in = (mat, wt, wt, wt, mat, wt, wt, mat, wt, wt, wt, mat, wt, mat, wt)
    return jax.shard_map(
        per_device,
        mesh=mesh,
        in_specs=(both, both) + params_in + (both,),
        out_specs=(both, both) + params_in,
        check_vma=False,
    )
```
